128 devices in a mesh: section: 2 (over y_lo), rep: 8 (over y_hi, x), shard: 8 (over z, core).
Axes of the slice: x: 4, y: 4 (y_hi: 2, y_lo: 2; y = y_hi * 2 + y_lo), z: 4, core: 2. Of those that a mesh axis runs over, the one named last changes fastest.
Arguments:
- inputs: bfloat16 [2, 8, 1024, 768], P(None, 'rep', 'shard'), may hold values from -6 to 6
- cotangent: bfloat16 [2, 8, 1024, 768], P(None, 'rep', 'shard'), may hold values from -6 to 6
- w_qkv: bfloat16 [2, 768, 2304], P('section', 'shard'), may hold values from -0.21875 to 0.21875
- w_attn_out: bfloat16 [2, 768, 768], P('section', 'shard'), may hold values from -2.5 to 2.5
- gain_attn: bfloat16 [2, 768], P('section', 'shard'), may hold values from 0.5 to 1.5
- gain_ffn: bfloat16 [2, 768], P('section', 'shard'), may hold values from 0.5 to 1.5
- rel_bias: bfloat16 [2, 32, 12], P('section', 'shard'), may hold values from -4 to 4
- w_in: bfloat16 [2, 64, 768, 3072], P('section', ('rep', 'shard')), may hold values from -0.21875 to 0.21875
- w_out: bfloat16 [2, 64, 3072, 768], P('section', ('rep', 'shard')), may hold values from -0.109375 to 0.109375
- routes: int32 [2, 2, 8, 1024, 2], P('section', None, 'rep', 'shard'), may hold values from 0 to 63, all different within a row; in each aligned block of 128 rows (0 to 127, 128 to 255, ..., all dimensions but the last counted through in order) at most 5 rows name the same one
- gates: float32 [2, 2, 8, 1024, 2], P('section', None, 'rep', 'shard'), may hold values from 0.25 to 0.75
Outputs:
- section_out: bfloat16 [2, 2, 8, 1024, 768], P('section', None, 'rep', 'shard')
- section_in_grad: bfloat16 [2, 2, 8, 1024, 768], P('section', None, 'rep', 'shard')
- grad_w_qkv: float32 [2, 768, 2304], P('section', 'shard')
- grad_w_attn_out: float32 [2, 768, 768], P('section', 'shard')
- grad_gain_attn: float32 [2, 768], P('section', 'shard')
- grad_gain_ffn: float32 [2, 768], P('section', 'shard')
- grad_rel_bias: float32 [2, 32, 12], P('section', 'shard')
- grad_w_in: float32 [2, 64, 768, 3072], P('section', ('rep', 'shard'))
- grad_w_out: float32 [2, 64, 3072, 768], P('section', ('rep', 'shard'))
The draws below stay inside these ranges and needn't reach their ends.
Inputs may be any that keep to these rules, and one draw needn't show every extreme that they name: `routes`: each token names two different experts. Within each aligned block of 128 tokens (one device's positions of one sequence) no expert is named more than 5 times, and in every draw some expert is named exactly 5 times in some block.
All inputs are finite; a program needn't handle non-finite values.
Results may differ from the reference program's by a relative error of at most 0.025.
Values may be sent and summed in bfloat16 or wider, within the bound.
No kernel may reach another device: no remote copies, remote signals or barrier semaphores. Data moves between devices by JAX's collectives and lax.ppermute only.
A program may use at most 320 MiB of HBM per device.

```python
import math
import jax
import jax.numpy as jnp
import numpy as np
from jax import lax

D = 768
H = 12
HD = 64
FF = 3072
MB = 2
SEQ_LEN = 1024
BLOCK = 256
RELB = 32
SEQ_DEV = 128
EXPERTS = 64
CAP = 5
N_REP = 8
N_SHARD = 8


def levels(key, extent, split, smallest, largest):
    def one(dim, shards_of):
        draws = jax.random.uniform(jax.random.fold_in(jax.random.fold_in(key, 6), dim), (shards_of,), jnp.float32, smallest / len(split), largest / len(split))
        return jnp.repeat(jnp.exp(draws), extent[dim] // shards_of).reshape((-1,) + (1,) * (len(extent) - dim - 1))

    loudness = one(*split[0])
    for cut in split[1:]:
        loudness = loudness * one(*cut)
    return loudness


def deal_out(own_key, own, number, rows, number_of, top, limit, lean):
    ranking = jax.random.permutation(own_key, number_of)
    crowded, usual = load_shares(number_of, rows * top, limit, lean, True), load_shares(number_of, rows * top, limit, lean, False)
    places = jnp.arange(number_of)

    def named(lengths, turn):
        used = int((lengths > 0).sum())
        fixed = max(1, used // 4)
        moved = fixed + (places - fixed + turn * (used - fixed)) % max(1, number_of - fixed)
        return jnp.zeros((number_of,), jnp.int32).at[ranking[jnp.where(places < fixed, places, moved)]].set(jnp.asarray(lengths, jnp.int32))

    lengths = jnp.where(number % 4 == 0, named(crowded, number // 4), named(usual, number - number // 4 - 1))
    mixed = jax.random.permutation(jax.random.fold_in(own, 3), number_of)
    donor, taker = mixed[0:number_of // 2 * 2:2], mixed[1:number_of // 2 * 2:2]
    slack = jnp.minimum(lengths[donor] - 1, limit - lengths[taker]) // 2
    slack = jnp.where((donor == ranking[0]) | (taker == ranking[0]) | (lengths[taker] == 0), 0, jnp.maximum(slack, 0))
    moved = jax.random.randint(jax.random.fold_in(own, 4), (number_of // 2,), 0, 1 << 20) % (slack + 1)
    lengths = lengths.at[donor].add(-moved).at[taker].add(moved)
    items = jnp.searchsorted(jnp.cumsum(lengths), jnp.arange(rows * top), side="right").astype(jnp.int32)
    listing = items.reshape(top, rows).T
    listing = listing[jax.random.permutation(jax.random.fold_in(own, 1), rows)]
    turn = jax.random.randint(jax.random.fold_in(own, 2), (rows, 1), 0, top)
    return jnp.take_along_axis(listing, (jnp.arange(top)[None, :] + turn) % top, axis=1)


def load_shares(count, total, most, lean, full):
    weights = [(1 << 20) // math.isqrt(rank ** lean) + 1 for rank in range(1, count + 1)]
    largest = most if full else min(most, max(-(-total // count), total * weights[0] // sum(weights)))
    least = 1 if total - largest >= count - 1 else 0
    holding, spare = [largest] + [least] * (count - 1), total - largest - least * (count - 1)
    while spare > 0:
        movable = [i for i in range(1, count) if holding[i] < largest] or [i for i in range(1, count) if holding[i] < most]
        mass, left = sum([weights[i] for i in movable]), spare
        for i in movable:
            addition = min(most - holding[i], max(1, left * weights[i] // mass), spare)
            holding[i] = holding[i] + addition
            spare = spare - addition
    return np.array(holding)


def normal_values(key, dims, width, bound, pieces=(), held_as=jnp.bfloat16):
    result = width * jax.random.normal(key, dims, jnp.float32)
    if pieces:
        result = result * levels(key, dims, pieces, -0.22, 0.18)
    return jnp.clip(result, -bound, bound).astype(held_as)


def setup_inputs(seed: int = 0) -> dict:
    seeds = jax.random.split(jax.random.key(seed), 12)
    inputs = normal_values(seeds[0], (MB, N_REP, SEQ_LEN, D), 1.0, 6.0, ((1, 8), (2, 8)))
    cotangent = normal_values(seeds[1], (MB, N_REP, SEQ_LEN, D), 1.0, 6.0, ((1, 8), (2, 8)))
    w_qkv = normal_values(seeds[2], (2, D, 3 * D), D ** -0.5, 0.21875, ((0, 2), (1, 8)))
    w_attn_out = normal_values(seeds[3], (2, D, D), (max(1, D // 128)) ** -0.5, 2.5, ((0, 2), (1, 8)))
    gain_attn = jnp.clip(1.0 + 0.1 * jax.random.normal(seeds[4], (2, D), jnp.float32), 0.5, 1.5).astype(jnp.bfloat16)
    gain_ffn = jnp.clip(1.0 + 0.1 * jax.random.normal(seeds[5], (2, D), jnp.float32), 0.5, 1.5).astype(jnp.bfloat16)
    rel_bias = normal_values(seeds[6], (2, RELB, H), 1.0, 4.0, ((0, 2), (1, 8)))
    w_in = normal_values(seeds[7], (2, EXPERTS, D, FF), D ** -0.5, 0.21875, ((0, 2), (1, 64)))
    w_out = normal_values(seeds[8], (2, EXPERTS, FF, D), FF ** -0.5, 0.109375, ((0, 2), (1, 64)))
    routes_keys = jax.random.split(jax.random.fold_in(seeds[9], 1), 2 * MB * N_REP * SEQ_LEN // SEQ_DEV)
    routes_turns = jax.random.permutation(jax.random.fold_in(seeds[9], 3), 2 * MB * N_REP * SEQ_LEN // SEQ_DEV)
    routes = jax.vmap(lambda own, number: deal_out(jax.random.fold_in(seeds[9], 2), own, number, SEQ_DEV, EXPERTS, 2, CAP, 2))(routes_keys, routes_turns).reshape((2, MB, N_REP, SEQ_LEN, 2))
    gates = jnp.clip(0.25 + 0.5 * jax.random.uniform(seeds[10], (2, MB, N_REP, SEQ_LEN, 2), jnp.float32) ** levels(seeds[10], (2, MB, N_REP, SEQ_LEN, 2), ((0, 2), (2, 8), (3, 8)), -0.2, 0.2), 0.25, 0.75)
    return {"inputs": inputs, "cotangent": cotangent, "w_qkv": w_qkv, "w_attn_out": w_attn_out, "gain_attn": gain_attn, "gain_ffn": gain_ffn, "rel_bias": rel_bias, "w_in": w_in, "w_out": w_out, "routes": routes, "gates": gates}


NORM_EPSILON = 1e-05
MASKED = -1e+30

@jax.custom_vjp
def low(v):
    return lax.optimization_barrier(v.astype(jnp.bfloat16)).astype(jnp.float32)

@jax.custom_vjp
def low_back(v):
    return v

def low_keep(v):
    return (low(v), None)

def low_pass(kept, grad):
    return (grad,)

def back_keep(v):
    return (v, None)

def back_low(kept, grad):
    return (low(grad),)
low.defvjp(low_keep, low_pass)
low_back.defvjp(back_keep, back_low)

def exact_dot(left, right):
    return jnp.dot(left, right, precision=lax.Precision.HIGHEST, preferred_element_type=jnp.float32)

def rms_norm(hidden, gain_vec):
    scaling = lax.rsqrt(lax.optimization_barrier(jnp.mean(hidden * hidden, axis=-1, keepdims=True)) + NORM_EPSILON)
    return hidden * scaling * gain_vec

def positions_table():
    places = jnp.arange(SEQ_LEN, dtype=jnp.int32)
    distance = places[:, None] - places[None, :]
    bucket = jnp.clip((distance + BLOCK) * RELB // (SEQ_LEN + BLOCK), 0, RELB - 1).astype(jnp.int32)
    allowed = places[None, :] // BLOCK <= places[:, None] // BLOCK
    return (bucket, allowed)

def attend(normed, w_qkv, w_attn_out, rel_bias, bucket, allowed):
    projected = low_back(low(exact_dot(normed, w_qkv)))
    queries = projected[:, :D].reshape(SEQ_LEN, H, HD)
    key_part = projected[:, D:2 * D].reshape(SEQ_LEN, H, HD)
    value_part = projected[:, 2 * D:].reshape(SEQ_LEN, H, HD)
    raw_scores = jnp.einsum('qhd,khd->hqk', queries, key_part, precision=lax.Precision.HIGHEST) * HD ** (-0.5)
    scores = low_back(raw_scores)
    bias_full = jnp.transpose(rel_bias[bucket], (2, 0, 1))
    logits = jnp.where(allowed[None], scores + bias_full, MASKED)
    row_max = lax.optimization_barrier(jnp.max(logits, axis=-1, keepdims=True))
    exp_terms = jnp.exp(logits - row_max)
    attn_weights = low(exp_terms / lax.optimization_barrier(jnp.sum(exp_terms, axis=-1, keepdims=True)))
    context = jnp.einsum('hqk,khd->qhd', attn_weights, value_part, precision=lax.Precision.HIGHEST)
    context = low_back(low(context.reshape(SEQ_LEN, D)))
    return low_back(exact_dot(context, w_attn_out))

def slot_tables(route_block):
    flat_routes = route_block.reshape(-1)
    onehot = (flat_routes[:, None] == jnp.arange(EXPERTS, dtype=jnp.int32)[None, :]).astype(jnp.int32)
    slot_rank = lax.optimization_barrier(jnp.sum((jnp.cumsum(onehot, axis=0) - onehot) * onehot, axis=1))
    slot_ids = (flat_routes * CAP + slot_rank).astype(jnp.int32)
    slot_owner = jnp.full((EXPERTS * CAP,), SEQ_DEV, jnp.int32).at[slot_ids].set(jnp.arange(2 * SEQ_DEV, dtype=jnp.int32) // 2)
    return (slot_ids, slot_owner)

def one_expert(packed):
    row_block, first_proj, second_proj = packed
    up_proj = low_back(exact_dot(row_block, first_proj))
    activated = low(jax.nn.gelu(up_proj, approximate=False))
    return low_back(low(exact_dot(activated, second_proj)))

def layer_forward(hidden, w_qkv, w_attn_out, gain_attn, gain_ffn, rel_bias, w_in, w_out, slot_ids, slot_owner, gate_blocks):
    bucket, allowed = positions_table()
    sequences = hidden.reshape(MB * N_REP, SEQ_LEN, D)

    def one_sequence(sequence):
        return attend(low(rms_norm(sequence, gain_attn)), w_qkv, w_attn_out, rel_bias, bucket, allowed)
    attn_out = lax.map(jax.checkpoint(one_sequence), sequences)
    middle = sequences + attn_out
    normed = low(rms_norm(middle, gain_ffn))
    block_count = MB * N_REP * N_SHARD
    blocks = normed.reshape(block_count, SEQ_DEV, D)
    padded = jnp.concatenate([blocks, jnp.zeros((block_count, 1, D), jnp.float32)], axis=1)
    dispatched = low_back(jnp.take_along_axis(padded, slot_owner[:, :, None], axis=1))
    by_expert = dispatched.reshape(block_count, EXPERTS, CAP, D).transpose(1, 0, 2, 3).reshape(EXPERTS, block_count * CAP, D)
    expert_out = lax.map(jax.checkpoint(one_expert), (by_expert, w_in, w_out))
    returned = expert_out.reshape(EXPERTS, block_count, CAP, D).transpose(1, 0, 2, 3).reshape(block_count, EXPERTS * CAP, D)
    picked = jnp.take_along_axis(returned, slot_ids[:, :, None], axis=1).reshape(block_count, SEQ_DEV, 2, D)
    expert_sum = lax.optimization_barrier(jnp.sum(picked * gate_blocks[..., None], axis=2))
    return (middle + expert_sum.reshape(MB * N_REP, SEQ_LEN, D)).reshape(MB, N_REP, SEQ_LEN, D)

def reference(inputs, cotangent, w_qkv, w_attn_out, gain_attn, gain_ffn, rel_bias, w_in, w_out, routes, gates):
    tables = [jax.vmap(slot_tables)(routes[number].reshape(-1, SEQ_DEV, 2)) for number in range(2)]
    gate_blocks = gates.reshape(2, -1, SEQ_DEV, 2).astype(jnp.float32)
    weights_f32 = tuple((item.astype(jnp.float32) for item in (w_qkv, w_attn_out, gain_attn, gain_ffn, rel_bias, w_in, w_out)))
    start = inputs.astype(jnp.float32)

    def forward(first_in, wq, wa, gain_a, gain_f, bias_table, wi, wo, offset):
        first_out = layer_forward(first_in, wq[0], wa[0], gain_a[0], gain_f[0], bias_table[0], wi[0], wo[0], tables[0][0], tables[0][1], gate_blocks[0])
        passed = low_back(low(first_out) + offset)
        second_out = layer_forward(passed, wq[1], wa[1], gain_a[1], gain_f[1], bias_table[1], wi[1], wo[1], tables[1][0], tables[1][1], gate_blocks[1])
        return (low(first_out), low(second_out))
    section_values, pull_back = jax.vjp(forward, start, *weights_f32, jnp.zeros_like(start))
    gradients = pull_back((jnp.zeros_like(start), cotangent.astype(jnp.float32)))
    grad_start, grad_qkv, grad_attn, grad_gain_a, grad_gain_f, grad_bias, grad_in, grad_out, grad_offset = gradients
    section_out = jnp.stack([section_values[0], section_values[1]]).astype(jnp.bfloat16)
    section_in_grad = jnp.stack([grad_start, grad_offset]).astype(jnp.bfloat16)
    return (section_out, section_in_grad, grad_qkv, grad_attn, grad_gain_a, grad_gain_f, grad_bias, grad_in, grad_out)
```

```python
from functools import partial

import jax
import jax.numpy as jnp
from jax import lax
from jax.experimental import pallas as pl
from jax.experimental.pallas import tpu as pltpu
from jax.sharding import PartitionSpec as P

F32 = jnp.float32
BF = jnp.bfloat16
D = 768
H = 12
HD = 64
FF = 3072
SEQ = 1024
TOK = 128
BLOCK = 256
RELB = 32
EXPERTS = 64
CAP = 5
LANES = 128
COLS = D // LANES
CHUNK = 32
GROUP = 16
SLOTS = EXPERTS * CAP
GROUPS_ALL = 2 * EXPERTS // GROUP
ROWS = 2 * EXPERTS * CAP
PAIRS = H // 2
EPS = 1e-05
EVERYONE = ("section", "rep", "shard")
HIGHEST = lax.Precision.HIGHEST
MIB = 1 << 20


def mm(a, b):
    return lax.dot_general(a, b, (((1,), (0,)), ((), ())), preferred_element_type=F32)


def mm_nt(a, b):
    return lax.dot_general(a, b, (((1,), (1,)), ((), ())), preferred_element_type=F32)


def mm_tn(a, b):
    return lax.dot_general(a, b, (((0,), (0,)), ((), ())), preferred_element_type=F32)


def call(kernel, outs, name, flops, moved, vmem=32, **more):
    return pl.pallas_call(
        kernel,
        out_shape=outs,
        name=name,
        compiler_params=pltpu.CompilerParams(vmem_limit_bytes=vmem * MIB),
        cost_estimate=pl.CostEstimate(flops=flops, bytes_accessed=moved, transcendentals=0),
        **more,
    )


def shape(*dims, dtype=BF):
    return jax.ShapeDtypeStruct(dims, dtype)


def pack_tables():
    row = jnp.arange(GROUP * CAP * COLS, dtype=jnp.int32)[:, None]
    col = jnp.arange(GROUP * CHUNK, dtype=jnp.int32)[None, :]
    block, inside = row // (GROUP * CAP), row % (GROUP * CAP)
    place = (inside // CAP) * CHUNK + block * CAP + inside % CAP
    return (place == col).astype(BF)


def unpack(chunks, table, target):
    for g in range(chunks.shape[0] // GROUP):
        raw = chunks[g * GROUP : (g + 1) * GROUP].reshape(GROUP * CHUNK, LANES)
        rows = mm(table, raw).astype(BF)
        for c in range(COLS):
            target[g * GROUP * CAP : (g + 1) * GROUP * CAP, c * LANES : (c + 1) * LANES] = rows[
                c * GROUP * CAP : (c + 1) * GROUP * CAP
            ]


def pack(rows, table_t, target, first):
    for g in range(rows.shape[0] // (GROUP * CAP)):
        part = rows[g * GROUP * CAP : (g + 1) * GROUP * CAP]
        stacked = jnp.concatenate([part[:, c * LANES : (c + 1) * LANES] for c in range(COLS)], axis=0)
        chunk = mm(table_t, stacked).astype(BF).reshape(GROUP, CHUNK, LANES)
        target[first + g * GROUP : first + (g + 1) * GROUP] = chunk


def pack_for_layer(rows, table_t, target, layer):
    pack(rows, table_t, target, layer * EXPERTS)
    other = (1 - layer) * EXPERTS
    target[other : other + EXPERTS] = jnp.zeros((EXPERTS, CHUNK, LANES), BF)


def slots_by_token(slot_rows):
    places = lax.broadcasted_iota(jnp.int32, (SLOTS, TOK), 0)
    return [jnp.where(places == slot_rows[k : k + 1, :], 1.0, 0.0).astype(BF) for k in range(2)]


def tokens_by_slot(slot_cols):
    places = lax.broadcasted_iota(jnp.int32, (TOK, SLOTS), 1)
    return [jnp.where(places == slot_cols[:, k : k + 1], 1.0, 0.0).astype(BF) for k in range(2)]


def norm_of(hidden, gain):
    scaling = lax.rsqrt(jnp.mean(hidden * hidden, axis=-1, keepdims=True) + EPS)
    return hidden * scaling * gain, scaling


def norm_back(hidden, scaling, gain, grad):
    gain_grad = jnp.sum(grad * hidden * scaling, axis=0, keepdims=True)
    weighted = grad * gain
    inner = jnp.mean(weighted * hidden, axis=-1, keepdims=True)
    return weighted * scaling - hidden * (scaling * scaling * scaling * inner), gain_grad


def bias_tiles_kernel(line_ref, out_ref):
    for h in range(2):
        for delta in range(4):
            line = jnp.broadcast_to(line_ref[h * 4 + delta : h * 4 + delta + 1, :], (BLOCK, 2 * BLOCK))
            turned = pltpu.roll(line, 0, 1, stride=1, stride_axis=0)
            out_ref[h * 4 + delta] = turned[:, :BLOCK].astype(BF)


def bias_tiles(table):
    m = jnp.arange(2 * BLOCK, dtype=jnp.int32)
    ahead = jnp.where(m < BLOCK, m, m - 2 * BLOCK)
    distance = jnp.arange(4, dtype=jnp.int32)[:, None] * BLOCK - ahead[None, :]
    bucket = jnp.clip((distance + BLOCK) * RELB // (SEQ + BLOCK), 0, RELB - 1)
    onehot = (bucket[..., None] == jnp.arange(RELB, dtype=jnp.int32)).astype(F32)
    lines = jnp.einsum("dmb,bh->hdm", onehot, table, precision=HIGHEST).reshape(8, 2 * BLOCK)
    return call(bias_tiles_kernel, shape(8, BLOCK, BLOCK), "bias_tiles", 0, 1 << 20)(lines)


def head_mask(h, rows):
    lane = lax.broadcasted_iota(jnp.int32, (rows, LANES), 1)
    return (lane < HD) if h == 0 else (lane >= HD)


def attention_kernel(qkv_ref, bias_ref, ctx_ref, weights_ref):
    step = 128
    for i in range(4):
        keys = (i + 1) * BLOCK
        key = qkv_ref[0:keys, LANES : 2 * LANES]
        value = qkv_ref[0:keys, 2 * LANES : 3 * LANES]
        for part in range(BLOCK // step):
            first = i * BLOCK + part * step
            query = qkv_ref[first : first + step, 0:LANES] * jnp.asarray(HD**-0.5, BF)
            mixed = []
            for h in range(2):
                mask = head_mask(h, step)
                own = jnp.where(mask, query, jnp.zeros_like(query))
                scores = mm_nt(own, key)
                offset = jnp.concatenate(
                    [bias_ref[h * 4 + i - b, part * step : (part + 1) * step, :] for b in range(i + 1)], axis=1
                ).astype(F32)
                scores = scores + offset
                top = jnp.max(scores, axis=-1, keepdims=True)
                terms = jnp.exp(scores - top)
                total = jnp.sum(terms, axis=-1, keepdims=True)
                weights = (terms * (1.0 / total)).astype(BF)
                weights_ref[h, first : first + step, 0:keys] = weights
                mixed.append(mm(weights, value))
            ctx_ref[first : first + step, :] = jnp.where(head_mask(0, step), mixed[0], mixed[1]).astype(BF)


def attention(qkv, tiles):
    return call(
        attention_kernel,
        (shape(SEQ, LANES), shape(2, SEQ, SEQ)),
        "attention",
        2 * 2 * 2 * SEQ * SEQ * LANES,
        8 << 20,
    )(qkv, tiles)


def attention_back_kernel(qkv_ref, weights_ref, dout_ref, flip_ref, dproj_ref, diag_ref, dkey, dvalue, tiles):
    step = 128
    dkey[...] = jnp.zeros_like(dkey)
    dvalue[...] = jnp.zeros_like(dvalue)
    tiles[...] = jnp.zeros_like(tiles)
    for i in range(4):
        keys = (i + 1) * BLOCK
        key = qkv_ref[0:keys, LANES : 2 * LANES]
        value = qkv_ref[0:keys, 2 * LANES : 3 * LANES]
        for part in range(BLOCK // step):
            first = i * BLOCK + part * step
            query = qkv_ref[first : first + step, 0:LANES]
            dout = dout_ref[first : first + step, :]
            query_t = query.astype(F32).T.astype(BF)
            dout_t = dout.astype(F32).T.astype(BF)
            moved = []
            for h in range(2):
                own = jnp.where(head_mask(h, step), dout, jnp.zeros_like(dout))
                low = weights_ref[h, first : first + step, 0:keys]
                weights = low.astype(F32)
                dweights = mm_nt(own, value)
                delta = jnp.sum(weights * dweights, axis=-1, keepdims=True)
                dscores = weights * (dweights - delta)
                for b in range(i + 1):
                    rows = slice(part * step, (part + 1) * step)
                    tiles[h * 4 + i - b, rows, :] += dscores[:, b * BLOCK : (b + 1) * BLOCK]
                dlow = dscores.astype(BF)
                moved.append(mm(dlow, key))
                head = slice(h * HD, (h + 1) * HD)
                dkey[head, 0:keys] += mm(query_t[head], dlow)
                dvalue[head, 0:keys] += mm(dout_t[head], low)
            dquery = jnp.where(head_mask(0, step), moved[0], moved[1]) * HD**-0.5
            dproj_ref[first : first + step, 0:LANES] = dquery.astype(BF)
    dproj_ref[:, LANES : 2 * LANES] = (dkey[...] * HD**-0.5).T.astype(BF)
    dproj_ref[:, 2 * LANES : 3 * LANES] = dvalue[...].T.astype(BF)
    for n in range(8):
        tile = tiles[n]
        high = tile.astype(BF)
        rest = (tile - high.astype(F32)).astype(BF)
        flipped = mm(high, flip_ref[...]) + mm(rest, flip_ref[...])
        wide = jnp.concatenate([flipped, jnp.zeros_like(flipped)], axis=1)
        turned = pltpu.roll(wide, 0, 1, stride=1, stride_axis=0)
        diag_ref[n : n + 1, :] = jnp.sum(turned, axis=0, keepdims=True)


def attention_back(qkv, weights, dout):
    at = jnp.arange(BLOCK, dtype=jnp.int32)
    flip = (at[:, None] + at[None, :] == BLOCK - 1).astype(BF)
    dproj, diag = call(
        attention_back_kernel,
        (shape(SEQ, 3 * LANES), shape(8, 2 * BLOCK, dtype=F32)),
        "attention_back",
        2 * 4 * 2 * SEQ * SEQ * LANES,
        8 << 20,
        scratch_shapes=[
            pltpu.VMEM((LANES, SEQ), F32),
            pltpu.VMEM((LANES, SEQ), F32),
            pltpu.VMEM((8, BLOCK, BLOCK), F32),
        ],
    )(qkv, weights, dout, flip)
    m = jnp.arange(2 * BLOCK, dtype=jnp.int32)
    distance = jnp.arange(4, dtype=jnp.int32)[:, None] * BLOCK + m[None, :] - (BLOCK - 1)
    bucket = jnp.clip((distance + BLOCK) * RELB // (SEQ + BLOCK), 0, RELB - 1)
    onehot = (bucket[..., None] == jnp.arange(RELB, dtype=jnp.int32)).astype(F32)
    return dproj, jnp.einsum("hdm,dmb->bh", diag.reshape(2, 4, 2 * BLOCK), onehot, precision=HIGHEST)


def middle_kernel(layer, ctx_ref, wao_ref, hidden_ref, gain_ref, slots_ref, table_ref, middle_ref, out_ref):
    context = jnp.concatenate([ctx_ref[g] for g in range(PAIRS)], axis=1)
    middle = hidden_ref[...].astype(F32) + mm(context, wao_ref[...])
    middle_ref[...] = middle
    normed = norm_of(middle, gain_ref[...])[0].astype(BF)
    first, second = slots_by_token(slots_ref[...])
    rows = mm(first + second, normed).astype(BF)
    pack_for_layer(rows, table_ref[...], out_ref, layer)


def middle_part(layer, ctx, wao, hidden, gain, slot_rows, table_t):
    return call(
        partial(middle_kernel, layer),
        (shape(TOK, D, dtype=F32), shape(2 * EXPERTS, CHUNK, LANES)),
        "middle",
        2 * TOK * D * D + 2 * SLOTS * TOK * D * 5,
        4 << 20,
    )(ctx, wao, hidden, gain, slot_rows, table_t)


def combined(back_ref, middle_ref, slots_ref, gates_ref, table_ref, rows):
    unpack(back_ref, table_ref[...], rows)
    picks = tokens_by_slot(slots_ref[...])
    gates = gates_ref[...]
    total = middle_ref[...]
    for k in range(2):
        total = total + gates[:, k : k + 1] * mm(picks[k], rows[...])
    return total.astype(BF)


def combine_kernel(back_ref, middle_ref, slots_ref, gates_ref, table_ref, out_ref, rows):
    out_ref[...] = combined(back_ref, middle_ref, slots_ref, gates_ref, table_ref, rows)


def combine_project_kernel(
    back_ref, middle_ref, slots_ref, gates_ref, table_ref, gain_ref, wqkv_ref, out_ref, normed_ref, send_ref, rows
):
    out = combined(back_ref, middle_ref, slots_ref, gates_ref, table_ref, rows)
    out_ref[...] = out
    normed = norm_of(out.astype(F32), gain_ref[...])[0].astype(BF)
    normed_ref[...] = normed
    projected = mm(normed, wqkv_ref[...]).astype(BF)
    for g in range(PAIRS):
        for part in range(3):
            first = part * D + g * LANES
            send_ref[g, :, part * LANES : (part + 1) * LANES] = projected[:, first : first + LANES]
    send_ref[PAIRS:8] = jnp.zeros((8 - PAIRS, TOK, 3 * LANES), BF)


def combine(back, middle, slot_cols, gates, table):
    return call(
        combine_kernel,
        shape(TOK, D),
        "combine",
        2 * TOK * SLOTS * D * 6,
        4 << 20,
        scratch_shapes=[pltpu.VMEM((SLOTS, D), BF)],
    )(back, middle, slot_cols, gates, table)


def combine_project(back, middle, slot_cols, gates, table, gain, wqkv):
    return call(
        combine_project_kernel,
        (shape(TOK, D), shape(TOK, D), shape(8, TOK, 3 * LANES)),
        "combine_project",
        2 * TOK * D * 3 * D,
        8 << 20,
        scratch_shapes=[pltpu.VMEM((SLOTS, D), BF)],
    )(back, middle, slot_cols, gates, table, gain, wqkv)


def send_grads(layer, dout, slot_rows, gates, table_t, out_ref):
    first, second = slots_by_token(slot_rows)
    wide = dout.astype(F32)
    rows = mm(first, (wide * gates[:, 0:1]).astype(BF)) + mm(second, (wide * gates[:, 1:2]).astype(BF))
    pack_for_layer(rows.astype(BF), table_t, out_ref, layer)


def grad_rows_kernel(layer, dout_ref, slots_ref, gates_ref, table_ref, out_ref):
    send_grads(layer, dout_ref[...], slots_ref[...], gates_ref[...], table_ref[...], out_ref)


def grad_rows(layer, dout, slot_rows, gates, table_t):
    return call(
        partial(grad_rows_kernel, layer),
        shape(2 * EXPERTS, CHUNK, LANES),
        "grad_rows",
        2 * TOK * SLOTS * D * 6,
        2 << 20,
    )(dout, slot_rows, gates, table_t)


def middle_back_kernel(
    back_ref, slots_ref, table_ref, dout_ref, middle_ref, gain_ref, wao_ref, dmid_ref, branch_ref, send_ref, dgain_ref, rows
):
    unpack(back_ref, table_ref[...], rows)
    first, second = tokens_by_slot(slots_ref[...])
    dnormed = mm(first + second, rows[...])
    middle = middle_ref[...]
    gain = gain_ref[...]
    scaling = lax.rsqrt(jnp.mean(middle * middle, axis=-1, keepdims=True) + EPS)
    moved, dgain = norm_back(middle, scaling, gain, dnormed)
    dgain_ref[...] = dgain
    dmid = dout_ref[...].astype(F32) + moved
    dmid_ref[...] = dmid
    branch = dmid.astype(BF)
    branch_ref[...] = branch
    dcontext = mm_nt(branch, wao_ref[...]).astype(BF)
    for g in range(PAIRS):
        send_ref[g] = dcontext[:, g * LANES : (g + 1) * LANES]
    send_ref[PAIRS:8] = jnp.zeros((8 - PAIRS, TOK, LANES), BF)


def middle_back(back, slot_cols, table, dout, middle, gain, wao):
    return call(
        middle_back_kernel,
        (shape(TOK, D, dtype=F32), shape(TOK, D), shape(8, TOK, LANES), shape(1, D, dtype=F32)),
        "middle_back",
        2 * TOK * D * D + 2 * TOK * SLOTS * D * 5,
        4 << 20,
        scratch_shapes=[pltpu.VMEM((SLOTS, D), BF)],
    )(back, slot_cols, table, dout, middle, gain, wao)


def hidden_grad(back_ref, wqkv_ref, hidden_ref, gain_ref, dmid_ref, dgain_ref):
    parts = [
        back_ref[g, :, part * LANES : (part + 1) * LANES] for part in range(3) for g in range(PAIRS)
    ]
    dnormed = mm_nt(jnp.concatenate(parts, axis=1), wqkv_ref[...])
    hidden = hidden_ref[...].astype(F32)
    scaling = lax.rsqrt(jnp.mean(hidden * hidden, axis=-1, keepdims=True) + EPS)
    moved, dgain = norm_back(hidden, scaling, gain_ref[...], dnormed)
    dgain_ref[...] = dgain
    return (dmid_ref[...] + moved).astype(BF)


def hidden_back_kernel(back_ref, wqkv_ref, hidden_ref, gain_ref, dmid_ref, dh_ref, dgain_ref):
    dh_ref[...] = hidden_grad(back_ref, wqkv_ref, hidden_ref, gain_ref, dmid_ref, dgain_ref)


def hidden_back_send_kernel(
    layer, back_ref, wqkv_ref, hidden_ref, gain_ref, dmid_ref, slots_ref, gates_ref, table_ref, dh_ref, dgain_ref, out_ref
):
    dh = hidden_grad(back_ref, wqkv_ref, hidden_ref, gain_ref, dmid_ref, dgain_ref)
    dh_ref[...] = dh
    send_grads(layer, dh, slots_ref[...], gates_ref[...], table_ref[...], out_ref)


def hidden_back(back, wqkv, hidden, gain, dmid):
    return call(
        hidden_back_kernel,
        (shape(TOK, D), shape(1, D, dtype=F32)),
        "hidden_back",
        2 * TOK * D * 3 * D,
        5 << 20,
    )(back, wqkv, hidden, gain, dmid)


def hidden_back_send(layer, back, wqkv, hidden, gain, dmid, slot_rows, gates, table_t):
    return call(
        partial(hidden_back_send_kernel, layer),
        (shape(TOK, D), shape(1, D, dtype=F32), shape(2 * EXPERTS, CHUNK, LANES)),
        "hidden_back_send",
        2 * TOK * D * 3 * D,
        6 << 20,
    )(back, wqkv, hidden, gain, dmid, slot_rows, gates, table_t)


FF_STEP = 512
ROW_STEP = 160


def gelu_parts(up):
    size = jnp.abs(up) * (0.5**0.5)
    t = 1.0 / (1.0 + 0.3275911 * size)
    bell = jnp.exp(up * up * -0.5)
    series = t * (0.254829592 + t * (-0.284496736 + t * (1.421413741 + t * (-1.453152027 + t * 1.061405429))))
    tail = 0.5 * series * bell
    phi = jnp.where(up < 0.0, tail, 1.0 - tail)
    return up * phi, phi + up * bell * 0.3989422804014327


def expert_forward_kernel(in_ref, win_ref, wout_ref, table_ref, table_t_ref, x_ref, act_ref, slope_ref, out_ref, total):
    step = pl.program_id(0)

    @pl.when(step == 0)
    def _():
        unpack(in_ref, table_ref[...], x_ref)
        total[...] = jnp.zeros_like(total)

    for r in range(ROWS // ROW_STEP):
        rows = slice(r * ROW_STEP, (r + 1) * ROW_STEP)
        act, slope = gelu_parts(mm(x_ref[rows, :], win_ref[...]))
        act = act.astype(BF)
        act_ref[rows, :] = act
        slope_ref[rows, :] = slope.astype(BF)
        total[rows, :] += mm(act, wout_ref[...])

    @pl.when(step == pl.num_programs(0) - 1)
    def _():
        pack(total[...].astype(BF), table_t_ref[...], out_ref, 0)


def whole(*dims):
    return pl.BlockSpec(dims, lambda f: (0,) * len(dims))


def ff_columns(rows):
    return pl.BlockSpec((rows, FF_STEP), lambda f: (0, f))


def ff_rows(columns):
    return pl.BlockSpec((FF_STEP, columns), lambda f: (f, 0))


CHUNKS = (2 * EXPERTS, CHUNK, LANES)
TABLE = (GROUP * CAP * COLS, GROUP * CHUNK)
TABLE_T = TABLE[::-1]


def expert_forward(arrived, first, second, table, table_t):
    return call(
        expert_forward_kernel,
        (shape(ROWS, D), shape(ROWS, FF), shape(ROWS, FF), shape(*CHUNKS)),
        "expert_forward",
        4 * ROWS * D * FF,
        20 << 20,
        vmem=40,
        grid=(FF // FF_STEP,),
        in_specs=[whole(*CHUNKS), ff_columns(D), ff_rows(D), whole(*TABLE), whole(*TABLE_T)],
        out_specs=(whole(ROWS, D), ff_columns(ROWS), ff_columns(ROWS), whole(*CHUNKS)),
        scratch_shapes=[pltpu.VMEM((ROWS, D), F32)],
    )(arrived, first, second, table, table_t)


def expert_back_kernel(in_ref, win_ref, wout_ref, slope_ref, table_ref, table_t_ref, grad_ref, dup_ref, out_ref, total):
    step = pl.program_id(0)

    @pl.when(step == 0)
    def _():
        unpack(in_ref, table_ref[...], grad_ref)
        total[...] = jnp.zeros_like(total)

    for r in range(ROWS // ROW_STEP):
        rows = slice(r * ROW_STEP, (r + 1) * ROW_STEP)
        dact = mm_nt(grad_ref[rows, :], wout_ref[...])
        dup = (dact * slope_ref[rows, :].astype(F32)).astype(BF)
        dup_ref[rows, :] = dup
        total[rows, :] += mm_nt(dup, win_ref[...])

    @pl.when(step == pl.num_programs(0) - 1)
    def _():
        pack(total[...].astype(BF), table_t_ref[...], out_ref, 0)


def expert_back(arrived, first, second, slope, table, table_t):
    return call(
        expert_back_kernel,
        (shape(ROWS, D), shape(ROWS, FF), shape(*CHUNKS)),
        "expert_back",
        4 * ROWS * D * FF,
        20 << 20,
        vmem=40,
        grid=(FF // FF_STEP,),
        in_specs=[whole(*CHUNKS), ff_columns(D), ff_rows(D), ff_columns(ROWS), whole(*TABLE), whole(*TABLE_T)],
        out_specs=(whole(ROWS, D), ff_columns(ROWS), whole(*CHUNKS)),
        scratch_shapes=[pltpu.VMEM((ROWS, D), F32)],
    )(arrived, first, second, slope, table, table_t)


def expert_both_kernel(
    in_ref, gin_ref, win_ref, wout_ref, table_ref, table_t_ref, x_ref, grad_ref, act_ref, dup_ref, out_ref, back_ref, total, dtotal
):
    step = pl.program_id(0)

    @pl.when(step == 0)
    def _():
        unpack(in_ref, table_ref[...], x_ref)
        unpack(gin_ref, table_ref[...], grad_ref)
        total[...] = jnp.zeros_like(total)
        dtotal[...] = jnp.zeros_like(dtotal)

    for r in range(ROWS // ROW_STEP):
        rows = slice(r * ROW_STEP, (r + 1) * ROW_STEP)
        act, slope = gelu_parts(mm(x_ref[rows, :], win_ref[...]))
        dup = (mm_nt(grad_ref[rows, :], wout_ref[...]) * slope).astype(BF)
        act = act.astype(BF)
        act_ref[rows, :] = act
        dup_ref[rows, :] = dup
        total[rows, :] += mm(act, wout_ref[...])
        dtotal[rows, :] += mm_nt(dup, win_ref[...])

    @pl.when(step == pl.num_programs(0) - 1)
    def _():
        pack(total[...].astype(BF), table_t_ref[...], out_ref, 0)
        pack(dtotal[...].astype(BF), table_t_ref[...], back_ref, 0)


def expert_both(arrived, grads, first, second, table, table_t):
    return call(
        expert_both_kernel,
        (shape(ROWS, D), shape(ROWS, D), shape(ROWS, FF), shape(ROWS, FF), shape(*CHUNKS), shape(*CHUNKS)),
        "expert_both",
        8 * ROWS * D * FF,
        24 << 20,
        vmem=44,
        grid=(FF // FF_STEP,),
        in_specs=[whole(*CHUNKS), whole(*CHUNKS), ff_columns(D), ff_rows(D), whole(*TABLE), whole(*TABLE_T)],
        out_specs=(
            whole(ROWS, D),
            whole(ROWS, D),
            ff_columns(ROWS),
            ff_columns(ROWS),
            whole(*CHUNKS),
            whole(*CHUNKS),
        ),
        scratch_shapes=[pltpu.VMEM((ROWS, D), F32), pltpu.VMEM((ROWS, D), F32)],
    )(arrived, grads, first, second, table, table_t)


def spread(chunks):
    return lax.all_to_all(chunks, EVERYONE, split_axis=0, concat_axis=0, tiled=True)


def across(chunks):
    return lax.all_to_all(chunks, "shard", split_axis=0, concat_axis=0, tiled=True)


def swap(value):
    return lax.ppermute(value, "section", [(0, 1), (1, 0)])


def slot_tables(routes):
    flat = routes.reshape(2, 2 * TOK)
    onehot = (flat[..., None] == jnp.arange(EXPERTS, dtype=jnp.int32)).astype(BF)
    at = jnp.arange(2 * TOK, dtype=jnp.int32)
    earlier = (at[None, :] < at[:, None]).astype(BF)
    before = jnp.einsum("ab,lbe->lae", earlier, onehot, preferred_element_type=F32)
    rank = jnp.sum(before * onehot.astype(F32), axis=-1).astype(jnp.int32)
    return (flat * CAP + rank).reshape(routes.shape)


def per_device(
    inputs, cotangent, w_qkv, w_attn_out, gain_attn, gain_ffn, rel_bias, w_in, w_out, routes, gates
):
    section = lax.axis_index("section")
    shard = lax.axis_index("shard")
    first_proj, second_proj = w_in[0, 0], w_out[0, 0]
    hidden0 = lax.dynamic_index_in_dim(inputs[:, 0], section, 0, keepdims=False)
    cot = lax.dynamic_index_in_dim(cotangent[:, 0], section, 0, keepdims=False)
    table = pack_tables()
    table_t = table.T

    rows = w_qkv.shape[1]
    columns = w_qkv[0].reshape(rows, 3, PAIRS, LANES).transpose(2, 0, 1, 3).reshape(PAIRS, rows, 3 * LANES)
    columns = jnp.concatenate([columns, jnp.zeros((2, rows, 3 * LANES), BF)], axis=0)
    biases = rel_bias[0].reshape(4, PAIRS, 2).transpose(1, 0, 2).reshape(PAIRS, 8)
    biases = jnp.pad(biases, ((0, 2), (0, 3 * LANES - 8)))
    gains = jnp.pad(jnp.concatenate([gain_attn, gain_ffn], axis=0), ((0, 0), (0, 3 * LANES - rows)))
    extra = jnp.concatenate(
        [jnp.broadcast_to(gains[None], (8, 2, 3 * LANES)), biases[:, None], jnp.zeros((8, 5, 3 * LANES), BF)], axis=1
    )
    parcel = jnp.concatenate([columns, extra], axis=1)
    parcel = jnp.concatenate([parcel, parcel], axis=0)
    got = lax.all_to_all(parcel, ("section", "shard"), split_axis=0, concat_axis=0, tiled=True)
    got = got.reshape(2, 8, rows + 8, 3 * LANES)
    w_own = got[:, :, :rows].reshape(2, D, 3 * LANES)
    gain_a = got[:, :, rows, :rows].reshape(2, 1, D).astype(F32)
    gain_f = got[:, :, rows + 1, :rows].reshape(2, 1, D).astype(F32)
    bias = got[:, :, rows + 2, :8].reshape(2, RELB, 2).astype(F32)
    tiles = [bias_tiles(bias[l]) for l in range(2)]

    full0 = lax.all_gather(hidden0, "shard", axis=0, tiled=True)
    w_ao = lax.all_gather(w_attn_out[0], ("section", "shard"), axis=0, tiled=True).reshape(2, D, D)
    w_full = lax.all_gather(w_qkv[0], ("section", "shard"), axis=0, tiled=True).reshape(2, D, 3 * D)

    def both_layers(values):
        own = lax.dynamic_index_in_dim(values[0, :, 0], section, 0, keepdims=False)
        other = swap(lax.dynamic_index_in_dim(values[0, :, 0], 1 - section, 0, keepdims=False))
        return jnp.where(section == 0, jnp.stack([own, other]), jnp.stack([other, own]))

    slot_cols = slot_tables(both_layers(routes))
    slot_rows = slot_cols.transpose(0, 2, 1)
    gate_cols = both_layers(gates)

    grads1 = spread(grad_rows(1, cot, slot_rows[1], gate_cols[1], table_t))

    normed0 = norm_of(full0.astype(F32), gain_a[0])[0].astype(BF)
    qkv0 = mm(normed0, w_own[0]).astype(BF)
    ctx0, weights0 = attention(qkv0, tiles[0])
    ctx0_tok = across(ctx0.reshape(8, TOK, LANES))
    middle0, send = middle_part(0, ctx0_tok, w_ao[0], hidden0, gain_f[0], slot_rows[0], table_t)
    x0, act0, slope0, made = expert_forward(spread(send), first_proj, second_proj, table, table_t)
    back = spread(made)[0:EXPERTS]
    out0, normed1, send = combine_project(back, middle0, slot_cols[0], gate_cols[0], table, gain_a[1], w_full[1])

    qkv1 = across(send).reshape(SEQ, 3 * LANES)
    normed1_full = lax.all_gather(normed1, "shard", axis=0, tiled=True)
    ctx1, weights1 = attention(qkv1, tiles[1])
    ctx1_tok = across(ctx1.reshape(8, TOK, LANES))
    middle1, send = middle_part(1, ctx1_tok, w_ao[1], out0, gain_f[1], slot_rows[1], table_t)
    x1, g1, act1, dup1, made1, dmade1 = expert_both(spread(send), grads1, first_proj, second_proj, table, table_t)

    back = spread(dmade1)[EXPERTS:]
    dmid1, branch1, send, dgain_f1 = middle_back(back, slot_cols[1], table, cot, middle1, gain_f[1], w_ao[1])
    branch1_full = lax.all_gather(branch1, "shard", axis=0, tiled=True)
    dproj1, drel1 = attention_back(qkv1, weights1, across(send).reshape(SEQ, LANES))
    dproj1_tok = across(dproj1.reshape(8, TOK, 3 * LANES))
    dh1, dgain_a1, send = hidden_back_send(
        0, dproj1_tok, w_full[1], out0, gain_a[1], dmid1, slot_rows[0], gate_cols[0], table_t
    )
    made1_back = spread(made1)[EXPERTS:]
    out1 = combine(made1_back, middle1, slot_cols[1], gate_cols[1], table)

    g0, dup0, dmade0 = expert_back(spread(send), first_proj, second_proj, slope0, table, table_t)
    back = spread(dmade0)[0:EXPERTS]
    dmid0, branch0, send, dgain_f0 = middle_back(back, slot_cols[0], table, dh1, middle0, gain_f[0], w_ao[0])
    branch0_full = lax.all_gather(branch0, "shard", axis=0, tiled=True)
    dproj0, drel0 = attention_back(qkv0, weights0, across(send).reshape(SEQ, LANES))
    dproj0_tok = across(dproj0.reshape(8, TOK, 3 * LANES))
    dh0, dgain_a0 = hidden_back(dproj0_tok, w_full[0], hidden0, gain_a[0], dmid0)

    def own(a, b):
        return jnp.where(section == 0, a, b)

    grad_in = mm_tn(own(x0, x1), own(dup0, dup1))
    grad_out = mm_tn(own(act0, act1), own(g0, g1))

    def parcel_of(normed, dproj, ctx, branch, dgain_a, dgain_f, drel):
        dqkv = mm_tn(normed, dproj).astype(BF).reshape(8, rows, 3 * LANES)
        dao = mm_tn(ctx, branch).astype(BF).reshape(8, 16, 2, 3 * LANES).transpose(0, 2, 1, 3)
        small = jnp.concatenate(
            [
                dgain_a.reshape(2, 3 * LANES),
                dgain_f.reshape(2, 3 * LANES),
                jnp.pad(drel.reshape(1, 2 * RELB), ((0, 3), (0, 3 * LANES - 2 * RELB))),
            ],
            axis=0,
        ).astype(BF)
        return jnp.concatenate(
            [dqkv, dao.reshape(8, 32, 3 * LANES), jnp.broadcast_to(small[None], (8, 8, 3 * LANES))], axis=1
        )

    parcels = jnp.concatenate(
        [
            parcel_of(normed0, dproj0, ctx0, branch0_full, dgain_a0, dgain_f0, drel0),
            parcel_of(normed1_full, dproj1, ctx1, branch1_full, dgain_a1, dgain_f1, drel1),
        ],
        axis=0,
    )
    got = lax.all_to_all(parcels, ("section", "rep"), split_axis=0, concat_axis=0, tiled=True)
    summed = jnp.sum(got.astype(F32), axis=0).astype(BF)

    turn = [(a * 8 + b, b * 8 + a) for a in range(8) for b in range(8)]
    block = lax.ppermute(summed[:rows], ("rep", "shard"), turn)
    blocks = lax.all_to_all(
        jnp.broadcast_to(block[None], (8, rows, 3 * LANES)), "rep", split_axis=0, concat_axis=0, tiled=True
    )
    grad_qkv = blocks[:PAIRS].reshape(PAIRS, rows, 3, LANES).transpose(1, 2, 0, 3).reshape(1, rows, 3 * D)
    rest = jnp.concatenate(
        [
            jnp.concatenate([summed[rows : rows + 16], summed[rows + 16 : rows + 32]], axis=1),
            summed[rows + 32 : rows + 40].reshape(4, D),
            jnp.zeros((4, D), BF),
        ],
        axis=0,
    )
    rests = lax.all_gather(rest, ("rep", "shard"), axis=0, tiled=False).reshape(8, 8, 24, D)
    dao = rests[:, :PAIRS, :16].transpose(1, 0, 2, 3).reshape(D, D)
    grad_ao = lax.dynamic_slice_in_dim(dao, shard * rows, rows, 0)[None]
    small = rests[0, :, 16:20].astype(F32)
    gains_sum = jnp.sum(small[:, 0:2], axis=0)
    grad_gain = lax.dynamic_slice_in_dim(gains_sum, shard * rows, rows, 1)
    drel = small[:PAIRS, 2, : 2 * RELB].reshape(PAIRS, RELB, 2).transpose(1, 0, 2).reshape(RELB, H)
    grad_bias = lax.dynamic_slice_in_dim(drel, shard * 4, 4, 0)[None]

    def by_layer(layer0, layer1):
        keep = jnp.where(section == 0, layer0, layer1)
        other = swap(jnp.where(section == 0, layer1, layer0))
        pair = jnp.where(section == 0, jnp.stack([keep, other]), jnp.stack([other, keep]))
        return pair.reshape(1, 2, 1, TOK, D)

    return (
        by_layer(out0, out1),
        by_layer(dh0, dh1),
        grad_qkv.astype(F32),
        grad_ao.astype(F32),
        grad_gain[0:1],
        grad_gain[1:2],
        grad_bias,
        grad_in[None, None],
        grad_out[None, None],
    )


def solution(mesh):
    placed = (
        P(None, "rep", "shard", None),
        P(None, "rep", "shard", None),
        P("section", "shard", None),
        P("section", "shard", None),
        P("section", "shard"),
        P("section", "shard"),
        P("section", "shard", None),
        P("section", ("rep", "shard"), None, None),
        P("section", ("rep", "shard"), None, None),
        P("section", None, "rep", "shard", None),
        P("section", None, "rep", "shard", None),
    )
    return jax.shard_map(
        per_device,
        mesh=mesh,
        in_specs=placed,
        out_specs=(
            P("section", None, "rep", "shard", None),
            P("section", None, "rep", "shard", None),
            P("section", "shard", None),
            P("section", "shard", None),
            P("section", "shard"),
            P("section", "shard"),
            P("section", "shard", None),
            P("section", ("rep", "shard"), None, None),
            P("section", ("rep", "shard"), None, None),
        ),
        check_vma=False,
    )
```

```python
from functools import partial

import jax
import jax.numpy as jnp
from jax import lax
from jax.experimental import pallas as pl
from jax.experimental.pallas import tpu as pltpu
from jax.sharding import PartitionSpec as P

F32 = jnp.float32
BF = jnp.bfloat16
D = 768
H = 12
HD = 64
FF = 3072
SEQ = 1024
TOK = 128
BLOCK = 256
RELB = 32
EXPERTS = 64
CAP = 5
LANES = 128
COLS = D // LANES
CHUNK = 32
GROUP = 16
SLOTS = EXPERTS * CAP
GROUPS_ALL = 2 * EXPERTS // GROUP
ROWS = 2 * EXPERTS * CAP
PAIRS = H // 2
EPS = 1e-05
EVERYONE = ("section", "rep", "shard")
HIGHEST = lax.Precision.HIGHEST
MIB = 1 << 20


def mm(a, b):
    return lax.dot_general(a, b, (((1,), (0,)), ((), ())), preferred_element_type=F32)


def mm_nt(a, b):
    return lax.dot_general(a, b, (((1,), (1,)), ((), ())), preferred_element_type=F32)


def mm_tn(a, b):
    return lax.dot_general(a, b, (((0,), (0,)), ((), ())), preferred_element_type=F32)


def call(kernel, outs, name, flops, moved, vmem=32, **more):
    run = pl.pallas_call(
        kernel,
        out_shape=outs,
        name=name,
        compiler_params=pltpu.CompilerParams(vmem_limit_bytes=vmem * MIB),
        cost_estimate=pl.CostEstimate(flops=flops, bytes_accessed=moved, transcendentals=0),
        **more,
    )

    def placed(*operands):
        return run(*(pltpu.with_memory_space_constraint(x, pltpu.HBM) if x.ndim > 1 else x for x in operands))

    return placed


def shape(*dims, dtype=BF):
    return pltpu.HBM(dims, dtype)


VMEM = pl.BlockSpec(memory_space=pltpu.VMEM)
ANYWHERE = pl.BlockSpec(memory_space=pl.ANY)


def pack_tables():
    row = jnp.arange(GROUP * CAP * COLS, dtype=jnp.int32)[:, None]
    col = jnp.arange(GROUP * CHUNK, dtype=jnp.int32)[None, :]
    block, inside = row // (GROUP * CAP), row % (GROUP * CAP)
    place = (inside // CAP) * CHUNK + block * CAP + inside % CAP
    return (place == col).astype(BF)


def unpack(chunks, table, target):
    size = GROUP * CAP
    for g in range(0, chunks.shape[0] // GROUP, 2):
        raw = [chunks[k * GROUP : (k + 1) * GROUP].reshape(GROUP * CHUNK, LANES) for k in (g, g + 1)]
        rows = mm(table, jnp.concatenate(raw, axis=1)).astype(BF)
        for k in range(2):
            for c in range(COLS):
                target[(g + k) * size : (g + k + 1) * size, c * LANES : (c + 1) * LANES] = rows[
                    c * size : (c + 1) * size, k * LANES : (k + 1) * LANES
                ]


def pack(rows, table_t, target, first):
    size = GROUP * CAP
    for g in range(0, rows.shape[0] // size, 2):
        stacked = jnp.concatenate(
            [
                jnp.concatenate(
                    [rows[k * size : (k + 1) * size, c * LANES : (c + 1) * LANES] for k in (g, g + 1)], axis=1
                )
                for c in range(COLS)
            ],
            axis=0,
        )
        both = mm(table_t, stacked).astype(BF)
        for k in range(2):
            chunk = both[:, k * LANES : (k + 1) * LANES].reshape(GROUP, CHUNK, LANES)
            target[first + (g + k) * GROUP : first + (g + k + 1) * GROUP] = chunk


def pack_for_layer(rows, table_t, target, layer):
    pack(rows, table_t, target, layer * EXPERTS)
    other = (1 - layer) * EXPERTS
    target[other : other + EXPERTS] = jnp.zeros((EXPERTS, CHUNK, LANES), BF)


def slots_by_token(slot_rows):
    places = lax.broadcasted_iota(jnp.int32, (SLOTS, TOK), 0)
    return [jnp.where(places == slot_rows[k : k + 1, :], 1.0, 0.0).astype(BF) for k in range(2)]


def tokens_by_slot(slot_cols):
    places = lax.broadcasted_iota(jnp.int32, (TOK, SLOTS), 1)
    return [jnp.where(places == slot_cols[:, k : k + 1], 1.0, 0.0).astype(BF) for k in range(2)]


def norm_of(hidden, gain):
    scaling = lax.rsqrt(jnp.mean(hidden * hidden, axis=-1, keepdims=True) + EPS)
    return hidden * scaling * gain, scaling


def norm_back(hidden, scaling, gain, grad):
    gain_grad = jnp.sum(grad * hidden * scaling, axis=0, keepdims=True)
    weighted = grad * gain
    inner = jnp.mean(weighted * hidden, axis=-1, keepdims=True)
    return weighted * scaling - hidden * (scaling * scaling * scaling * inner), gain_grad


def bias_tiles_kernel(line_ref, out_ref):
    for h in range(2):
        for delta in range(4):
            line = jnp.broadcast_to(line_ref[h * 4 + delta : h * 4 + delta + 1, :], (BLOCK, 2 * BLOCK))
            turned = pltpu.roll(line, 0, 1, stride=1, stride_axis=0)
            out_ref[h * 4 + delta] = turned[:, :BLOCK].astype(BF)


def bias_tiles(table):
    m = jnp.arange(2 * BLOCK, dtype=jnp.int32)
    ahead = jnp.where(m < BLOCK, m, m - 2 * BLOCK)
    distance = jnp.arange(4, dtype=jnp.int32)[:, None] * BLOCK - ahead[None, :]
    bucket = jnp.clip((distance + BLOCK) * RELB // (SEQ + BLOCK), 0, RELB - 1)
    onehot = (bucket[..., None] == jnp.arange(RELB, dtype=jnp.int32)).astype(F32)
    lines = jnp.einsum("dmb,bh->hdm", onehot, table, precision=HIGHEST).reshape(8, 2 * BLOCK)
    return call(bias_tiles_kernel, shape(8, BLOCK, BLOCK), "bias_tiles", 0, 1 << 20)(lines)


def head_mask(h, rows):
    lane = lax.broadcasted_iota(jnp.int32, (rows, LANES), 1)
    return (lane < HD) if h == 0 else (lane >= HD)


ATT_STEP = 128


def weight_blocks():
    return [(i, h) for i in range(4) for h in range(2)]


def weight_copy(i, h, vmem, hbm, sems, into):
    rows, keys = pl.ds(i * BLOCK, BLOCK), pl.ds(0, (i + 1) * BLOCK)
    ends = vmem.at[h, rows, keys], hbm.at[h, rows, keys]
    return pltpu.make_async_copy(*(ends if into else ends[::-1]), sems.at[h, i])


def attention_kernel(qkv_ref, bias_ref, ctx_ref, weights_hbm, held, sems):
    step = ATT_STEP
    for i in range(4):
        keys = (i + 1) * BLOCK
        key = qkv_ref[0:keys, LANES : 2 * LANES]
        value = qkv_ref[0:keys, 2 * LANES : 3 * LANES]
        for part in range(BLOCK // step):
            first = i * BLOCK + part * step
            query = qkv_ref[first : first + step, 0:LANES] * jnp.asarray(HD**-0.5, BF)
            mixed = []
            for h in range(2):
                mask = head_mask(h, step)
                own = jnp.where(mask, query, jnp.zeros_like(query))
                scores = mm_nt(own, key)
                offset = jnp.concatenate(
                    [bias_ref[h * 4 + i - b, part * step : (part + 1) * step, :] for b in range(i + 1)], axis=1
                ).astype(F32)
                scores = scores + offset
                top = jnp.max(scores, axis=-1, keepdims=True)
                terms = jnp.exp(scores - top)
                total = jnp.sum(terms, axis=-1, keepdims=True)
                weights = (terms * (1.0 / total)).astype(BF)
                held[h, first : first + step, 0:keys] = weights
                mixed.append(mm(weights, value))
            ctx_ref[first : first + step, :] = jnp.where(head_mask(0, step), mixed[0], mixed[1]).astype(BF)
        for h in range(2):
            weight_copy(i, h, held, weights_hbm, sems, True).start()
    for i, h in weight_blocks():
        weight_copy(i, h, held, weights_hbm, sems, True).wait()


def attention(qkv, tiles):
    return call(
        attention_kernel,
        (shape(SEQ, LANES), shape(2, SEQ, SEQ)),
        "attention",
        2 * 2 * 2 * SEQ * SEQ * LANES,
        8 << 20,
        in_specs=[VMEM] * 2,
        out_specs=(VMEM, ANYWHERE),
        scratch_shapes=[pltpu.VMEM((2, SEQ, SEQ), BF), pltpu.SemaphoreType.DMA((2, 4))],
    )(qkv, tiles)


def attention_back_kernel(qkv_ref, weights_hbm, dout_ref, flip_ref, dproj_ref, diag_ref, dkey, dvalue, tiles, held, sems):
    step = ATT_STEP
    for i, h in weight_blocks():
        weight_copy(i, h, held, weights_hbm, sems, False).start()
    dkey[...] = jnp.zeros_like(dkey)
    dvalue[...] = jnp.zeros_like(dvalue)
    for i in range(4):
        keys = (i + 1) * BLOCK
        key = qkv_ref[0:keys, LANES : 2 * LANES]
        value = qkv_ref[0:keys, 2 * LANES : 3 * LANES]
        for h in range(2):
            weight_copy(i, h, held, weights_hbm, sems, False).wait()
        for part in range(BLOCK // step):
            first = i * BLOCK + part * step
            rows = slice(part * step, (part + 1) * step)
            query = qkv_ref[first : first + step, 0:LANES]
            dout = dout_ref[first : first + step, :]
            query_t = query.astype(F32).T.astype(BF)
            dout_t = dout.astype(F32).T.astype(BF)
            moved = []
            for h in range(2):
                own = jnp.where(head_mask(h, step), dout, jnp.zeros_like(dout))
                low = held[h, first : first + step, 0:keys]
                weights = low.astype(F32)
                dweights = mm_nt(own, value)
                delta = jnp.sum(weights * dweights, axis=-1, keepdims=True)
                dscores = weights * (dweights - delta)
                for b in range(i + 1):
                    tile = dscores[:, b * BLOCK : (b + 1) * BLOCK]
                    n = h * 4 + i - b
                    tiles[n, rows, :] = tile if b == 0 else tiles[n, rows, :] + tile
                dlow = dscores.astype(BF)
                moved.append(mm(dlow, key))
                head = slice(h * HD, (h + 1) * HD)
                dkey[head, 0:keys] += mm(query_t[head], dlow)
                dvalue[head, 0:keys] += mm(dout_t[head], low)
            dquery = jnp.where(head_mask(0, step), moved[0], moved[1]) * HD**-0.5
            dproj_ref[first : first + step, 0:LANES] = dquery.astype(BF)
    dproj_ref[:, LANES : 2 * LANES] = (dkey[...] * HD**-0.5).T.astype(BF)
    dproj_ref[:, 2 * LANES : 3 * LANES] = dvalue[...].T.astype(BF)
    for n in range(8):
        tile = tiles[n]
        high = tile.astype(BF)
        rest = (tile - high.astype(F32)).astype(BF)
        flipped = mm(high, flip_ref[...]) + mm(rest, flip_ref[...])
        wide = jnp.concatenate([flipped, jnp.zeros_like(flipped)], axis=1)
        turned = pltpu.roll(wide, 0, 1, stride=1, stride_axis=0)
        diag_ref[n : n + 1, :] = jnp.sum(turned, axis=0, keepdims=True)


def attention_back(qkv, weights, dout):
    at = jnp.arange(BLOCK, dtype=jnp.int32)
    flip = (at[:, None] + at[None, :] == BLOCK - 1).astype(BF)
    return call(
        attention_back_kernel,
        (shape(SEQ, 3 * LANES), shape(8, 2 * BLOCK, dtype=F32)),
        "attention_back",
        2 * 4 * 2 * SEQ * SEQ * LANES,
        8 << 20,
        in_specs=[VMEM, ANYWHERE, VMEM, VMEM],
        out_specs=(VMEM, VMEM),
        scratch_shapes=[
            pltpu.VMEM((LANES, SEQ), F32),
            pltpu.VMEM((LANES, SEQ), F32),
            pltpu.VMEM((8, BLOCK, BLOCK), F32),
            pltpu.VMEM((2, SEQ, SEQ), BF),
            pltpu.SemaphoreType.DMA((2, 4)),
        ],
    )(qkv, weights, dout, flip)


def bias_grad(diag):
    m = jnp.arange(2 * BLOCK, dtype=jnp.int32)
    distance = jnp.arange(4, dtype=jnp.int32)[:, None] * BLOCK + m[None, :] - (BLOCK - 1)
    bucket = jnp.clip((distance + BLOCK) * RELB // (SEQ + BLOCK), 0, RELB - 1)
    onehot = (bucket[..., None] == jnp.arange(RELB, dtype=jnp.int32)).astype(F32)
    return jnp.einsum("hdm,dmb->bh", diag.reshape(2, 4, 2 * BLOCK), onehot, precision=HIGHEST)


def middle_kernel(
    layer, ctx_ref, wao_hbm, hidden_ref, gain_ref, slots_ref, table_ref, middle_ref, out_ref, context_ref, wao_ref, sem
):
    load = pltpu.make_async_copy(wao_hbm.at[layer], wao_ref, sem)
    load.start()
    context = jnp.concatenate([ctx_ref[g] for g in range(PAIRS)], axis=1)
    context_ref[...] = context
    load.wait()
    middle = hidden_ref[...].astype(F32) + mm(context, wao_ref[...])
    middle_ref[...] = middle
    normed = norm_of(middle, gain_ref[layer])[0].astype(BF)
    first, second = slots_by_token(slots_ref[layer])
    rows = mm(first + second, normed).astype(BF)
    pack_for_layer(rows, table_ref[...], out_ref, layer)


def weight_space(columns):
    return [pltpu.VMEM((D, columns), BF), pltpu.SemaphoreType.DMA]


def middle_part(layer, ctx, wao, hidden, gain, slot_rows, table_t):
    return call(
        partial(middle_kernel, layer),
        (shape(TOK, D, dtype=F32), shape(2 * EXPERTS, CHUNK, LANES), shape(TOK, D)),
        "middle",
        2 * TOK * D * D + 2 * SLOTS * TOK * D * 5,
        4 << 20,
        in_specs=[VMEM, ANYWHERE, VMEM, VMEM, VMEM, VMEM],
        scratch_shapes=weight_space(D),
    )(ctx, wao, hidden, gain, slot_rows, table_t)


def combined(layer, back_ref, middle_ref, slots_ref, gates_ref, table_ref, rows):
    unpack(back_ref.at[layer * EXPERTS : (layer + 1) * EXPERTS], table_ref[...], rows)
    picks = tokens_by_slot(slots_ref[layer])
    gates = gates_ref[layer]
    total = middle_ref[...]
    for k in range(2):
        total = total + gates[:, k : k + 1] * mm(picks[k], rows[...])
    return total.astype(BF)


def combine_kernel(layer, back_ref, middle_ref, slots_ref, gates_ref, table_ref, out_ref, rows):
    out_ref[...] = combined(layer, back_ref, middle_ref, slots_ref, gates_ref, table_ref, rows)


def combine(layer, back, middle, slot_cols, gates, table):
    return call(
        partial(combine_kernel, layer),
        shape(TOK, D),
        "combine",
        2 * TOK * SLOTS * D * 6,
        4 << 20,
        in_specs=[VMEM, VMEM, VMEM, VMEM, VMEM],
        scratch_shapes=[pltpu.VMEM((SLOTS, D), BF)],
    )(back, middle, slot_cols, gates, table)


def send_grads(layer, dout, slot_rows, gates, table_t, out_ref):
    first, second = slots_by_token(slot_rows)
    wide = dout.astype(F32)
    rows = mm(first, (wide * gates[:, 0:1]).astype(BF)) + mm(second, (wide * gates[:, 1:2]).astype(BF))
    pack_for_layer(rows.astype(BF), table_t, out_ref, layer)


def grad_rows_kernel(dout_ref, slots_ref, gates_ref, table_ref, out_ref):
    for m in range(2):
        first, second = slots_by_token(slots_ref[m])
        gates = gates_ref[m]
        wide = dout_ref[m].astype(F32)
        rows = mm(first, (wide * gates[:, 0:1]).astype(BF)) + mm(second, (wide * gates[:, 1:2]).astype(BF))
        pack(rows.astype(BF), table_ref[...], out_ref.at[:, m], 0)


def grad_rows(dout, slot_rows, gates, table_t):
    return call(
        grad_rows_kernel,
        shape(EXPERTS, 2, CHUNK, LANES),
        "grad_rows",
        4 * TOK * SLOTS * D * 6,
        2 << 20,
    )(dout, slot_rows, gates, table_t)


def middle_back_kernel(
    layer, back_ref, slots_ref, table_ref, dout_ref, middle_ref, gain_ref, wao_hbm, dmid_ref, branch_ref, send_ref, dgain_ref,
    rows, wao_ref, sem,
):
    load = pltpu.make_async_copy(wao_hbm.at[layer], wao_ref, sem)
    load.start()
    unpack(back_ref.at[layer * EXPERTS : (layer + 1) * EXPERTS], table_ref[...], rows)
    first, second = tokens_by_slot(slots_ref[layer])
    dnormed = mm(first + second, rows[...])
    middle = middle_ref[...]
    gain = gain_ref[layer]
    scaling = lax.rsqrt(jnp.mean(middle * middle, axis=-1, keepdims=True) + EPS)
    moved, dgain = norm_back(middle, scaling, gain, dnormed)
    dgain_ref[...] = dgain
    dmid = dout_ref[...].astype(F32) + moved
    dmid_ref[...] = dmid
    branch = dmid.astype(BF)
    branch_ref[...] = branch
    load.wait()
    dcontext = mm_nt(branch, wao_ref[...]).astype(BF)
    for g in range(PAIRS):
        send_ref[g] = dcontext[:, g * LANES : (g + 1) * LANES]
    send_ref[PAIRS:8] = jnp.zeros((8 - PAIRS, TOK, LANES), BF)


def middle_back(layer, back, slot_cols, table, dout, middle, gain, wao):
    return call(
        partial(middle_back_kernel, layer),
        (shape(TOK, D, dtype=F32), shape(TOK, D), shape(8, TOK, LANES), shape(1, D, dtype=F32)),
        "middle_back",
        2 * TOK * D * D + 2 * TOK * SLOTS * D * 5,
        4 << 20,
        in_specs=[VMEM] * 6 + [ANYWHERE],
        scratch_shapes=[pltpu.VMEM((SLOTS, D), BF)] + weight_space(D),
    )(back, slot_cols, table, dout, middle, gain, wao)


def hidden_grad(layer, back_ref, wqkv_hbm, hidden_ref, gain_ref, dmid_ref, wqkv_ref, sem):
    load = pltpu.make_async_copy(wqkv_hbm.at[layer], wqkv_ref, sem)
    load.start()
    parts = [
        back_ref[g, :, part * LANES : (part + 1) * LANES] for part in range(3) for g in range(PAIRS)
    ]
    hidden = hidden_ref[...].astype(F32)
    scaling = lax.rsqrt(jnp.mean(hidden * hidden, axis=-1, keepdims=True) + EPS)
    load.wait()
    dnormed = mm_nt(jnp.concatenate(parts, axis=1), wqkv_ref[...])
    moved, _ = norm_back(hidden, scaling, gain_ref[layer], dnormed)
    return (dmid_ref[...] + moved).astype(BF)


def hidden_back_kernel(layer, back_ref, wqkv_hbm, hidden_ref, gain_ref, dmid_ref, dh_ref, wqkv_ref, sem):
    dh_ref[...] = hidden_grad(layer, back_ref, wqkv_hbm, hidden_ref, gain_ref, dmid_ref, wqkv_ref, sem)


def hidden_back_send_kernel(
    layer, back_ref, wqkv_hbm, hidden_ref, gain_ref, dmid_ref, slots_ref, gates_ref, table_ref, dh_ref, out_ref, wqkv_ref, sem
):
    dh = hidden_grad(layer, back_ref, wqkv_hbm, hidden_ref, gain_ref, dmid_ref, wqkv_ref, sem)
    dh_ref[...] = dh
    send_grads(layer - 1, dh, slots_ref[layer - 1], gates_ref[layer - 1], table_ref[...], out_ref)


def hidden_back(layer, back, wqkv, hidden, gain, dmid):
    return call(
        partial(hidden_back_kernel, layer),
        shape(TOK, D),
        "hidden_back",
        2 * TOK * D * 3 * D,
        5 << 20,
        in_specs=[VMEM, ANYWHERE, VMEM, VMEM, VMEM],
        scratch_shapes=weight_space(3 * D),
    )(back, wqkv, hidden, gain, dmid)


def hidden_back_send(layer, back, wqkv, hidden, gain, dmid, slot_rows, gates, table_t):
    return call(
        partial(hidden_back_send_kernel, layer),
        (shape(TOK, D), shape(2 * EXPERTS, CHUNK, LANES)),
        "hidden_back_send",
        2 * TOK * D * 3 * D,
        6 << 20,
        in_specs=[VMEM, ANYWHERE] + [VMEM] * 6,
        scratch_shapes=weight_space(3 * D),
    )(back, wqkv, hidden, gain, dmid, slot_rows, gates, table_t)


FF_STEP = 1024
ROW_STEP = 320
CHUNKS = (2 * EXPERTS, CHUNK, LANES)


def gelu_parts(up):
    phi = 0.5 + 0.5 * lax.erf(up * 0.5**0.5)
    return up * phi, phi + up * (jnp.exp(up * up * -0.5) * 0.3989422804014327)


def row_blocks():
    return [slice(r, r + ROW_STEP) for r in range(0, ROWS, ROW_STEP)]


def over_hidden_units(one, weights, buffers, targets, sems):
    def copy(f, slot, k):
        columns = pl.ds(pl.multiple_of(f * FF_STEP, FF_STEP), FF_STEP)
        return pltpu.make_async_copy(buffers[k].at[slot], targets[k].at[:, columns], sems.at[slot, k])

    def step(f, carry):
        slot = lax.rem(f, 2)

        @pl.when(f >= 2)
        def _():
            for k in range(len(buffers)):
                copy(f - 2, slot, k).wait()

        for load in weights(f):
            load.wait()
        one(pl.ds(pl.multiple_of(f * FF_STEP, FF_STEP), FF_STEP), [b.at[slot] for b in buffers])
        for k in range(len(buffers)):
            copy(f, slot, k).start()
        return carry

    last = FF // FF_STEP
    lax.fori_loop(0, last, step, 0)
    for f in range(last - 2, last):
        for k in range(len(buffers)):
            copy(f, f % 2, k).wait()


def start_weights(win_hbm, wout_hbm, win_ref, wout_ref, sems, slope_hbm=None, slope=None):
    def copies(f):
        units = pl.ds(pl.multiple_of(f * FF_STEP, FF_STEP), FF_STEP)
        loads = [
            pltpu.make_async_copy(win_hbm.at[:, units], win_ref.at[:, units], sems.at[f, 0]),
            pltpu.make_async_copy(wout_hbm.at[units, :], wout_ref.at[units, :], sems.at[f, 1]),
        ]
        if slope is not None:
            loads.append(pltpu.make_async_copy(slope_hbm.at[:, units], slope.at[:, units], sems.at[f, 2]))
        return loads

    for f in range(FF // FF_STEP):
        for load in copies(f):
            load.start()
    return copies


def expert_space():
    return [
        pltpu.VMEM((D, FF), BF),
        pltpu.VMEM((FF, D), BF),
        pltpu.SemaphoreType.DMA((FF // FF_STEP, 3)),
    ]


def held_blocks():
    return pltpu.VMEM((2, ROWS, FF_STEP), BF)


def expert_forward_kernel(
    in_ref, win_hbm, wout_hbm, table_ref, table_t_ref, x_ref, act_hbm, slope_hbm, out_ref,
    win_ref, wout_ref, weight_sems, total, act_held, slope_held, sems,
):
    weights = start_weights(win_hbm, wout_hbm, win_ref, wout_ref, weight_sems)
    unpack(in_ref, table_ref[...], x_ref)
    total[...] = jnp.zeros_like(total)

    def one(columns, held):
        blocks = row_blocks()
        ups = mm(x_ref[blocks[0], :], win_ref[:, columns])
        for n, rows in enumerate(blocks):
            up = ups
            if n + 1 < len(blocks):
                ups = mm(x_ref[blocks[n + 1], :], win_ref[:, columns])
            act, slope = gelu_parts(up)
            act = act.astype(BF)
            held[0][rows, :] = act
            held[1][rows, :] = slope.astype(BF)
            total[rows, :] += mm(act, wout_ref[columns, :])

    over_hidden_units(one, weights, [act_held, slope_held], [act_hbm, slope_hbm], sems)
    pack(total[...].astype(BF), table_t_ref[...], out_ref, 0)


def expert_forward(arrived, first, second, table, table_t):
    return call(
        expert_forward_kernel,
        (shape(ROWS, D), shape(ROWS, FF), shape(ROWS, FF), shape(*CHUNKS)),
        "expert_forward",
        4 * ROWS * D * FF,
        20 << 20,
        vmem=40,
        in_specs=[VMEM, ANYWHERE, ANYWHERE, VMEM, VMEM],
        out_specs=(VMEM, ANYWHERE, ANYWHERE, VMEM),
        scratch_shapes=expert_space()
        + [pltpu.VMEM((ROWS, D), F32), held_blocks(), held_blocks(), pltpu.SemaphoreType.DMA((2, 2))],
    )(arrived, first, second, table, table_t)


def expert_back_kernel(
    in_ref, win_hbm, wout_hbm, slope_hbm, table_ref, table_t_ref, grad_ref, dup_hbm, out_ref,
    win_ref, wout_ref, weight_sems, total, slope, dup_held, sems,
):
    weights = start_weights(win_hbm, wout_hbm, win_ref, wout_ref, weight_sems, slope_hbm, slope)
    unpack(in_ref, table_ref[...], grad_ref)
    total[...] = jnp.zeros_like(total)

    def one(columns, held):
        blocks = row_blocks()
        dacts = mm_nt(grad_ref[blocks[0], :], wout_ref[columns, :])
        for n, rows in enumerate(blocks):
            dact = dacts
            if n + 1 < len(blocks):
                dacts = mm_nt(grad_ref[blocks[n + 1], :], wout_ref[columns, :])
            dup = (dact * slope[rows, columns].astype(F32)).astype(BF)
            held[0][rows, :] = dup
            total[rows, :] += mm_nt(dup, win_ref[:, columns])

    over_hidden_units(one, weights, [dup_held], [dup_hbm], sems)
    pack(total[...].astype(BF), table_t_ref[...], out_ref, 0)


def expert_back(arrived, first, second, slope, table, table_t):
    return call(
        expert_back_kernel,
        (shape(ROWS, D), shape(ROWS, FF), shape(*CHUNKS)),
        "expert_back",
        4 * ROWS * D * FF,
        20 << 20,
        vmem=40,
        in_specs=[VMEM, ANYWHERE, ANYWHERE, ANYWHERE, VMEM, VMEM],
        out_specs=(VMEM, ANYWHERE, VMEM),
        scratch_shapes=expert_space()
        + [
            pltpu.VMEM((ROWS, D), F32),
            pltpu.VMEM((ROWS, FF), BF),
            held_blocks(),
            pltpu.SemaphoreType.DMA((2, 1)),
        ],
    )(arrived, first, second, slope, table, table_t)


def expert_both_kernel(
    in_ref, gin_ref, win_hbm, wout_hbm, table_ref, table_t_ref, x_ref, grad_ref, act_hbm, dup_hbm, out_ref, back_ref,
    win_ref, wout_ref, weight_sems, total, dtotal, act_held, dup_held, sems,
):
    weights = start_weights(win_hbm, wout_hbm, win_ref, wout_ref, weight_sems)
    unpack(in_ref, table_ref[...], x_ref)
    for m in range(2):
        unpack(gin_ref.at[:, m], table_ref[...], grad_ref.at[m * SLOTS : (m + 1) * SLOTS])
    total[...] = jnp.zeros_like(total)
    dtotal[...] = jnp.zeros_like(dtotal)

    def one(columns, held):
        blocks = row_blocks()

        def first_products(rows):
            return mm(x_ref[rows, :], win_ref[:, columns]), mm_nt(grad_ref[rows, :], wout_ref[columns, :])

        ahead = first_products(blocks[0])
        for n, rows in enumerate(blocks):
            up, dact = ahead
            if n + 1 < len(blocks):
                ahead = first_products(blocks[n + 1])
            act, slope = gelu_parts(up)
            dup = (dact * slope).astype(BF)
            act = act.astype(BF)
            held[0][rows, :] = act
            held[1][rows, :] = dup
            total[rows, :] += mm(act, wout_ref[columns, :])
            dtotal[rows, :] += mm_nt(dup, win_ref[:, columns])

    over_hidden_units(one, weights, [act_held, dup_held], [act_hbm, dup_hbm], sems)
    pack(dtotal[...].astype(BF), table_t_ref[...], back_ref, 0)
    pack(total[...].astype(BF), table_t_ref[...], out_ref, 0)


def expert_both(arrived, grads, first, second, table, table_t):
    return call(
        expert_both_kernel,
        (shape(ROWS, D), shape(ROWS, D), shape(ROWS, FF), shape(ROWS, FF), shape(*CHUNKS), shape(*CHUNKS)),
        "expert_both",
        8 * ROWS * D * FF,
        24 << 20,
        vmem=44,
        in_specs=[VMEM, VMEM, ANYWHERE, ANYWHERE, VMEM, VMEM],
        out_specs=(VMEM, VMEM, ANYWHERE, ANYWHERE, VMEM, VMEM),
        scratch_shapes=expert_space()
        + [
            pltpu.VMEM((ROWS, D), F32),
            pltpu.VMEM((ROWS, D), F32),
            held_blocks(),
            held_blocks(),
            pltpu.SemaphoreType.DMA((2, 2)),
        ],
    )(arrived, grads, first, second, table, table_t)


ROWS_OWN = 96
TAIL = 16


def parcel_kernel(w_ref, tail_ref, out_ref):
    for g in range(8):
        for part in range(3):
            lanes = slice(part * LANES, (part + 1) * LANES)
            if g < PAIRS:
                block = w_ref[:, part * D + g * LANES : part * D + (g + 1) * LANES]
            else:
                block = jnp.zeros((ROWS_OWN, LANES), BF)
            out_ref[g, 0:ROWS_OWN, lanes] = block
            out_ref[8 + g, 0:ROWS_OWN, lanes] = block
        out_ref[g, ROWS_OWN:, :] = tail_ref[...]
        out_ref[8 + g, ROWS_OWN:, :] = tail_ref[...]


def parcels_of(w_qkv, gain_attn, gain_ffn, rel_bias):
    row = jnp.concatenate([gain_attn.reshape(1, -1), gain_ffn.reshape(1, -1), rel_bias.reshape(1, -1)], axis=1)
    tail = jnp.pad(row, ((0, TAIL - 1), (0, 3 * LANES - row.shape[1])))
    return call(parcel_kernel, shape(16, ROWS_OWN + TAIL, 3 * LANES), "parcels", 0, 2 << 20)(w_qkv, tail)


def small_parts(parcels):
    rows = parcels[:, ROWS_OWN].astype(F32).reshape(2, 8, 3 * LANES)
    gain_a = rows[:, :, :ROWS_OWN].reshape(2, 1, D)
    gain_f = rows[:, :, ROWS_OWN : 2 * ROWS_OWN].reshape(2, 1, D)
    bias = rows[:, :, 2 * ROWS_OWN : 2 * ROWS_OWN + 4 * H].reshape(2, RELB, H)
    first = 2 * jnp.minimum(lax.axis_index("shard"), PAIRS - 1)
    return gain_a, gain_f, lax.dynamic_slice_in_dim(bias, first, 2, 2)


def project_kernel(layer, shard_ref, parcel_ref, gain_ref, *refs):
    blocks, normed_ref, qkv_ref = refs[:8], refs[8], refs[9]
    own = jnp.concatenate([parcel_ref[layer * 8 + j, 0:ROWS_OWN, :] for j in range(8)], axis=0)
    shard = shard_ref[0]
    for n in range(8):
        back, other = n % 4, n // 4
        source = lax.rem(shard + 8 - 2 * back, 8)
        if other:
            source = source + 1 - 2 * lax.rem(source, 2)
        rows = pl.ds(pl.multiple_of(source * TOK, TOK), TOK)
        normed = norm_of(blocks[n][...].astype(F32), gain_ref[layer])[0].astype(BF)
        normed_ref[rows, :] = normed
        qkv_ref[rows, :] = mm(normed, own).astype(BF)


def project(layer, shard, parcels, gain, blocks):
    return call(
        partial(project_kernel, layer),
        (shape(SEQ, D), shape(SEQ, 3 * LANES)),
        "project",
        2 * SEQ * D * 3 * LANES,
        5 << 20,
        in_specs=[pl.BlockSpec(memory_space=pltpu.SMEM)] + [VMEM] * 10,
    )(shard, parcels, gain, *blocks)


WIDE = 4 * LANES


def dense_grads_kernel(layer, shard_ref, normed_ref, dproj_ref, context_ref, branch_ref, tail_ref, *refs):
    out_hbm, held, sem = refs[-3:]
    dqkv = mm_tn(normed_ref[...], dproj_ref[...]).astype(BF)
    group = jnp.minimum(shard_ref[0], PAIRS - 1)
    columns = pl.ds(pl.multiple_of(group * LANES, LANES), LANES)
    dao = mm_tn(context_ref[...], branch_ref[:, columns]).astype(BF)
    for r in range(8):
        rows = slice(r * ROWS_OWN, (r + 1) * ROWS_OWN)
        held[r, 0:ROWS_OWN, 0 : 3 * LANES] = dqkv[rows]
        held[r, 0:ROWS_OWN, 3 * LANES :] = dao[rows]
        held[r, ROWS_OWN:, :] = tail_ref[r]
    store = pltpu.make_async_copy(held, out_hbm.at[layer * 8 : (layer + 1) * 8], sem)
    store.start()
    store.wait()


def dense_grads(layer, shard, normed, dproj, context, branch, dgain_f, diag, filled=None):
    gains = jnp.pad(dgain_f.reshape(8, ROWS_OWN), ((0, 0), (0, LANES - ROWS_OWN)))
    biases = jnp.pad(bias_grad(diag).reshape(8, 8), ((0, 0), (0, 3 * LANES - 8)))
    tail = jnp.pad(jnp.concatenate([gains, biases], axis=1)[:, None].astype(BF), ((0, 0), (0, TAIL - 1), (0, 0)))
    more = () if filled is None else (filled,)
    return call(
        partial(dense_grads_kernel, layer),
        shape(16, ROWS_OWN + TAIL, WIDE),
        "dense_grads",
        2 * SEQ * D * WIDE,
        6 << 20,
        in_specs=[pl.BlockSpec(memory_space=pltpu.SMEM)] + [VMEM] * 5 + [ANYWHERE] * len(more),
        out_specs=ANYWHERE,
        scratch_shapes=[pltpu.VMEM((8, ROWS_OWN + TAIL, WIDE), BF), pltpu.SemaphoreType.DMA],
        input_output_aliases={6: 0} if more else {},
    )(shard, normed, dproj, context, branch, tail, *more)


def finish_kernel(rep_ref, w_ref, gain_ref, *refs):
    blocks, (qkv_ref, ao_ref, gain_a_ref, gain_f_ref, bias_ref, products) = refs[:8], refs[8:]
    rep = rep_ref[0]
    gain_f_ref[...] = jnp.zeros_like(gain_f_ref)
    products[...] = jnp.zeros_like(products)
    for n in range(8):
        other, back = n // 4, n % 4
        group = lax.rem(rep + 4 - back, 4) + lax.rem(rep // 4 + other, 2) * 4
        block = blocks[n][0:ROWS_OWN, :].astype(F32)
        extra = blocks[n][ROWS_OWN:, 0 : 2 * LANES].astype(F32)
        gain_f_ref[...] += extra[0:1, 0:ROWS_OWN]
        bias_ref[pl.ds(group, 1), :] = extra[0:1, LANES:]

        @pl.when(group < PAIRS)
        def _(block=block, group=group):
            for part in range(3):
                columns = pl.ds(pl.multiple_of(part * D + group * LANES, LANES), LANES)
                grad = block[:, part * LANES : (part + 1) * LANES]
                qkv_ref[:, columns] = grad
                products[...] += grad * w_ref[:, columns].astype(F32)
            ao_ref[:, pl.ds(pl.multiple_of(group * LANES, LANES), LANES)] = block[:, 3 * LANES :]

    sums = lax.dot_general(
        jnp.ones((8, LANES), F32), products[...], (((1,), (1,)), ((), ())), precision=HIGHEST, preferred_element_type=F32
    )
    gain_a_ref[...] = sums[0:1, :] / gain_ref[...]


def finish(rep, w_qkv, gain, blocks):
    return call(
        finish_kernel,
        (
            shape(ROWS_OWN, 3 * D, dtype=F32),
            shape(ROWS_OWN, D, dtype=F32),
            shape(1, ROWS_OWN, dtype=F32),
            shape(1, ROWS_OWN, dtype=F32),
            shape(8, LANES, dtype=F32),
        ),
        "finish",
        0,
        2 << 20,
        in_specs=[pl.BlockSpec(memory_space=pltpu.SMEM)] + [VMEM] * 10,
        scratch_shapes=[pltpu.VMEM((ROWS_OWN, LANES), F32)],
    )(rep, w_qkv, gain, *blocks)


def spread(chunks):
    return lax.all_to_all(chunks, EVERYONE, split_axis=0, concat_axis=0, tiled=True)


def across(chunks):
    return lax.all_to_all(chunks, "shard", split_axis=0, concat_axis=0, tiled=True)


def swap(value):
    return lax.ppermute(value, "section", [(0, 1), (1, 0)])


def after(value, *others):
    return lax.optimization_barrier((value, *others))[0]


def tokens_of_all(own):
    n = 8

    def from_chip(back):
        return lax.ppermute(own, "shard", [(j, (j + 2 * back) % n) for j in range(n)])

    same_core = [own, from_chip(1), from_chip(2), from_chip(3)]
    return same_core + [lax.ppermute(block, "shard", [(j, j ^ 1) for j in range(n)]) for block in same_core]


def slot_tables(routes):
    flat = routes.reshape(2, 2 * TOK)
    onehot = (flat[..., None] == jnp.arange(EXPERTS, dtype=jnp.int32)).astype(BF)
    at = jnp.arange(2 * TOK, dtype=jnp.int32)
    earlier = (at[None, :] < at[:, None]).astype(BF)
    before = jnp.einsum("ab,lbe->lae", earlier, onehot, preferred_element_type=F32)
    rank = jnp.sum(before * onehot.astype(F32), axis=-1).astype(jnp.int32)
    return (flat * CAP + rank).reshape(routes.shape)


def per_device(
    inputs, cotangent, w_qkv, w_attn_out, gain_attn, gain_ffn, rel_bias, w_in, w_out, routes, gates
):
    section = lax.axis_index("section")
    shard = lax.axis_index("shard")
    first_proj, second_proj = w_in[0, 0], w_out[0, 0]
    hidden0 = lax.dynamic_index_in_dim(inputs[:, 0], section, 0, keepdims=False)
    cot = lax.dynamic_index_in_dim(cotangent[:, 0], section, 0, keepdims=False)
    table = pack_tables()
    table_t = table.T

    full0 = tokens_of_all(hidden0)
    got = lax.all_to_all(
        after(parcels_of(w_qkv[0], gain_attn, gain_ffn, rel_bias[0]), *full0[1:]),
        ("section", "shard"),
        split_axis=0,
        concat_axis=0,
        tiled=True,
    )
    gain_a, gain_f, bias = small_parts(got)
    tiles = [bias_tiles(bias[l]) for l in range(2)]
    w_ao = lax.all_gather(after(w_attn_out[0], got), ("section", "shard"), axis=0, tiled=True).reshape(2, D, D)

    def both_layers(values):
        own = lax.dynamic_index_in_dim(values[0, :, 0], section, 0, keepdims=False)
        other = swap(lax.dynamic_index_in_dim(values[0, :, 0], 1 - section, 0, keepdims=False))
        return jnp.where(section == 0, jnp.stack([own, other]), jnp.stack([other, own]))

    slot_cols = slot_tables(both_layers(routes))
    slot_rows = slot_cols.transpose(0, 2, 1)
    gate_cols = both_layers(gates)

    own_slots = slot_tables(routes[0, :, 0]).transpose(0, 2, 1)
    own_grads = grad_rows(cotangent[:, 0], own_slots, gates[0, :, 0], table_t)

    own_index = shard.reshape(1)
    normed0, qkv0 = project(0, own_index, got, gain_a, full0)
    ctx0, weights0 = attention(qkv0, tiles[0])
    ctx0_tok = across(ctx0.reshape(8, TOK, LANES))
    middle0, send, ctx0_own = middle_part(0, ctx0_tok, w_ao, hidden0, gain_f, slot_rows, table_t)
    arrived = spread(send)
    grads1 = lax.all_to_all(
        after(own_grads, arrived), ("rep", "shard"), split_axis=0, concat_axis=0, tiled=True
    )
    x0, act0, slope0, made = expert_forward(arrived, first_proj, second_proj, table, table_t)
    back = spread(after(made, grads1))
    ctx0_full = lax.all_gather(ctx0_own, "shard", axis=0, tiled=True)
    w_full = lax.all_gather(after(w_qkv[0], arrived), ("section", "shard"), axis=0, tiled=True).reshape(2, D, 3 * D)
    out0 = combine(0, back, middle0, slot_cols, gate_cols, table)

    normed1, qkv1 = project(1, own_index, got, gain_a, tokens_of_all(out0))
    ctx1, weights1 = attention(qkv1, tiles[1])
    ctx1_tok = across(ctx1.reshape(8, TOK, LANES))
    middle1, send, ctx1_own = middle_part(1, ctx1_tok, w_ao, out0, gain_f, slot_rows, table_t)
    ctx1_full = lax.all_gather(ctx1_own, "shard", axis=0, tiled=True)
    x1, g1, act1, dup1, made1, dmade1 = expert_both(spread(send), grads1, first_proj, second_proj, table, table_t)

    back = spread(dmade1)
    dmid1, branch1, send, dgain_f1 = middle_back(1, back, slot_cols, table, cot, middle1, gain_f, w_ao)
    branch1_full = lax.all_gather(branch1, "shard", axis=0, tiled=True)
    dproj1, diag1 = attention_back(qkv1, weights1, across(send).reshape(SEQ, LANES))
    dproj1_tok = across(dproj1.reshape(8, TOK, 3 * LANES))
    dh1, send = hidden_back_send(1, dproj1_tok, w_full, out0, gain_a, dmid1, slot_rows, gate_cols, table_t)

    arrived = spread(send)
    made1_back = spread(after(made1, arrived))
    out1 = combine(1, made1_back, middle1, slot_cols, gate_cols, table)
    g0, dup0, dmade0 = expert_back(arrived, first_proj, second_proj, slope0, table, table_t)
    back = spread(after(dmade0, made1_back))
    dmid0, branch0, send, dgain_f0 = middle_back(0, back, slot_cols, table, dh1, middle0, gain_f, w_ao)
    branch0_full = lax.all_gather(branch0, "shard", axis=0, tiled=True)
    dproj0, diag0 = attention_back(qkv0, weights0, across(send).reshape(SEQ, LANES))

    dproj0_tok = across(dproj0.reshape(8, TOK, 3 * LANES))
    parcels = dense_grads(1, own_index, normed1, dproj1, ctx1_full, branch1_full, dgain_f1, diag1)
    parcels = dense_grads(0, own_index, normed0, dproj0, ctx0_full, branch0_full, dgain_f0, diag0, parcels)
    parcels = after(parcels, dproj0_tok)
    got = lax.all_to_all(parcels, ("section", "rep"), split_axis=0, concat_axis=0, tiled=True)

    def own(a, b):
        return jnp.where(section == 0, a, b)

    grad_in = mm_tn(own(x0, x1), own(dup0, dup1))
    grad_out = mm_tn(own(act0, act1), own(g0, g1))
    dh0 = hidden_back(0, dproj0_tok, w_full, hidden0, gain_a, dmid0)
    got, grad_in, grad_out, dh0 = lax.optimization_barrier((got, grad_in, grad_out, dh0))
    summed = jnp.sum(got.astype(F32), axis=0).astype(BF)

    block = lax.ppermute(summed, ("rep", "shard"), [(a * 8 + b, b * 8 + a) for a in range(8) for b in range(8)])
    blocks = [block] + [
        lax.ppermute(block, "rep", [(r, r // 4 * 4 + (r + k) % 4) for r in range(8)]) for k in range(1, 4)
    ]
    blocks = blocks + [lax.ppermute(b, "rep", [(r, (r + 4) % 8) for r in range(8)]) for b in blocks]
    grad_qkv, grad_ao, dgain_a, dgain_f, drel = finish(
        lax.axis_index("rep").reshape(1), w_qkv[0], gain_attn.astype(F32), blocks
    )
    grad_bias = drel[:PAIRS, :8].reshape(PAIRS, 4, 2).transpose(1, 0, 2).reshape(1, 4, H)

    def by_layer(layer0, layer1):
        keep = jnp.where(section == 0, layer0, layer1)
        other = swap(jnp.where(section == 0, layer1, layer0))
        pair = jnp.where(section == 0, jnp.stack([keep, other]), jnp.stack([other, keep]))
        return pair.reshape(1, 2, 1, TOK, D)

    return (
        by_layer(out0, out1),
        by_layer(dh0, dh1),
        grad_qkv[None],
        grad_ao[None],
        dgain_a,
        dgain_f,
        grad_bias,
        grad_in[None, None],
        grad_out[None, None],
    )


def solution(mesh):
    placed = (
        P(None, "rep", "shard", None),
        P(None, "rep", "shard", None),
        P("section", "shard", None),
        P("section", "shard", None),
        P("section", "shard"),
        P("section", "shard"),
        P("section", "shard", None),
        P("section", ("rep", "shard"), None, None),
        P("section", ("rep", "shard"), None, None),
        P("section", None, "rep", "shard", None),
        P("section", None, "rep", "shard", None),
    )
    return jax.shard_map(
        per_device,
        mesh=mesh,
        in_specs=placed,
        out_specs=(
            P("section", None, "rep", "shard", None),
            P("section", None, "rep", "shard", None),
            P("section", "shard", None),
            P("section", "shard", None),
            P("section", "shard"),
            P("section", "shard"),
            P("section", "shard", None),
            P("section", ("rep", "shard"), None, None),
            P("section", ("rep", "shard"), None, None),
        ),
        check_vma=False,
    )
```

```python
from functools import partial

import jax
import jax.numpy as jnp
from jax import lax
from jax.experimental import pallas as pl
from jax.experimental.pallas import tpu as pltpu
from jax.sharding import PartitionSpec as P

F32 = jnp.float32
BF = jnp.bfloat16
D = 768
H = 12
HD = 64
FF = 3072
SEQ = 1024
TOK = 128
BLOCK = 256
RELB = 32
EXPERTS = 64
CAP = 5
LANES = 128
COLS = D // LANES
CHUNK = 32
GROUP = 16
SLOTS = EXPERTS * CAP
GROUPS_ALL = 2 * EXPERTS // GROUP
ROWS = 2 * EXPERTS * CAP
PAIRS = H // 2
EPS = 1e-05
EVERYONE = ("section", "rep", "shard")
HIGHEST = lax.Precision.HIGHEST
MIB = 1 << 20


def mm(a, b):
    return lax.dot_general(a, b, (((1,), (0,)), ((), ())), preferred_element_type=F32)


def mm_nt(a, b):
    return lax.dot_general(a, b, (((1,), (1,)), ((), ())), preferred_element_type=F32)


def mm_tn(a, b):
    return lax.dot_general(a, b, (((0,), (0,)), ((), ())), preferred_element_type=F32)


def call(kernel, outs, name, flops, moved, vmem=32, free=(), **more):
    run = pl.pallas_call(
        kernel,
        out_shape=outs,
        name=name,
        compiler_params=pltpu.CompilerParams(vmem_limit_bytes=vmem * MIB),
        cost_estimate=pl.CostEstimate(flops=flops, bytes_accessed=moved, transcendentals=0),
        **more,
    )

    def placed(*operands):
        return run(
            *(
                x if x.ndim == 1 or n in free else pltpu.with_memory_space_constraint(x, pltpu.HBM)
                for n, x in enumerate(operands)
            )
        )

    return placed


def shape(*dims, dtype=BF):
    return pltpu.HBM(dims, dtype)


VMEM = pl.BlockSpec(memory_space=pltpu.VMEM)
ANYWHERE = pl.BlockSpec(memory_space=pl.ANY)


def pack_tables():
    row = jnp.arange(GROUP * CAP * COLS, dtype=jnp.int32)[:, None]
    col = jnp.arange(GROUP * CHUNK, dtype=jnp.int32)[None, :]
    block, inside = row // (GROUP * CAP), row % (GROUP * CAP)
    place = (inside // CAP) * CHUNK + block * CAP + inside % CAP
    return (place == col).astype(BF)


def unpack(chunks, table, target):
    size = GROUP * CAP
    for g in range(0, chunks.shape[0] // GROUP, 2):
        raw = [chunks[k * GROUP : (k + 1) * GROUP].reshape(GROUP * CHUNK, LANES) for k in (g, g + 1)]
        rows = mm(table, jnp.concatenate(raw, axis=1)).astype(BF)
        for k in range(2):
            for c in range(COLS):
                target[(g + k) * size : (g + k + 1) * size, c * LANES : (c + 1) * LANES] = rows[
                    c * size : (c + 1) * size, k * LANES : (k + 1) * LANES
                ]


def pack(rows, table_t, target, first):
    size = GROUP * CAP
    for g in range(0, rows.shape[0] // size, 2):
        stacked = jnp.concatenate(
            [
                jnp.concatenate(
                    [rows[k * size : (k + 1) * size, c * LANES : (c + 1) * LANES] for k in (g, g + 1)], axis=1
                )
                for c in range(COLS)
            ],
            axis=0,
        )
        both = mm(table_t, stacked).astype(BF)
        for k in range(2):
            chunk = both[:, k * LANES : (k + 1) * LANES].reshape(GROUP, CHUNK, LANES)
            target[first + (g + k) * GROUP : first + (g + k + 1) * GROUP] = chunk


def slots_by_token(slot_rows):
    places = lax.broadcasted_iota(jnp.int32, (SLOTS, TOK), 0)
    return [jnp.where(places == slot_rows[k : k + 1, :], 1.0, 0.0).astype(BF) for k in range(2)]


def tokens_by_slot(slot_cols):
    places = lax.broadcasted_iota(jnp.int32, (TOK, SLOTS), 1)
    return [jnp.where(places == slot_cols[:, k : k + 1], 1.0, 0.0).astype(BF) for k in range(2)]


def norm_of(hidden, gain):
    scaling = lax.rsqrt(jnp.mean(hidden * hidden, axis=-1, keepdims=True) + EPS)
    return hidden * scaling * gain, scaling


def norm_back(hidden, scaling, gain, grad):
    gain_grad = jnp.sum(grad * hidden * scaling, axis=0, keepdims=True)
    weighted = grad * gain
    inner = jnp.mean(weighted * hidden, axis=-1, keepdims=True)
    return weighted * scaling - hidden * (scaling * scaling * scaling * inner), gain_grad


def bias_tiles_kernel(line_ref, out_ref):
    for h in range(2):
        for delta in range(4):
            line = jnp.broadcast_to(line_ref[h * 4 + delta : h * 4 + delta + 1, :], (BLOCK, 2 * BLOCK))
            turned = pltpu.roll(line, 0, 1, stride=1, stride_axis=0)
            out_ref[h * 4 + delta] = turned[:, :BLOCK].astype(BF)


def bias_tiles(table):
    m = jnp.arange(2 * BLOCK, dtype=jnp.int32)
    ahead = jnp.where(m < BLOCK, m, m - 2 * BLOCK)
    distance = jnp.arange(4, dtype=jnp.int32)[:, None] * BLOCK - ahead[None, :]
    bucket = jnp.clip((distance + BLOCK) * RELB // (SEQ + BLOCK), 0, RELB - 1)
    onehot = (bucket[..., None] == jnp.arange(RELB, dtype=jnp.int32)).astype(F32)
    lines = jnp.einsum("dmb,bh->hdm", onehot, table, precision=HIGHEST).reshape(8, 2 * BLOCK)
    return call(bias_tiles_kernel, shape(8, BLOCK, BLOCK), "bias_tiles", 0, 1 << 20)(lines)


def head_mask(h, rows):
    lane = lax.broadcasted_iota(jnp.int32, (rows, LANES), 1)
    return (lane < HD) if h == 0 else (lane >= HD)


ATT_STEP = 256


def weight_blocks():
    return [(i, h) for i in range(4) for h in range(2)]


def weight_copy(i, h, vmem, hbm, sems, into):
    rows, keys = pl.ds(i * BLOCK, BLOCK), pl.ds(0, (i + 1) * BLOCK)
    ends = vmem.at[h, rows, keys], hbm.at[h, rows, keys]
    return pltpu.make_async_copy(*(ends if into else ends[::-1]), sems.at[h, i])


def attention_kernel(qkv_ref, bias_ref, ctx_ref, weights_hbm, held, sems):
    step = ATT_STEP
    for i in range(4):
        keys = (i + 1) * BLOCK
        key = qkv_ref[0:keys, LANES : 2 * LANES]
        value = qkv_ref[0:keys, 2 * LANES : 3 * LANES]
        for part in range(BLOCK // step):
            first = i * BLOCK + part * step
            query = qkv_ref[first : first + step, 0:LANES] * jnp.asarray(HD**-0.5, BF)
            zero = jnp.zeros_like(query)
            own = jnp.concatenate([jnp.where(head_mask(h, step), query, zero) for h in range(2)], axis=0)
            offset = jnp.concatenate(
                [
                    jnp.concatenate(
                        [bias_ref[h * 4 + i - b, part * step : (part + 1) * step, :] for b in range(i + 1)], axis=1
                    )
                    for h in range(2)
                ],
                axis=0,
            ).astype(F32)
            scores = mm_nt(own, key) + offset
            top = jnp.max(scores, axis=-1, keepdims=True)
            terms = jnp.exp(scores - top)
            total = jnp.sum(terms, axis=-1, keepdims=True)
            weights = (terms * (1.0 / total)).astype(BF)
            for h in range(2):
                held[h, first : first + step, 0:keys] = weights[h * step : (h + 1) * step]
            mixed = mm(weights, value)
            ctx_ref[first : first + step, :] = jnp.where(head_mask(0, step), mixed[:step], mixed[step:]).astype(BF)
        for h in range(2):
            weight_copy(i, h, held, weights_hbm, sems, True).start()
    for i, h in weight_blocks():
        weight_copy(i, h, held, weights_hbm, sems, True).wait()


def attention(qkv, tiles):
    return call(
        attention_kernel,
        (shape(SEQ, LANES), shape(2, SEQ, SEQ)),
        "attention",
        2 * 2 * 2 * SEQ * SEQ * LANES,
        8 << 20,
        in_specs=[VMEM] * 2,
        out_specs=(VMEM, ANYWHERE),
        scratch_shapes=[pltpu.VMEM((2, SEQ, SEQ), BF), pltpu.SemaphoreType.DMA((2, 4))],
    )(qkv, tiles)


def attention_back_kernel(qkv_ref, weights_hbm, dout_ref, flip_ref, dproj_ref, diag_ref, dkey, dvalue, tiles, held, sems):
    step = ATT_STEP
    for i, h in weight_blocks():
        weight_copy(i, h, held, weights_hbm, sems, False).start()
    dkey[...] = jnp.zeros_like(dkey)
    dvalue[...] = jnp.zeros_like(dvalue)
    for i in range(4):
        keys = (i + 1) * BLOCK
        key = qkv_ref[0:keys, LANES : 2 * LANES]
        value = qkv_ref[0:keys, 2 * LANES : 3 * LANES]
        for h in range(2):
            weight_copy(i, h, held, weights_hbm, sems, False).wait()
        for part in range(BLOCK // step):
            first = i * BLOCK + part * step
            rows = slice(part * step, (part + 1) * step)
            query = qkv_ref[first : first + step, 0:LANES]
            dout = dout_ref[first : first + step, :]
            query_t = query.astype(F32).T.astype(BF)
            dout_t = dout.astype(F32).T.astype(BF)
            zero = jnp.zeros_like(dout)
            own = jnp.concatenate([jnp.where(head_mask(h, step), dout, zero) for h in range(2)], axis=0)
            low = jnp.concatenate([held[h, first : first + step, 0:keys] for h in range(2)], axis=0)
            weights = low.astype(F32)
            dweights = mm_nt(own, value)
            delta = jnp.sum(weights * dweights, axis=-1, keepdims=True)
            dscores = weights * (dweights - delta)
            dlow = dscores.astype(BF)
            moved = mm(dlow, key)
            for h in range(2):
                mine = slice(h * step, (h + 1) * step)
                for b in range(i + 1):
                    tile = dscores[mine, b * BLOCK : (b + 1) * BLOCK]
                    n = h * 4 + i - b
                    tiles[n, rows, :] = tile if b == 0 else tiles[n, rows, :] + tile
                head = slice(h * HD, (h + 1) * HD)
                dkey[head, 0:keys] += mm(query_t[head], dlow[mine])
                dvalue[head, 0:keys] += mm(dout_t[head], low[mine])
            dquery = jnp.where(head_mask(0, step), moved[:step], moved[step:]) * HD**-0.5
            dproj_ref[first : first + step, 0:LANES] = dquery.astype(BF)
    dproj_ref[:, LANES : 2 * LANES] = (dkey[...] * HD**-0.5).T.astype(BF)
    dproj_ref[:, 2 * LANES : 3 * LANES] = dvalue[...].T.astype(BF)
    for n in range(8):
        tile = tiles[n]
        high = tile.astype(BF)
        rest = (tile - high.astype(F32)).astype(BF)
        flipped = mm(high, flip_ref[...]) + mm(rest, flip_ref[...])
        wide = jnp.concatenate([flipped, jnp.zeros_like(flipped)], axis=1)
        turned = pltpu.roll(wide, 0, 1, stride=1, stride_axis=0)
        diag_ref[n : n + 1, :] = jnp.sum(turned, axis=0, keepdims=True)


def attention_back(qkv, weights, dout):
    at = jnp.arange(BLOCK, dtype=jnp.int32)
    flip = (at[:, None] + at[None, :] == BLOCK - 1).astype(BF)
    return call(
        attention_back_kernel,
        (shape(SEQ, 3 * LANES), shape(8, 2 * BLOCK, dtype=F32)),
        "attention_back",
        2 * 4 * 2 * SEQ * SEQ * LANES,
        8 << 20,
        free=(2,),
        in_specs=[VMEM, ANYWHERE, VMEM, VMEM],
        out_specs=(VMEM, VMEM),
        scratch_shapes=[
            pltpu.VMEM((LANES, SEQ), F32),
            pltpu.VMEM((LANES, SEQ), F32),
            pltpu.VMEM((8, BLOCK, BLOCK), F32),
            pltpu.VMEM((2, SEQ, SEQ), BF),
            pltpu.SemaphoreType.DMA((2, 4)),
        ],
    )(qkv, weights, dout, flip)


def bias_grad(diag):
    m = jnp.arange(2 * BLOCK, dtype=jnp.int32)
    distance = jnp.arange(4, dtype=jnp.int32)[:, None] * BLOCK + m[None, :] - (BLOCK - 1)
    bucket = jnp.clip((distance + BLOCK) * RELB // (SEQ + BLOCK), 0, RELB - 1)
    onehot = (bucket[..., None] == jnp.arange(RELB, dtype=jnp.int32)).astype(F32)
    return jnp.einsum("hdm,dmb->bh", diag.reshape(2, 4, 2 * BLOCK), onehot, precision=HIGHEST)


def middle_kernel(
    layer, ctx_ref, wao_hbm, hidden_ref, gain_ref, slots_ref, table_ref, other_ref, middle_ref, out_ref, context_ref, wao_ref, sem
):
    load = pltpu.make_async_copy(wao_hbm.at[layer], wao_ref, sem)
    load.start()
    context = jnp.concatenate([ctx_ref[g] for g in range(PAIRS)], axis=1)
    context_ref[...] = context
    load.wait()
    middle = hidden_ref[...].astype(F32) + mm(context, wao_ref[...])
    middle_ref[...] = middle
    normed = norm_of(middle, gain_ref[layer])[0].astype(BF)
    first, second = slots_by_token(slots_ref[layer])
    rows = mm(first + second, normed).astype(BF)
    pack(rows, table_ref[...], out_ref, layer * EXPERTS)
    other = (1 - layer) * EXPERTS
    out_ref[other : other + EXPERTS] = other_ref[...]


def weight_space(columns):
    return [pltpu.VMEM((D, columns), BF), pltpu.SemaphoreType.DMA]


def middle_part(layer, ctx, wao, hidden, gain, slot_rows, table_t, other):
    return call(
        partial(middle_kernel, layer),
        (shape(TOK, D, dtype=F32), shape(2 * EXPERTS, CHUNK, LANES), shape(TOK, D)),
        "middle",
        2 * TOK * D * D + 2 * SLOTS * TOK * D * 5,
        4 << 20,
        free=(0,),
        in_specs=[VMEM, ANYWHERE, VMEM, VMEM, VMEM, VMEM, VMEM],
        scratch_shapes=weight_space(D),
    )(ctx, wao, hidden, gain, slot_rows, table_t, other)


def combined(layer, back_ref, middle_ref, slots_ref, gates_ref, table_ref, rows):
    unpack(back_ref.at[layer * EXPERTS : (layer + 1) * EXPERTS], table_ref[...], rows)
    picks = tokens_by_slot(slots_ref[layer])
    gates = gates_ref[layer]
    total = middle_ref[...]
    for k in range(2):
        total = total + gates[:, k : k + 1] * mm(picks[k], rows[...])
    return total.astype(BF)


def combine_kernel(layer, back_ref, middle_ref, slots_ref, gates_ref, table_ref, out_ref, rows):
    out_ref[...] = combined(layer, back_ref, middle_ref, slots_ref, gates_ref, table_ref, rows)


def combine(layer, back, middle, slot_cols, gates, table):
    return call(
        partial(combine_kernel, layer),
        shape(TOK, D),
        "combine",
        2 * TOK * SLOTS * D * 6,
        4 << 20,
        free=(0,),
        in_specs=[VMEM, VMEM, VMEM, VMEM, VMEM],
        scratch_shapes=[pltpu.VMEM((SLOTS, D), BF)],
    )(back, middle, slot_cols, gates, table)


def grad_chunks(dout, slot_rows, gates, table_t, out_ref, first):
    picks = slots_by_token(slot_rows)
    wide = dout.astype(F32)
    rows = mm(picks[0], (wide * gates[:, 0:1]).astype(BF)) + mm(picks[1], (wide * gates[:, 1:2]).astype(BF))
    pack(rows.astype(BF), table_t, out_ref, first)


def grad_rows_kernel(layer, dout_ref, slots_ref, gates_ref, table_ref, out_ref):
    grad_chunks(dout_ref[...], slots_ref[layer], gates_ref[layer], table_ref[...], out_ref, 0)


def grad_rows(layer, dout, slot_rows, gates, table_t):
    return call(
        partial(grad_rows_kernel, layer),
        shape(EXPERTS, CHUNK, LANES),
        "grad_rows",
        4 * TOK * SLOTS * D * 3,
        2 << 20,
    )(dout, slot_rows, gates, table_t)


def middle_back_kernel(
    layer, back_ref, slots_ref, table_ref, dout_ref, middle_ref, gain_ref, wao_hbm, dmid_ref, branch_ref, send_ref, dgain_ref,
    rows, wao_ref, sem,
):
    load = pltpu.make_async_copy(wao_hbm.at[layer], wao_ref, sem)
    load.start()
    unpack(back_ref.at[layer * EXPERTS : (layer + 1) * EXPERTS], table_ref[...], rows)
    first, second = tokens_by_slot(slots_ref[layer])
    dnormed = mm(first + second, rows[...])
    middle = middle_ref[...]
    gain = gain_ref[layer]
    scaling = lax.rsqrt(jnp.mean(middle * middle, axis=-1, keepdims=True) + EPS)
    moved, dgain = norm_back(middle, scaling, gain, dnormed)
    dgain_ref[...] = dgain
    dmid = dout_ref[...].astype(F32) + moved
    dmid_ref[...] = dmid
    branch = dmid.astype(BF)
    branch_ref[...] = branch
    load.wait()
    dcontext = mm_nt(branch, wao_ref[...]).astype(BF)
    for g in range(PAIRS):
        send_ref[g] = dcontext[:, g * LANES : (g + 1) * LANES]
    send_ref[PAIRS:8] = jnp.zeros((8 - PAIRS, TOK, LANES), BF)


def middle_back(layer, back, slot_cols, table, dout, middle, gain, wao):
    return call(
        partial(middle_back_kernel, layer),
        (shape(TOK, D, dtype=F32), shape(TOK, D), shape(8, TOK, LANES), shape(1, D, dtype=F32)),
        "middle_back",
        2 * TOK * D * D + 2 * TOK * SLOTS * D * 5,
        4 << 20,
        free=(0,),
        in_specs=[VMEM] * 6 + [ANYWHERE],
        scratch_shapes=[pltpu.VMEM((SLOTS, D), BF)] + weight_space(D),
    )(back, slot_cols, table, dout, middle, gain, wao)


def hidden_grad(layer, back_ref, wqkv_hbm, hidden_ref, gain_ref, dmid_ref, wqkv_ref, sem):
    load = pltpu.make_async_copy(wqkv_hbm.at[layer], wqkv_ref, sem)
    load.start()
    parts = [
        back_ref[g, :, part * LANES : (part + 1) * LANES] for part in range(3) for g in range(PAIRS)
    ]
    hidden = hidden_ref[...].astype(F32)
    scaling = lax.rsqrt(jnp.mean(hidden * hidden, axis=-1, keepdims=True) + EPS)
    load.wait()
    dnormed = mm_nt(jnp.concatenate(parts, axis=1), wqkv_ref[...])
    moved, _ = norm_back(hidden, scaling, gain_ref[layer], dnormed)
    return (dmid_ref[...] + moved).astype(BF)


def hidden_back_kernel(layer, back_ref, wqkv_hbm, hidden_ref, gain_ref, dmid_ref, dh_ref, wqkv_ref, sem):
    dh_ref[...] = hidden_grad(layer, back_ref, wqkv_hbm, hidden_ref, gain_ref, dmid_ref, wqkv_ref, sem)


def hidden_back_send_kernel(
    layer, back_ref, wqkv_hbm, hidden_ref, gain_ref, dmid_ref, slots_ref, gates_ref, table_ref, dh_ref, out_ref, wqkv_ref, sem
):
    dh = hidden_grad(layer, back_ref, wqkv_hbm, hidden_ref, gain_ref, dmid_ref, wqkv_ref, sem)
    dh_ref[...] = dh
    below = layer - 1
    grad_chunks(dh, slots_ref[below], gates_ref[below], table_ref[...], out_ref, below * EXPERTS)
    out_ref[layer * EXPERTS : (layer + 1) * EXPERTS] = jnp.zeros((EXPERTS, CHUNK, LANES), BF)


def hidden_back(layer, back, wqkv, hidden, gain, dmid):
    return call(
        partial(hidden_back_kernel, layer),
        shape(TOK, D),
        "hidden_back",
        2 * TOK * D * 3 * D,
        5 << 20,
        free=(0,),
        in_specs=[VMEM, ANYWHERE, VMEM, VMEM, VMEM],
        scratch_shapes=weight_space(3 * D),
    )(back, wqkv, hidden, gain, dmid)


def hidden_back_send(layer, back, wqkv, hidden, gain, dmid, slot_rows, gates, table_t):
    return call(
        partial(hidden_back_send_kernel, layer),
        (shape(TOK, D), shape(2 * EXPERTS, CHUNK, LANES)),
        "hidden_back_send",
        2 * TOK * D * 3 * D,
        6 << 20,
        free=(0,),
        in_specs=[VMEM, ANYWHERE] + [VMEM] * 6,
        scratch_shapes=weight_space(3 * D),
    )(back, wqkv, hidden, gain, dmid, slot_rows, gates, table_t)


FF_STEP = 1024
ROW_STEP = 320
CHUNKS = (2 * EXPERTS, CHUNK, LANES)


def gelu_parts(up):
    phi = 0.5 + 0.5 * lax.erf(up * 0.5**0.5)
    return up * phi, phi + up * (jnp.exp(up * up * -0.5) * 0.3989422804014327)


def row_blocks():
    return [slice(r, r + ROW_STEP) for r in range(0, ROWS, ROW_STEP)]


def over_hidden_units(one, weights, buffers, targets, sems):
    def copy(f, slot, k):
        columns = pl.ds(pl.multiple_of(f * FF_STEP, FF_STEP), FF_STEP)
        return pltpu.make_async_copy(buffers[k].at[slot], targets[k].at[:, columns], sems.at[slot, k])

    def step(f, carry):
        slot = lax.rem(f, 2)

        @pl.when(f >= 2)
        def _():
            for k in range(len(buffers)):
                copy(f - 2, slot, k).wait()

        for load in weights(f):
            load.wait()
        one(pl.ds(pl.multiple_of(f * FF_STEP, FF_STEP), FF_STEP), [b.at[slot] for b in buffers])
        for k in range(len(buffers)):
            copy(f, slot, k).start()
        return carry

    last = FF // FF_STEP
    lax.fori_loop(0, last, step, 0)
    for f in range(last - 2, last):
        for k in range(len(buffers)):
            copy(f, f % 2, k).wait()


def start_weights(win_hbm, wout_hbm, win_ref, wout_ref, sems, slope_hbm=None, slope=None):
    def copies(f):
        units = pl.ds(pl.multiple_of(f * FF_STEP, FF_STEP), FF_STEP)
        loads = [
            pltpu.make_async_copy(win_hbm.at[:, units], win_ref.at[:, units], sems.at[f, 0]),
            pltpu.make_async_copy(wout_hbm.at[units, :], wout_ref.at[units, :], sems.at[f, 1]),
        ]
        if slope is not None:
            loads.append(pltpu.make_async_copy(slope_hbm.at[:, units], slope.at[:, units], sems.at[f, 2]))
        return loads

    for f in range(FF // FF_STEP):
        for load in copies(f):
            load.start()
    return copies


def expert_space():
    return [
        pltpu.VMEM((D, FF), BF),
        pltpu.VMEM((FF, D), BF),
        pltpu.SemaphoreType.DMA((FF // FF_STEP, 3)),
    ]


def held_blocks():
    return pltpu.VMEM((2, ROWS, FF_STEP), BF)


def expert_forward_kernel(
    in_ref, win_hbm, wout_hbm, table_ref, table_t_ref, x_ref, act_hbm, slope_hbm, out_ref,
    win_ref, wout_ref, weight_sems, total, act_held, slope_held, sems,
):
    weights = start_weights(win_hbm, wout_hbm, win_ref, wout_ref, weight_sems)
    unpack(in_ref, table_ref[...], x_ref)
    total[...] = jnp.zeros_like(total)

    def one(columns, held):
        blocks = row_blocks()
        ups = mm(x_ref[blocks[0], :], win_ref[:, columns])
        for n, rows in enumerate(blocks):
            up = ups
            if n + 1 < len(blocks):
                ups = mm(x_ref[blocks[n + 1], :], win_ref[:, columns])
            act, slope = gelu_parts(up)
            act = act.astype(BF)
            held[0][rows, :] = act
            held[1][rows, :] = slope.astype(BF)
            total[rows, :] += mm(act, wout_ref[columns, :])

    over_hidden_units(one, weights, [act_held, slope_held], [act_hbm, slope_hbm], sems)
    pack(total[...].astype(BF), table_t_ref[...], out_ref, 0)


def expert_forward(arrived, first, second, table, table_t):
    return call(
        expert_forward_kernel,
        (shape(ROWS, D), shape(ROWS, FF), shape(ROWS, FF), shape(*CHUNKS)),
        "expert_forward",
        4 * ROWS * D * FF,
        20 << 20,
        vmem=40,
        free=(0,),
        in_specs=[VMEM, ANYWHERE, ANYWHERE, VMEM, VMEM],
        out_specs=(VMEM, ANYWHERE, ANYWHERE, VMEM),
        scratch_shapes=expert_space()
        + [pltpu.VMEM((ROWS, D), F32), held_blocks(), held_blocks(), pltpu.SemaphoreType.DMA((2, 2))],
    )(arrived, first, second, table, table_t)


def expert_back_kernel(
    section_ref, in_ref, win_hbm, wout_hbm, slope_hbm, table_ref, table_t_ref, other_ref, grad_ref, dup_hbm, out_ref,
    win_ref, wout_ref, weight_sems, total, slope, dup_held, sems,
):
    weights = start_weights(win_hbm, wout_hbm, win_ref, wout_ref, weight_sems, slope_hbm, slope)
    unpack(in_ref, table_ref[...], grad_ref)
    total[...] = jnp.zeros_like(total)

    def one(columns, held):
        blocks = row_blocks()
        dacts = mm_nt(grad_ref[blocks[0], :], wout_ref[columns, :])
        for n, rows in enumerate(blocks):
            dact = dacts
            if n + 1 < len(blocks):
                dacts = mm_nt(grad_ref[blocks[n + 1], :], wout_ref[columns, :])
            dup = (dact * slope[rows, columns].astype(F32)).astype(BF)
            held[0][rows, :] = dup
            total[rows, :] += mm_nt(dup, win_ref[:, columns])

    over_hidden_units(one, weights, [dup_held], [dup_hbm], sems)

    @pl.when(section_ref[0] == 0)
    def _():
        pack(total[...].astype(BF), table_t_ref[...], out_ref, 0)

    @pl.when(section_ref[0] == 1)
    def _():
        out_ref[...] = other_ref[...]


def expert_back(section, arrived, first, second, slope, table, table_t, other):
    return call(
        expert_back_kernel,
        (shape(ROWS, D), shape(ROWS, FF), shape(*CHUNKS)),
        "expert_back",
        4 * ROWS * D * FF,
        20 << 20,
        vmem=40,
        free=(1,),
        in_specs=[pl.BlockSpec(memory_space=pltpu.SMEM), VMEM, ANYWHERE, ANYWHERE, ANYWHERE, VMEM, VMEM, VMEM],
        out_specs=(VMEM, ANYWHERE, VMEM),
        scratch_shapes=expert_space()
        + [
            pltpu.VMEM((ROWS, D), F32),
            pltpu.VMEM((ROWS, FF), BF),
            held_blocks(),
            pltpu.SemaphoreType.DMA((2, 1)),
        ],
    )(section, arrived, first, second, slope, table, table_t, other)


def expert_both_kernel(
    in_ref, gin_ref, win_hbm, wout_hbm, table_ref, table_t_ref, x_ref, grad_ref, act_hbm, dup_hbm, out_ref, back_ref,
    win_ref, wout_ref, weight_sems, total, dtotal, act_held, dup_held, sems,
):
    weights = start_weights(win_hbm, wout_hbm, win_ref, wout_ref, weight_sems)
    unpack(in_ref, table_ref[...], x_ref)
    unpack(gin_ref, table_ref[...], grad_ref)
    total[...] = jnp.zeros_like(total)
    dtotal[...] = jnp.zeros_like(dtotal)

    def one(columns, held):
        blocks = row_blocks()

        def first_products(rows):
            return mm(x_ref[rows, :], win_ref[:, columns]), mm_nt(grad_ref[rows, :], wout_ref[columns, :])

        ahead = first_products(blocks[0])
        for n, rows in enumerate(blocks):
            up, dact = ahead
            if n + 1 < len(blocks):
                ahead = first_products(blocks[n + 1])
            act, slope = gelu_parts(up)
            dup = (dact * slope).astype(BF)
            act = act.astype(BF)
            held[0][rows, :] = act
            held[1][rows, :] = dup
            total[rows, :] += mm(act, wout_ref[columns, :])
            dtotal[rows, :] += mm_nt(dup, win_ref[:, columns])

    over_hidden_units(one, weights, [act_held, dup_held], [act_hbm, dup_hbm], sems)
    pack(dtotal[...].astype(BF), table_t_ref[...], back_ref, 0)
    pack(total[...].astype(BF), table_t_ref[...], out_ref, 0)


def expert_both(arrived, grads, first, second, table, table_t):
    return call(
        expert_both_kernel,
        (shape(ROWS, D), shape(ROWS, D), shape(ROWS, FF), shape(ROWS, FF), shape(*CHUNKS), shape(*CHUNKS)),
        "expert_both",
        8 * ROWS * D * FF,
        24 << 20,
        vmem=44,
        free=(0, 1),
        in_specs=[VMEM, VMEM, ANYWHERE, ANYWHERE, VMEM, VMEM],
        out_specs=(VMEM, VMEM, ANYWHERE, ANYWHERE, VMEM, VMEM),
        scratch_shapes=expert_space()
        + [
            pltpu.VMEM((ROWS, D), F32),
            pltpu.VMEM((ROWS, D), F32),
            held_blocks(),
            held_blocks(),
            pltpu.SemaphoreType.DMA((2, 2)),
        ],
    )(arrived, grads, first, second, table, table_t)


ROWS_OWN = 96
TAIL = 16


def parcel_kernel(w_ref, tail_ref, out_ref):
    for g in range(8):
        for part in range(3):
            lanes = slice(part * LANES, (part + 1) * LANES)
            if g < PAIRS:
                block = w_ref[:, part * D + g * LANES : part * D + (g + 1) * LANES]
            else:
                block = jnp.zeros((ROWS_OWN, LANES), BF)
            out_ref[g, 0:ROWS_OWN, lanes] = block
            out_ref[8 + g, 0:ROWS_OWN, lanes] = block
        out_ref[g, ROWS_OWN:, :] = tail_ref[...]
        out_ref[8 + g, ROWS_OWN:, :] = tail_ref[...]


def parcels_of(w_qkv, gain_attn, gain_ffn, rel_bias):
    row = jnp.concatenate([gain_attn.reshape(1, -1), gain_ffn.reshape(1, -1), rel_bias.reshape(1, -1)], axis=1)
    tail = jnp.pad(row, ((0, TAIL - 1), (0, 3 * LANES - row.shape[1])))
    return call(parcel_kernel, shape(16, ROWS_OWN + TAIL, 3 * LANES), "parcels", 0, 2 << 20)(w_qkv, tail)


def small_parts(parcels):
    rows = parcels[:, ROWS_OWN].astype(F32).reshape(2, 8, 3 * LANES)
    gain_a = rows[:, :, :ROWS_OWN].reshape(2, 1, D)
    gain_f = rows[:, :, ROWS_OWN : 2 * ROWS_OWN].reshape(2, 1, D)
    bias = rows[:, :, 2 * ROWS_OWN : 2 * ROWS_OWN + 4 * H].reshape(2, RELB, H)
    first = 2 * jnp.minimum(lax.axis_index("shard"), PAIRS - 1)
    return gain_a, gain_f, lax.dynamic_slice_in_dim(bias, first, 2, 2)


def project_kernel(layer, shard_ref, parcel_ref, gain_ref, *refs):
    blocks, normed_ref, qkv_ref = refs[:8], refs[8], refs[9]
    own = jnp.concatenate([parcel_ref[layer * 8 + j, 0:ROWS_OWN, :] for j in range(8)], axis=0)
    shard = shard_ref[0]
    for n in range(8):
        back, other = n % 4, n // 4
        source = lax.rem(shard + 8 - 2 * back, 8)
        if other:
            source = source + 1 - 2 * lax.rem(source, 2)
        rows = pl.ds(pl.multiple_of(source * TOK, TOK), TOK)
        normed = norm_of(blocks[n][...].astype(F32), gain_ref[layer])[0].astype(BF)
        normed_ref[rows, :] = normed
        qkv_ref[rows, :] = mm(normed, own).astype(BF)


def project(layer, shard, parcels, gain, blocks):
    return call(
        partial(project_kernel, layer),
        (shape(SEQ, D), shape(SEQ, 3 * LANES)),
        "project",
        2 * SEQ * D * 3 * LANES,
        5 << 20,
        in_specs=[pl.BlockSpec(memory_space=pltpu.SMEM)] + [VMEM] * 10,
    )(shard, parcels, gain, *blocks)


WIDE = 4 * LANES


PIECE = 16


def dense_grads_kernel(layer, shard_ref, normed_ref, dproj_ref, context_ref, branch_ref, tail_ref, *refs):
    out_hbm, held, sem = refs[-3:]
    dqkv = mm_tn(normed_ref[...], dproj_ref[...]).astype(BF)
    group = jnp.minimum(shard_ref[0], PAIRS - 1)
    columns = pl.ds(pl.multiple_of(group * LANES, LANES), LANES)
    dao = mm_tn(context_ref[...], branch_ref[:, columns]).astype(BF)
    for j in range(8):
        for r in range(ROWS_OWN // PIECE):
            rows = slice(j * ROWS_OWN + r * PIECE, j * ROWS_OWN + (r + 1) * PIECE)
            held[r * 8 + j, :, 0 : 3 * LANES] = dqkv[rows]
            held[r * 8 + j, :, 3 * LANES :] = dao[rows]
        held[48 + j] = tail_ref[j]
        held[56 + j] = jnp.zeros((PIECE, WIDE), BF)
    store = pltpu.make_async_copy(held, out_hbm.at[layer * 64 : (layer + 1) * 64], sem)
    store.start()
    store.wait()


def dense_grads(layer, shard, normed, dproj, context, branch, dgain_f, diag, filled=None):
    gains = jnp.pad(dgain_f.reshape(8, ROWS_OWN), ((0, 0), (0, LANES - ROWS_OWN)))
    biases = jnp.pad(bias_grad(diag).reshape(8, 8), ((0, 0), (0, 3 * LANES - 8)))
    tail = jnp.pad(jnp.concatenate([gains, biases], axis=1)[:, None].astype(BF), ((0, 0), (0, PIECE - 1), (0, 0)))
    more = () if filled is None else (filled,)
    return call(
        partial(dense_grads_kernel, layer),
        shape(128, PIECE, WIDE),
        "dense_grads",
        2 * SEQ * D * WIDE,
        6 << 20,
        in_specs=[pl.BlockSpec(memory_space=pltpu.SMEM)] + [VMEM] * 5 + [ANYWHERE] * len(more),
        out_specs=ANYWHERE,
        scratch_shapes=[pltpu.VMEM((64, PIECE, WIDE), BF), pltpu.SemaphoreType.DMA],
        input_output_aliases={6: 0} if more else {},
    )(shard, normed, dproj, context, branch, tail, *more)


def finish_kernel(rep_ref, w_ref, gain_ref, *refs):
    blocks, (qkv_ref, ao_ref, gain_a_ref, gain_f_ref, bias_ref) = refs[:8], refs[8:]
    rep = rep_ref[0]
    for n in range(8):
        other, back = n // 4, n % 4
        piece = lax.rem(rep + 4 - back, 4) + lax.rem(rep // 4 + other, 2) * 4
        block = blocks[n]

        @pl.when(piece < ROWS_OWN // PIECE)
        def _(block=block, piece=piece):
            rows = pl.ds(pl.multiple_of(piece * PIECE, PIECE), PIECE)
            for g in range(PAIRS):
                grads = block[g].astype(F32)
                for part in range(3):
                    first = part * D + g * LANES
                    qkv_ref[rows, first : first + LANES] = grads[:, part * LANES : (part + 1) * LANES]
                ao_ref[rows, g * LANES : (g + 1) * LANES] = grads[:, 3 * LANES :]

        @pl.when(piece == ROWS_OWN // PIECE)
        def _(block=block):
            firsts = [block[g].astype(F32)[0:1, :] for g in range(8)]
            gain_f_ref[...] = sum(f[:, 0:ROWS_OWN] for f in firsts)
            bias_ref[...] = jnp.concatenate([f[:, LANES : 2 * LANES] for f in firsts], axis=0)

    products = jnp.zeros((ROWS_OWN, LANES), F32)
    for first in range(0, 3 * D, LANES):
        columns = slice(first, first + LANES)
        products = products + qkv_ref[:, columns] * w_ref[:, columns].astype(F32)
    sums = lax.dot_general(
        jnp.ones((8, LANES), F32), products, (((1,), (1,)), ((), ())), precision=HIGHEST, preferred_element_type=F32
    )
    gain_a_ref[...] = sums[0:1, :] / gain_ref[...]


def finish(rep, w_qkv, gain, blocks):
    return call(
        finish_kernel,
        (
            shape(ROWS_OWN, 3 * D, dtype=F32),
            shape(ROWS_OWN, D, dtype=F32),
            shape(1, ROWS_OWN, dtype=F32),
            shape(1, ROWS_OWN, dtype=F32),
            shape(8, LANES, dtype=F32),
        ),
        "finish",
        0,
        2 << 20,
        in_specs=[pl.BlockSpec(memory_space=pltpu.SMEM)] + [VMEM] * 10,
    )(rep, w_qkv, gain, *blocks)


def spread(chunks):
    return lax.all_to_all(chunks, EVERYONE, split_axis=0, concat_axis=0, tiled=True)


def across(chunks):
    return lax.all_to_all(chunks, "shard", split_axis=0, concat_axis=0, tiled=True)


def swap(value):
    return lax.ppermute(value, "section", [(0, 1), (1, 0)])


def after(value, *others):
    return lax.optimization_barrier((value, *others))[0]


def tokens_of_all(own):
    n = 8

    def from_chip(back):
        return lax.ppermute(own, "shard", [(j, (j + 2 * back) % n) for j in range(n)])

    same_core = [own, from_chip(1), from_chip(2), from_chip(3)]
    return same_core + [lax.ppermute(block, "shard", [(j, j ^ 1) for j in range(n)]) for block in same_core]


def slot_tables(routes):
    flat = routes.reshape(2, 2 * TOK)
    onehot = (flat[..., None] == jnp.arange(EXPERTS, dtype=jnp.int32)).astype(BF)
    at = jnp.arange(2 * TOK, dtype=jnp.int32)
    earlier = (at[None, :] < at[:, None]).astype(BF)
    before = jnp.einsum("ab,lbe->lae", earlier, onehot, preferred_element_type=F32)
    rank = jnp.sum(before * onehot.astype(F32), axis=-1).astype(jnp.int32)
    return (flat * CAP + rank).reshape(routes.shape)


def per_device(
    inputs, cotangent, w_qkv, w_attn_out, gain_attn, gain_ffn, rel_bias, w_in, w_out, routes, gates
):
    section = lax.axis_index("section")
    shard = lax.axis_index("shard")
    first_proj, second_proj = w_in[0, 0], w_out[0, 0]
    hidden0 = lax.dynamic_index_in_dim(inputs[:, 0], section, 0, keepdims=False)
    cot = lax.dynamic_index_in_dim(cotangent[:, 0], section, 0, keepdims=False)
    table = pack_tables()
    table_t = table.T

    parcels = parcels_of(w_qkv[0], gain_attn, gain_ffn, rel_bias[0])
    got = lax.all_to_all(parcels, ("section", "shard"), split_axis=0, concat_axis=0, tiled=True)
    full0 = tokens_of_all(after(hidden0, parcels))
    w_start = after(w_attn_out[0], *full0[1:4])
    got, *full0 = lax.optimization_barrier((got, *full0))

    def both_layers(values):
        own = lax.dynamic_index_in_dim(values[0, :, 0], section, 0, keepdims=False)
        other = swap(lax.dynamic_index_in_dim(values[0, :, 0], 1 - section, 0, keepdims=False))
        return jnp.where(section == 0, jnp.stack([own, other]), jnp.stack([other, own]))

    slot_cols = slot_tables(both_layers(routes))
    slot_rows = slot_cols.transpose(0, 2, 1)
    gate_cols = both_layers(gates)

    cot_rows = grad_rows(1, cot, slot_rows, gate_cols, table_t)
    gain_a, gain_f, bias = small_parts(got)
    tiles = [bias_tiles(bias[l]) for l in range(2)]
    w_ao = lax.all_gather(w_start, ("section", "shard"), axis=0, tiled=True).reshape(2, D, D)

    own_index = shard.reshape(1)
    normed0, qkv0 = project(0, own_index, got, gain_a, full0)
    ctx0, weights0 = attention(qkv0, tiles[0])
    ctx0_tok = across(ctx0.reshape(8, TOK, LANES))
    ctx0_tok, cot_rows, slot_cols, slot_rows, gate_cols, table, table_t = lax.optimization_barrier(
        (ctx0_tok, cot_rows, slot_cols, slot_rows, gate_cols, table, table_t)
    )
    middle0, send, ctx0_own = middle_part(0, ctx0_tok, w_ao, hidden0, gain_f, slot_rows, table_t, cot_rows)
    arrived0 = spread(send)
    x0, act0, slope0, made = expert_forward(arrived0, first_proj, second_proj, table, table_t)
    back, tiles[1] = lax.optimization_barrier((spread(made), tiles[1]))
    ctx0_full = lax.all_gather(ctx0_own, "shard", axis=0, tiled=True)
    out0 = combine(0, back, middle0, slot_cols, gate_cols, table)

    normed1, qkv1 = project(1, own_index, got, gain_a, tokens_of_all(out0))
    ctx1, weights1 = attention(qkv1, tiles[1])
    ctx1_tok = across(ctx1.reshape(8, TOK, LANES))
    middle1, send, ctx1_own = middle_part(
        1, ctx1_tok, w_ao, out0, gain_f, slot_rows, table_t, cot_rows
    )
    ctx1_full = lax.all_gather(ctx1_own, "shard", axis=0, tiled=True)
    arrived1 = spread(send)
    w_full = lax.all_gather(after(w_qkv[0], arrived1), ("section", "shard"), axis=0, tiled=True).reshape(2, D, 3 * D)
    x1, g1, act1, dup1, made1, dmade1 = expert_both(arrived1, arrived0, first_proj, second_proj, table, table_t)

    back = spread(dmade1)
    dmid1, branch1, send, dgain_f1 = middle_back(1, back, slot_cols, table, cot, middle1, gain_f, w_ao)
    branch1_full = lax.all_gather(branch1, "shard", axis=0, tiled=True)
    dproj1, diag1 = attention_back(qkv1, weights1, across(send).reshape(SEQ, LANES))
    dproj1_tok = across(dproj1.reshape(8, TOK, 3 * LANES))
    dh1, send = hidden_back_send(1, dproj1_tok, w_full, out0, gain_a, dmid1, slot_rows, gate_cols, table_t)

    g0, dup0, dmade0 = expert_back(
        section.reshape(1), spread(send), first_proj, second_proj, slope0, table, table_t, made1
    )
    back = spread(dmade0)
    out1 = combine(1, back, middle1, slot_cols, gate_cols, table)
    dmid0, branch0, send, dgain_f0 = middle_back(0, back, slot_cols, table, dh1, middle0, gain_f, w_ao)
    branch0_full = lax.all_gather(branch0, "shard", axis=0, tiled=True)
    dproj0, diag0 = attention_back(qkv0, weights0, across(send).reshape(SEQ, LANES))

    dproj0_tok = across(dproj0.reshape(8, TOK, 3 * LANES))
    parcels = dense_grads(1, own_index, normed1, dproj1, ctx1_full, branch1_full, dgain_f1, diag1)
    parcels = dense_grads(0, own_index, normed0, dproj0, ctx0_full, branch0_full, dgain_f0, diag0, parcels)
    parcels = after(parcels, dproj0_tok)
    got = spread(parcels)

    def own(a, b):
        return jnp.where(section == 0, a, b)

    grad_in = mm_tn(own(x0, x1), own(dup0, dup1))
    grad_out = mm_tn(own(act0, act1), own(g0, g1))
    dh0 = hidden_back(0, dproj0_tok, w_full, hidden0, gain_a, dmid0)
    got, grad_in, grad_out, dh0 = lax.optimization_barrier((got, grad_in, grad_out, dh0))
    summed = jnp.sum(got.reshape(16, 8, PIECE, WIDE).astype(F32), axis=0).astype(BF)

    blocks = [summed] + [
        lax.ppermute(summed, "rep", [(r, r // 4 * 4 + (r + k) % 4) for r in range(8)]) for k in range(1, 4)
    ]
    blocks = blocks + [lax.ppermute(b, "rep", [(r, (r + 4) % 8) for r in range(8)]) for b in blocks]
    grad_qkv, grad_ao, dgain_a, dgain_f, drel = finish(
        lax.axis_index("rep").reshape(1), w_qkv[0], gain_attn.astype(F32), blocks
    )
    grad_bias = drel[:PAIRS, :8].reshape(PAIRS, 4, 2).transpose(1, 0, 2).reshape(1, 4, H)

    def by_layer(layer0, layer1):
        keep = jnp.where(section == 0, layer0, layer1)
        other = swap(jnp.where(section == 0, layer1, layer0))
        pair = jnp.where(section == 0, jnp.stack([keep, other]), jnp.stack([other, keep]))
        return pair.reshape(1, 2, 1, TOK, D)

    return (
        by_layer(out0, out1),
        by_layer(dh0, dh1),
        grad_qkv[None],
        grad_ao[None],
        dgain_a,
        dgain_f,
        grad_bias,
        grad_in[None, None],
        grad_out[None, None],
    )


def solution(mesh):
    placed = (
        P(None, "rep", "shard", None),
        P(None, "rep", "shard", None),
        P("section", "shard", None),
        P("section", "shard", None),
        P("section", "shard"),
        P("section", "shard"),
        P("section", "shard", None),
        P("section", ("rep", "shard"), None, None),
        P("section", ("rep", "shard"), None, None),
        P("section", None, "rep", "shard", None),
        P("section", None, "rep", "shard", None),
    )
    return jax.shard_map(
        per_device,
        mesh=mesh,
        in_specs=placed,
        out_specs=(
            P("section", None, "rep", "shard", None),
            P("section", None, "rep", "shard", None),
            P("section", "shard", None),
            P("section", "shard", None),
            P("section", "shard"),
            P("section", "shard"),
            P("section", "shard", None),
            P("section", ("rep", "shard"), None, None),
            P("section", ("rep", "shard"), None, None),
        ),
        check_vma=False,
    )
```

```python
from functools import partial

import jax
import jax.numpy as jnp
from jax import lax
from jax.experimental import pallas as pl
from jax.experimental.pallas import tpu as pltpu
from jax.sharding import PartitionSpec as P

F32 = jnp.float32
BF = jnp.bfloat16
D = 768
H = 12
HD = 64
FF = 3072
SEQ = 1024
TOK = 128
BLOCK = 256
RELB = 32
EXPERTS = 64
CAP = 5
LANES = 128
COLS = D // LANES
CHUNK = 32
GROUP = 16
SLOTS = EXPERTS * CAP
GROUPS_ALL = 2 * EXPERTS // GROUP
ROWS = 2 * EXPERTS * CAP
PAIRS = H // 2
EPS = 1e-05
ROWS_OWN = 96
EXTRA = 16
EVERYONE = ("section", "rep", "shard")
HIGHEST = lax.Precision.HIGHEST
MIB = 1 << 20


def mm(a, b):
    return lax.dot_general(a, b, (((1,), (0,)), ((), ())), preferred_element_type=F32)


def mm_nt(a, b):
    return lax.dot_general(a, b, (((1,), (1,)), ((), ())), preferred_element_type=F32)


def mm_tn(a, b):
    return lax.dot_general(a, b, (((0,), (0,)), ((), ())), preferred_element_type=F32)


def call(kernel, outs, name, flops, moved, vmem=32, free=(), **more):
    run = pl.pallas_call(
        kernel,
        out_shape=outs,
        name=name,
        compiler_params=pltpu.CompilerParams(vmem_limit_bytes=vmem * MIB),
        cost_estimate=pl.CostEstimate(flops=flops, bytes_accessed=moved, transcendentals=0),
        **more,
    )

    def placed(*operands):
        return run(
            *(
                x if x.ndim == 1 or n in free else pltpu.with_memory_space_constraint(x, pltpu.HBM)
                for n, x in enumerate(operands)
            )
        )

    return placed


def shape(*dims, dtype=BF):
    return pltpu.HBM(dims, dtype)


VMEM = pl.BlockSpec(memory_space=pltpu.VMEM)
ANYWHERE = pl.BlockSpec(memory_space=pl.ANY)
SMEM = pl.BlockSpec(memory_space=pltpu.SMEM)


def pack_tables():
    row = jnp.arange(GROUP * CAP * COLS, dtype=jnp.int32)[:, None]
    col = jnp.arange(GROUP * CHUNK, dtype=jnp.int32)[None, :]
    block, inside = row // (GROUP * CAP), row % (GROUP * CAP)
    place = (inside // CAP) * CHUNK + block * CAP + inside % CAP
    return (place == col).astype(BF)


def unpack(chunks, table, target):
    size = GROUP * CAP
    for g in range(0, chunks.shape[0] // GROUP, 2):
        raw = [chunks[k * GROUP : (k + 1) * GROUP].reshape(GROUP * CHUNK, LANES) for k in (g, g + 1)]
        rows = mm(table, jnp.concatenate(raw, axis=1)).astype(BF)
        for k in range(2):
            for c in range(COLS):
                target[(g + k) * size : (g + k + 1) * size, c * LANES : (c + 1) * LANES] = rows[
                    c * size : (c + 1) * size, k * LANES : (k + 1) * LANES
                ]


def pack(rows, table_t, target, first):
    size = GROUP * CAP
    for g in range(0, rows.shape[0] // size, 2):
        stacked = jnp.concatenate(
            [
                jnp.concatenate(
                    [rows[k * size : (k + 1) * size, c * LANES : (c + 1) * LANES] for k in (g, g + 1)], axis=1
                )
                for c in range(COLS)
            ],
            axis=0,
        )
        both = mm(table_t, stacked).astype(BF)
        for k in range(2):
            chunk = both[:, k * LANES : (k + 1) * LANES].reshape(GROUP, CHUNK, LANES)
            target[first + (g + k) * GROUP : first + (g + k + 1) * GROUP] = chunk


def slots_by_token(slot_rows):
    places = lax.broadcasted_iota(jnp.int32, (SLOTS, TOK), 0)
    return [jnp.where(places == slot_rows[k : k + 1, :], 1.0, 0.0).astype(BF) for k in range(2)]


def tokens_by_slot(slot_cols):
    places = lax.broadcasted_iota(jnp.int32, (TOK, SLOTS), 1)
    return [jnp.where(places == slot_cols[:, k : k + 1], 1.0, 0.0).astype(BF) for k in range(2)]


def norm_of(hidden, gain):
    scaling = lax.rsqrt(jnp.mean(hidden * hidden, axis=-1, keepdims=True) + EPS)
    return hidden * scaling * gain, scaling


def norm_back(hidden, scaling, gain, grad):
    gain_grad = jnp.sum(grad * hidden * scaling, axis=0, keepdims=True)
    weighted = grad * gain
    inner = jnp.mean(weighted * hidden, axis=-1, keepdims=True)
    return weighted * scaling - hidden * (scaling * scaling * scaling * inner), gain_grad


def bias_tiles_kernel(line_ref, out_ref):
    for h in range(2):
        for delta in range(4):
            line = jnp.broadcast_to(line_ref[h * 4 + delta : h * 4 + delta + 1, :], (BLOCK, 2 * BLOCK))
            turned = pltpu.roll(line, 0, 1, stride=1, stride_axis=0)
            out_ref[h * 4 + delta] = turned[:, :BLOCK].astype(BF)


def bias_tiles(table):
    m = jnp.arange(2 * BLOCK, dtype=jnp.int32)
    ahead = jnp.where(m < BLOCK, m, m - 2 * BLOCK)
    distance = jnp.arange(4, dtype=jnp.int32)[:, None] * BLOCK - ahead[None, :]
    bucket = jnp.clip((distance + BLOCK) * RELB // (SEQ + BLOCK), 0, RELB - 1)
    onehot = (bucket[..., None] == jnp.arange(RELB, dtype=jnp.int32)).astype(F32)
    lines = jnp.einsum("dmb,bh->hdm", onehot, table, precision=HIGHEST).reshape(8, 2 * BLOCK)
    return call(bias_tiles_kernel, shape(8, BLOCK, BLOCK), "bias_tiles", 0, 1 << 20)(lines)


def head_mask(h, rows):
    lane = lax.broadcasted_iota(jnp.int32, (rows, LANES), 1)
    return (lane < HD) if h == 0 else (lane >= HD)


ATT_STEP = 256


def weight_blocks():
    return [(i, h) for i in range(4) for h in range(2)]


def weight_copy(i, h, vmem, hbm, sems, into):
    rows, keys = pl.ds(i * BLOCK, BLOCK), pl.ds(0, (i + 1) * BLOCK)
    ends = vmem.at[h, rows, keys], hbm.at[h, rows, keys]
    return pltpu.make_async_copy(*(ends if into else ends[::-1]), sems.at[h, i])


def attention_kernel(qkv_ref, bias_ref, ctx_ref, weights_hbm, held, sems):
    step = ATT_STEP
    for i in range(4):
        keys = (i + 1) * BLOCK
        key = qkv_ref[0:keys, LANES : 2 * LANES]
        value = qkv_ref[0:keys, 2 * LANES : 3 * LANES]
        for part in range(BLOCK // step):
            first = i * BLOCK + part * step
            query = qkv_ref[first : first + step, 0:LANES] * jnp.asarray(HD**-0.5, BF)
            zero = jnp.zeros_like(query)
            own = jnp.concatenate([jnp.where(head_mask(h, step), query, zero) for h in range(2)], axis=0)
            offset = jnp.concatenate(
                [
                    jnp.concatenate(
                        [bias_ref[h * 4 + i - b, part * step : (part + 1) * step, :] for b in range(i + 1)], axis=1
                    )
                    for h in range(2)
                ],
                axis=0,
            ).astype(F32)
            scores = mm_nt(own, key) + offset
            top = jnp.max(scores, axis=-1, keepdims=True)
            terms = jnp.exp(scores - top)
            total = jnp.sum(terms, axis=-1, keepdims=True)
            weights = (terms * (1.0 / total)).astype(BF)
            for h in range(2):
                held[h, first : first + step, 0:keys] = weights[h * step : (h + 1) * step]
            mixed = mm(weights, value)
            ctx_ref[first : first + step, :] = jnp.where(head_mask(0, step), mixed[:step], mixed[step:]).astype(BF)
        for h in range(2):
            weight_copy(i, h, held, weights_hbm, sems, True).start()
    for i, h in weight_blocks():
        weight_copy(i, h, held, weights_hbm, sems, True).wait()


def attention(qkv, tiles):
    return call(
        attention_kernel,
        (shape(SEQ, LANES), shape(2, SEQ, SEQ)),
        "attention",
        2 * 2 * 2 * SEQ * SEQ * LANES,
        8 << 20,
        in_specs=[VMEM] * 2,
        out_specs=(VMEM, ANYWHERE),
        scratch_shapes=[pltpu.VMEM((2, SEQ, SEQ), BF), pltpu.SemaphoreType.DMA((2, 4))],
    )(qkv, tiles)


def attention_back_kernel(qkv_ref, weights_hbm, dout_ref, flip_ref, dproj_ref, diag_ref, dkey, dvalue, tiles, held, sems):
    step = ATT_STEP
    for i, h in weight_blocks():
        weight_copy(i, h, held, weights_hbm, sems, False).start()
    dkey[...] = jnp.zeros_like(dkey)
    dvalue[...] = jnp.zeros_like(dvalue)
    for i in range(4):
        keys = (i + 1) * BLOCK
        key = qkv_ref[0:keys, LANES : 2 * LANES]
        value = qkv_ref[0:keys, 2 * LANES : 3 * LANES]
        for h in range(2):
            weight_copy(i, h, held, weights_hbm, sems, False).wait()
        for part in range(BLOCK // step):
            first = i * BLOCK + part * step
            rows = slice(part * step, (part + 1) * step)
            query = qkv_ref[first : first + step, 0:LANES]
            dout = dout_ref[first : first + step, :]
            query_t = query.astype(F32).T.astype(BF)
            dout_t = dout.astype(F32).T.astype(BF)
            zero = jnp.zeros_like(dout)
            own = jnp.concatenate([jnp.where(head_mask(h, step), dout, zero) for h in range(2)], axis=0)
            low = jnp.concatenate([held[h, first : first + step, 0:keys] for h in range(2)], axis=0)
            weights = low.astype(F32)
            dweights = mm_nt(own, value)
            delta = jnp.sum(weights * dweights, axis=-1, keepdims=True)
            dscores = weights * (dweights - delta)
            dlow = dscores.astype(BF)
            moved = mm(dlow, key)
            for h in range(2):
                mine = slice(h * step, (h + 1) * step)
                for b in range(i + 1):
                    tile = dscores[mine, b * BLOCK : (b + 1) * BLOCK]
                    n = h * 4 + i - b
                    tiles[n, rows, :] = tile if b == 0 else tiles[n, rows, :] + tile
                head = slice(h * HD, (h + 1) * HD)
                dkey[head, 0:keys] += mm(query_t[head], dlow[mine])
                dvalue[head, 0:keys] += mm(dout_t[head], low[mine])
            dquery = jnp.where(head_mask(0, step), moved[:step], moved[step:]) * HD**-0.5
            dproj_ref[first : first + step, 0:LANES] = dquery.astype(BF)
    dproj_ref[:, LANES : 2 * LANES] = (dkey[...] * HD**-0.5).T.astype(BF)
    dproj_ref[:, 2 * LANES : 3 * LANES] = dvalue[...].T.astype(BF)
    for n in range(8):
        tile = tiles[n]
        high = tile.astype(BF)
        rest = (tile - high.astype(F32)).astype(BF)
        flipped = mm(high, flip_ref[...]) + mm(rest, flip_ref[...])
        wide = jnp.concatenate([flipped, jnp.zeros_like(flipped)], axis=1)
        turned = pltpu.roll(wide, 0, 1, stride=1, stride_axis=0)
        diag_ref[n : n + 1, :] = jnp.sum(turned, axis=0, keepdims=True)


def attention_back(qkv, weights, dout):
    at = jnp.arange(BLOCK, dtype=jnp.int32)
    flip = (at[:, None] + at[None, :] == BLOCK - 1).astype(BF)
    return call(
        attention_back_kernel,
        (shape(SEQ, 3 * LANES), shape(8, 2 * BLOCK, dtype=F32)),
        "attention_back",
        2 * 4 * 2 * SEQ * SEQ * LANES,
        8 << 20,
        free=(2,),
        in_specs=[VMEM, ANYWHERE, VMEM, VMEM],
        out_specs=(VMEM, VMEM),
        scratch_shapes=[
            pltpu.VMEM((LANES, SEQ), F32),
            pltpu.VMEM((LANES, SEQ), F32),
            pltpu.VMEM((8, BLOCK, BLOCK), F32),
            pltpu.VMEM((2, SEQ, SEQ), BF),
            pltpu.SemaphoreType.DMA((2, 4)),
        ],
    )(qkv, weights, dout, flip)


def bias_grad(diag):
    m = jnp.arange(2 * BLOCK, dtype=jnp.int32)
    distance = jnp.arange(4, dtype=jnp.int32)[:, None] * BLOCK + m[None, :] - (BLOCK - 1)
    bucket = jnp.clip((distance + BLOCK) * RELB // (SEQ + BLOCK), 0, RELB - 1)
    onehot = (bucket[..., None] == jnp.arange(RELB, dtype=jnp.int32)).astype(F32)
    return jnp.einsum("hdm,dmb->bh", diag.reshape(2, 4, 2 * BLOCK), onehot, precision=HIGHEST)


def middle_kernel(
    layer, ctx_ref, wao_hbm, hidden_ref, gain_ref, slots_ref, table_ref, other_ref, middle_ref, out_ref, context_ref, wao_ref, sem
):
    load = pltpu.make_async_copy(wao_hbm, wao_ref, sem)
    load.start()
    context = jnp.concatenate([ctx_ref[g] for g in range(PAIRS)], axis=1)
    context_ref[...] = context
    load.wait()
    middle = hidden_ref[...].astype(F32) + mm(context, wao_ref[...])
    middle_ref[...] = middle
    normed = norm_of(middle, gain_ref[layer])[0].astype(BF)
    first, second = slots_by_token(slots_ref[layer])
    rows = mm(first + second, normed).astype(BF)
    pack(rows, table_ref[...], out_ref, layer * EXPERTS)
    other = (1 - layer) * EXPERTS
    out_ref[other : other + EXPERTS] = other_ref[...]


def weight_space(columns):
    return [pltpu.VMEM((D, columns), BF), pltpu.SemaphoreType.DMA]


def middle_part(layer, ctx, wao, hidden, gain, slot_rows, table_t, other):
    return call(
        partial(middle_kernel, layer),
        (shape(TOK, D, dtype=F32), shape(2 * EXPERTS, CHUNK, LANES), shape(TOK, D)),
        "middle",
        2 * TOK * D * D + 2 * SLOTS * TOK * D * 5,
        4 << 20,
        free=(0,),
        in_specs=[VMEM, ANYWHERE, VMEM, VMEM, VMEM, VMEM, VMEM],
        scratch_shapes=weight_space(D),
    )(ctx, wao, hidden, gain, slot_rows, table_t, other)


def combined(layer, back_ref, middle_ref, slots_ref, gates_ref, table_ref, rows):
    unpack(back_ref.at[layer * EXPERTS : (layer + 1) * EXPERTS], table_ref[...], rows)
    picks = tokens_by_slot(slots_ref[layer])
    gates = gates_ref[layer]
    total = middle_ref[...]
    for k in range(2):
        total = total + gates[:, k : k + 1] * mm(picks[k], rows[...])
    return total.astype(BF)


def combine_kernel(layer, back_ref, middle_ref, slots_ref, gates_ref, table_ref, out_ref, rows):
    out_ref[...] = combined(layer, back_ref, middle_ref, slots_ref, gates_ref, table_ref, rows)


def combine(layer, back, middle, slot_cols, gates, table):
    return call(
        partial(combine_kernel, layer),
        shape(TOK, D),
        "combine",
        2 * TOK * SLOTS * D * 6,
        4 << 20,
        free=(0,),
        in_specs=[VMEM, VMEM, VMEM, VMEM, VMEM],
        scratch_shapes=[pltpu.VMEM((SLOTS, D), BF)],
    )(back, middle, slot_cols, gates, table)


def grad_chunks(dout, slot_rows, gates, table_t, out_ref, first):
    picks = slots_by_token(slot_rows)
    wide = dout.astype(F32)
    rows = mm(picks[0], (wide * gates[:, 0:1]).astype(BF)) + mm(picks[1], (wide * gates[:, 1:2]).astype(BF))
    pack(rows.astype(BF), table_t, out_ref, first)


def grad_rows_kernel(layer, dout_ref, slots_ref, gates_ref, table_ref, out_ref):
    grad_chunks(dout_ref[...], slots_ref[layer], gates_ref[layer], table_ref[...], out_ref, 0)


def grad_rows(layer, dout, slot_rows, gates, table_t):
    return call(
        partial(grad_rows_kernel, layer),
        shape(EXPERTS, CHUNK, LANES),
        "grad_rows",
        4 * TOK * SLOTS * D * 3,
        2 << 20,
    )(dout, slot_rows, gates, table_t)


def middle_back_kernel(
    layer, back_ref, slots_ref, table_ref, dout_ref, middle_ref, gain_ref, wao_hbm, dmid_ref, branch_ref, send_ref, dgain_ref,
    rows, wao_ref, sem,
):
    load = pltpu.make_async_copy(wao_hbm, wao_ref, sem)
    load.start()
    unpack(back_ref.at[layer * EXPERTS : (layer + 1) * EXPERTS], table_ref[...], rows)
    first, second = tokens_by_slot(slots_ref[layer])
    dnormed = mm(first + second, rows[...])
    middle = middle_ref[...]
    gain = gain_ref[layer]
    scaling = lax.rsqrt(jnp.mean(middle * middle, axis=-1, keepdims=True) + EPS)
    moved, dgain = norm_back(middle, scaling, gain, dnormed)
    dgain_ref[...] = dgain
    dmid = dout_ref[...].astype(F32) + moved
    dmid_ref[...] = dmid
    branch = dmid.astype(BF)
    branch_ref[...] = branch
    load.wait()
    dcontext = mm_nt(branch, wao_ref[...]).astype(BF)
    for g in range(PAIRS):
        send_ref[g] = dcontext[:, g * LANES : (g + 1) * LANES]
    send_ref[PAIRS:8] = jnp.zeros((8 - PAIRS, TOK, LANES), BF)


def middle_back(layer, back, slot_cols, table, dout, middle, gain, wao):
    return call(
        partial(middle_back_kernel, layer),
        (shape(TOK, D, dtype=F32), shape(TOK, D), shape(8, TOK, LANES), shape(1, D, dtype=F32)),
        "middle_back",
        2 * TOK * D * D + 2 * TOK * SLOTS * D * 5,
        4 << 20,
        free=(0,),
        in_specs=[VMEM] * 6 + [ANYWHERE],
        scratch_shapes=[pltpu.VMEM((SLOTS, D), BF)] + weight_space(D),
    )(back, slot_cols, table, dout, middle, gain, wao)


def hidden_grad(layer, back_ref, wqkv_hbm, hidden_ref, gain_ref, dmid_ref, wqkv_ref, sem):
    load = pltpu.make_async_copy(wqkv_hbm, wqkv_ref, sem)
    load.start()
    parts = [
        back_ref[g, :, part * LANES : (part + 1) * LANES] for part in range(3) for g in range(PAIRS)
    ]
    hidden = hidden_ref[...].astype(F32)
    scaling = lax.rsqrt(jnp.mean(hidden * hidden, axis=-1, keepdims=True) + EPS)
    load.wait()
    dnormed = mm_nt(jnp.concatenate(parts, axis=1), wqkv_ref[...])
    moved, _ = norm_back(hidden, scaling, gain_ref[layer], dnormed)
    return (dmid_ref[...] + moved).astype(BF)


def hidden_back_kernel(layer, back_ref, wqkv_hbm, hidden_ref, gain_ref, dmid_ref, dh_ref, wqkv_ref, sem):
    dh_ref[...] = hidden_grad(layer, back_ref, wqkv_hbm, hidden_ref, gain_ref, dmid_ref, wqkv_ref, sem)


def hidden_back_send_kernel(
    layer, back_ref, wqkv_hbm, hidden_ref, gain_ref, dmid_ref, slots_ref, gates_ref, table_ref, dh_ref, out_ref, wqkv_ref, sem
):
    dh = hidden_grad(layer, back_ref, wqkv_hbm, hidden_ref, gain_ref, dmid_ref, wqkv_ref, sem)
    dh_ref[...] = dh
    below = layer - 1
    grad_chunks(dh, slots_ref[below], gates_ref[below], table_ref[...], out_ref, below * EXPERTS)
    out_ref[layer * EXPERTS : (layer + 1) * EXPERTS] = jnp.zeros((EXPERTS, CHUNK, LANES), BF)


def hidden_back(layer, back, wqkv, hidden, gain, dmid):
    return call(
        partial(hidden_back_kernel, layer),
        shape(TOK, D),
        "hidden_back",
        2 * TOK * D * 3 * D,
        5 << 20,
        free=(0,),
        in_specs=[VMEM, ANYWHERE, VMEM, VMEM, VMEM],
        scratch_shapes=weight_space(3 * D),
    )(back, wqkv, hidden, gain, dmid)


def hidden_back_send(layer, back, wqkv, hidden, gain, dmid, slot_rows, gates, table_t):
    return call(
        partial(hidden_back_send_kernel, layer),
        (shape(TOK, D), shape(2 * EXPERTS, CHUNK, LANES)),
        "hidden_back_send",
        2 * TOK * D * 3 * D,
        6 << 20,
        free=(0,),
        in_specs=[VMEM, ANYWHERE] + [VMEM] * 6,
        scratch_shapes=weight_space(3 * D),
    )(back, wqkv, hidden, gain, dmid, slot_rows, gates, table_t)


FF_STEP = 1024
ROW_STEP = 320
CHUNKS = (2 * EXPERTS, CHUNK, LANES)


def gelu_parts(up):
    phi = 0.5 + 0.5 * lax.erf(up * 0.5**0.5)
    return up * phi, phi + up * (jnp.exp(up * up * -0.5) * 0.3989422804014327)


def row_blocks():
    return [slice(r, r + ROW_STEP) for r in range(0, ROWS, ROW_STEP)]


def over_hidden_units(one, weights, buffers, targets, sems):
    def copy(f, slot, k):
        columns = pl.ds(pl.multiple_of(f * FF_STEP, FF_STEP), FF_STEP)
        return pltpu.make_async_copy(buffers[k].at[slot], targets[k].at[:, columns], sems.at[slot, k])

    def step(f, carry):
        slot = lax.rem(f, 2)

        @pl.when(f >= 2)
        def _():
            for k in range(len(buffers)):
                copy(f - 2, slot, k).wait()

        for load in weights(f):
            load.wait()
        one(pl.ds(pl.multiple_of(f * FF_STEP, FF_STEP), FF_STEP), [b.at[slot] for b in buffers])
        for k in range(len(buffers)):
            copy(f, slot, k).start()
        return carry

    last = FF // FF_STEP
    lax.fori_loop(0, last, step, 0)
    for f in range(last - 2, last):
        for k in range(len(buffers)):
            copy(f, f % 2, k).wait()


def start_weights(win_hbm, wout_hbm, win_ref, wout_ref, sems, slope_hbm=None, slope=None):
    def copies(f):
        units = pl.ds(pl.multiple_of(f * FF_STEP, FF_STEP), FF_STEP)
        loads = [
            pltpu.make_async_copy(win_hbm.at[:, units], win_ref.at[:, units], sems.at[f, 0]),
            pltpu.make_async_copy(wout_hbm.at[units, :], wout_ref.at[units, :], sems.at[f, 1]),
        ]
        if slope is not None:
            loads.append(pltpu.make_async_copy(slope_hbm.at[:, units], slope.at[:, units], sems.at[f, 2]))
        return loads

    for f in range(FF // FF_STEP):
        for load in copies(f):
            load.start()
    return copies


def expert_space():
    return [
        pltpu.VMEM((D, FF), BF),
        pltpu.VMEM((FF, D), BF),
        pltpu.SemaphoreType.DMA((FF // FF_STEP, 3)),
    ]


def held_blocks():
    return pltpu.VMEM((2, ROWS, FF_STEP), BF)


def expert_forward_kernel(
    in_ref, win_hbm, wout_hbm, table_ref, table_t_ref, x_ref, act_hbm, slope_hbm, out_ref,
    win_ref, wout_ref, weight_sems, total, act_held, slope_held, sems,
):
    weights = start_weights(win_hbm, wout_hbm, win_ref, wout_ref, weight_sems)
    unpack(in_ref, table_ref[...], x_ref)
    total[...] = jnp.zeros_like(total)

    def one(columns, held):
        blocks = row_blocks()
        ups = mm(x_ref[blocks[0], :], win_ref[:, columns])
        for n, rows in enumerate(blocks):
            up = ups
            if n + 1 < len(blocks):
                ups = mm(x_ref[blocks[n + 1], :], win_ref[:, columns])
            act, slope = gelu_parts(up)
            act = act.astype(BF)
            held[0][rows, :] = act
            held[1][rows, :] = slope.astype(BF)
            total[rows, :] += mm(act, wout_ref[columns, :])

    over_hidden_units(one, weights, [act_held, slope_held], [act_hbm, slope_hbm], sems)
    pack(total[...].astype(BF), table_t_ref[...], out_ref, 0)


def expert_forward(arrived, first, second, table, table_t):
    return call(
        expert_forward_kernel,
        (shape(ROWS, D), shape(ROWS, FF), shape(ROWS, FF), shape(*CHUNKS)),
        "expert_forward",
        4 * ROWS * D * FF,
        20 << 20,
        vmem=40,
        free=(0,),
        in_specs=[VMEM, ANYWHERE, ANYWHERE, VMEM, VMEM],
        out_specs=(VMEM, ANYWHERE, ANYWHERE, VMEM),
        scratch_shapes=expert_space()
        + [pltpu.VMEM((ROWS, D), F32), held_blocks(), held_blocks(), pltpu.SemaphoreType.DMA((2, 2))],
    )(arrived, first, second, table, table_t)


def expert_back_kernel(
    section_ref, in_ref, win_hbm, wout_hbm, slope_hbm, table_ref, table_t_ref, other_ref, grad_ref, dup_hbm, out_ref,
    win_ref, wout_ref, weight_sems, total, slope, dup_held, sems,
):
    weights = start_weights(win_hbm, wout_hbm, win_ref, wout_ref, weight_sems, slope_hbm, slope)
    unpack(in_ref, table_ref[...], grad_ref)
    total[...] = jnp.zeros_like(total)

    def one(columns, held):
        blocks = row_blocks()
        dacts = mm_nt(grad_ref[blocks[0], :], wout_ref[columns, :])
        for n, rows in enumerate(blocks):
            dact = dacts
            if n + 1 < len(blocks):
                dacts = mm_nt(grad_ref[blocks[n + 1], :], wout_ref[columns, :])
            dup = (dact * slope[rows, columns].astype(F32)).astype(BF)
            held[0][rows, :] = dup
            total[rows, :] += mm_nt(dup, win_ref[:, columns])

    over_hidden_units(one, weights, [dup_held], [dup_hbm], sems)

    @pl.when(section_ref[0] == 0)
    def _():
        pack(total[...].astype(BF), table_t_ref[...], out_ref, 0)

    @pl.when(section_ref[0] == 1)
    def _():
        out_ref[...] = other_ref[...]


def expert_back(section, arrived, first, second, slope, table, table_t, other):
    return call(
        expert_back_kernel,
        (shape(ROWS, D), shape(ROWS, FF), shape(*CHUNKS)),
        "expert_back",
        4 * ROWS * D * FF,
        20 << 20,
        vmem=40,
        free=(1,),
        in_specs=[SMEM, VMEM, ANYWHERE, ANYWHERE, ANYWHERE, VMEM, VMEM, VMEM],
        out_specs=(VMEM, ANYWHERE, VMEM),
        scratch_shapes=expert_space()
        + [
            pltpu.VMEM((ROWS, D), F32),
            pltpu.VMEM((ROWS, FF), BF),
            held_blocks(),
            pltpu.SemaphoreType.DMA((2, 1)),
        ],
    )(section, arrived, first, second, slope, table, table_t, other)


def expert_both_kernel(
    in_ref, gin_ref, win_hbm, wout_hbm, table_ref, table_t_ref, x_ref, grad_ref, act_hbm, dup_hbm, back_ref,
    win_ref, wout_ref, weight_sems, dtotal, act_held, dup_held, sems,
):
    weights = start_weights(win_hbm, wout_hbm, win_ref, wout_ref, weight_sems)
    unpack(in_ref, table_ref[...], x_ref)
    unpack(gin_ref, table_ref[...], grad_ref)
    dtotal[...] = jnp.zeros_like(dtotal)

    def one(columns, held):
        blocks = row_blocks()

        def first_products(rows):
            return mm(x_ref[rows, :], win_ref[:, columns]), mm_nt(grad_ref[rows, :], wout_ref[columns, :])

        ahead = first_products(blocks[0])
        for n, rows in enumerate(blocks):
            up, dact = ahead
            if n + 1 < len(blocks):
                ahead = first_products(blocks[n + 1])
            act, slope = gelu_parts(up)
            dup = (dact * slope).astype(BF)
            act = act.astype(BF)
            held[0][rows, :] = act
            held[1][rows, :] = dup
            dtotal[rows, :] += mm_nt(dup, win_ref[:, columns])

    over_hidden_units(one, weights, [act_held, dup_held], [act_hbm, dup_hbm], sems)
    pack(dtotal[...].astype(BF), table_t_ref[...], back_ref, 0)


def expert_both(arrived, grads, first, second, table, table_t):
    return call(
        expert_both_kernel,
        (shape(ROWS, D), shape(ROWS, D), shape(ROWS, FF), shape(ROWS, FF), shape(*CHUNKS)),
        "expert_both",
        6 * ROWS * D * FF,
        24 << 20,
        vmem=44,
        free=(0, 1),
        in_specs=[VMEM, VMEM, ANYWHERE, ANYWHERE, VMEM, VMEM],
        out_specs=(VMEM, VMEM, ANYWHERE, ANYWHERE, VMEM),
        scratch_shapes=expert_space()
        + [
            pltpu.VMEM((ROWS, D), F32),
            held_blocks(),
            held_blocks(),
            pltpu.SemaphoreType.DMA((2, 2)),
        ],
    )(arrived, grads, first, second, table, table_t)


def expert_out_kernel(act_ref, wout_ref, table_t_ref, out_ref):
    pack(mm(act_ref[...], wout_ref[...]).astype(BF), table_t_ref[...], out_ref, 0)


def expert_out(act, second, table_t):
    return call(
        expert_out_kernel,
        shape(*CHUNKS),
        "expert_out",
        2 * ROWS * D * FF,
        10 << 20,
    )(act, second, table_t)


def parcel_kernel(w_ref, tail_ref, out_ref):
    for g in range(8):
        for part in range(3):
            lanes = slice(part * LANES, (part + 1) * LANES)
            if g < PAIRS:
                block = w_ref[:, part * D + g * LANES : part * D + (g + 1) * LANES]
            else:
                block = jnp.zeros((ROWS_OWN, LANES), BF)
            out_ref[g, 0:ROWS_OWN, lanes] = block
            out_ref[8 + g, 0:ROWS_OWN, lanes] = block
        out_ref[g, ROWS_OWN:, :] = tail_ref[...]
        out_ref[8 + g, ROWS_OWN:, :] = tail_ref[...]


def parcels_of(w_qkv, gain_attn, gain_ffn, rel_bias):
    row = jnp.concatenate([gain_attn.reshape(1, -1), gain_ffn.reshape(1, -1), rel_bias.reshape(1, -1)], axis=1)
    tail = jnp.pad(row, ((0, EXTRA - 1), (0, 3 * LANES - row.shape[1])))
    return call(parcel_kernel, shape(16, ROWS_OWN + EXTRA, 3 * LANES), "parcels", 0, 2 << 20)(w_qkv, tail)


def small_parts(parcels):
    rows = parcels[:, ROWS_OWN].astype(F32).reshape(2, 8, 3 * LANES)
    gain_a = rows[:, :, :ROWS_OWN].reshape(2, 1, D)
    gain_f = rows[:, :, ROWS_OWN : 2 * ROWS_OWN].reshape(2, 1, D)
    bias = rows[:, :, 2 * ROWS_OWN : 2 * ROWS_OWN + 4 * H].reshape(2, RELB, H)
    first = 2 * jnp.minimum(lax.axis_index("shard"), PAIRS - 1)
    return gain_a, gain_f, lax.dynamic_slice_in_dim(bias, first, 2, 2)


def project_kernel(layer, shard_ref, parcel_ref, gain_ref, *refs):
    blocks, normed_ref, qkv_ref = refs[:8], refs[8], refs[9]
    own = jnp.concatenate([parcel_ref[layer * 8 + j, 0:ROWS_OWN, :] for j in range(8)], axis=0)
    shard = shard_ref[0]
    for n in range(8):
        back, other = n % 4, n // 4
        source = lax.rem(shard + 8 - 2 * back, 8)
        if other:
            source = source + 1 - 2 * lax.rem(source, 2)
        rows = pl.ds(pl.multiple_of(source * TOK, TOK), TOK)
        normed = norm_of(blocks[n][0:TOK, :].astype(F32), gain_ref[layer])[0].astype(BF)
        normed_ref[rows, :] = normed
        qkv_ref[rows, :] = mm(normed, own).astype(BF)


def project(layer, shard, parcels, gain, blocks):
    return call(
        partial(project_kernel, layer),
        (shape(SEQ, D), shape(SEQ, 3 * LANES)),
        "project",
        2 * SEQ * D * 3 * LANES,
        5 << 20,
        in_specs=[SMEM] + [VMEM] * 10,
    )(shard, parcels, gain, *blocks)


WIDE = 4 * LANES


PIECE = 16
TILES = 3


def dense_grads_kernel(layer, shard_ref, normed_ref, dproj_ref, context_ref, branch_ref, *refs):
    out_hbm, held, sem = refs[-3:]
    dqkv = mm_tn(normed_ref[...], dproj_ref[...]).astype(BF)
    group = jnp.minimum(shard_ref[0], PAIRS - 1)
    columns = pl.ds(pl.multiple_of(group * LANES, LANES), LANES)
    dao = mm_tn(context_ref[...], branch_ref[:, columns]).astype(BF)
    for j in range(8):
        for tile in range(8 * TILES):
            first = j * ROWS_OWN + tile // 4 * PIECE
            part = tile % 4
            source = dqkv[:, part * LANES : (part + 1) * LANES] if part < 3 else dao
            lanes = slice(tile % TILES * LANES, (tile % TILES + 1) * LANES)
            held[tile // TILES * 8 + j, :, lanes] = source[first : first + PIECE]
    store = pltpu.make_async_copy(held, out_hbm.at[layer * 64 : (layer + 1) * 64], sem)
    store.start()
    store.wait()


def dense_grads(layer, shard, normed, dproj, context, branch, filled=None):
    more = () if filled is None else (filled,)
    return call(
        partial(dense_grads_kernel, layer),
        shape(128, PIECE, TILES * LANES),
        "dense_grads",
        2 * SEQ * D * 4 * LANES,
        6 << 20,
        in_specs=[SMEM] + [VMEM] * 4 + [ANYWHERE] * len(more),
        out_specs=ANYWHERE,
        scratch_shapes=[pltpu.VMEM((64, PIECE, TILES * LANES), BF), pltpu.SemaphoreType.DMA],
        input_output_aliases={5: 0} if more else {},
    )(shard, normed, dproj, context, branch, *more)


def finish_kernel(rep_ref, w_ref, gain_ref, *refs):
    blocks, (qkv_ref, ao_ref, gain_a_ref, gain_f_ref, bias_ref) = refs[:8], refs[8:]
    rep = rep_ref[0]
    for n in range(8):
        other, back = n // 4, n % 4
        piece = lax.rem(rep + 4 - back, 4) + lax.rem(rep // 4 + other, 2) * 4
        block = blocks[n]
        for q in range(TILES):
            tile = piece * TILES + q
            rows = pl.ds(pl.multiple_of(tile // 4 * PIECE, PIECE), PIECE)
            part = lax.rem(tile, 4)
            lanes = slice(q * LANES, (q + 1) * LANES)

            @pl.when(part < 3)
            def _(block=block, rows=rows, part=part, lanes=lanes):
                for g in range(PAIRS):
                    columns = pl.ds(pl.multiple_of(part * D + g * LANES, LANES), LANES)
                    qkv_ref[rows, columns] = block[g, :, lanes].astype(F32)

            @pl.when(part == 3)
            def _(block=block, rows=rows, lanes=lanes):
                for g in range(PAIRS):
                    ao_ref[rows, g * LANES : (g + 1) * LANES] = block[g, :, lanes].astype(F32)

    small = sum(blocks[n][8].astype(F32)[0:1, :] for n in range(8))
    gain_f_ref[...] = small[:, 0:ROWS_OWN]
    bias_ref[...] = small[:, LANES : 2 * LANES]
    products = jnp.zeros((ROWS_OWN, LANES), F32)
    for first in range(0, 3 * D, LANES):
        columns = slice(first, first + LANES)
        products = products + qkv_ref[:, columns] * w_ref[:, columns].astype(F32)
    sums = lax.dot_general(
        jnp.ones((8, LANES), F32), products, (((1,), (1,)), ((), ())), precision=HIGHEST, preferred_element_type=F32
    )
    gain_a_ref[...] = sums[0:1, :] / gain_ref[...]


def finish(rep, w_qkv, gain, blocks):
    return call(
        finish_kernel,
        (
            shape(ROWS_OWN, 3 * D, dtype=F32),
            shape(ROWS_OWN, D, dtype=F32),
            shape(1, ROWS_OWN, dtype=F32),
            shape(1, ROWS_OWN, dtype=F32),
            shape(1, LANES, dtype=F32),
        ),
        "finish",
        0,
        2 << 20,
        in_specs=[SMEM] + [VMEM] * 10,
    )(rep, w_qkv, gain, *blocks)


def spread(chunks):
    return lax.all_to_all(chunks, EVERYONE, split_axis=0, concat_axis=0, tiled=True)


def across(chunks):
    return lax.all_to_all(chunks, "shard", split_axis=0, concat_axis=0, tiled=True)


def swap(value):
    return lax.ppermute(value, "section", [(0, 1), (1, 0)])


def after(value, *others):
    return lax.optimization_barrier((value, *others))[0]


def tokens_of_all(own):
    n = 8

    def from_chip(back):
        return lax.ppermute(own, "shard", [(j, (j + 2 * back) % n) for j in range(n)])

    same_core = [own, from_chip(1), from_chip(2), from_chip(3)]
    return same_core + [lax.ppermute(block, "shard", [(j, j ^ 1) for j in range(n)]) for block in same_core]


def slot_tables(routes):
    flat = routes.reshape(2, 2 * TOK)
    onehot = (flat[..., None] == jnp.arange(EXPERTS, dtype=jnp.int32)).astype(BF)
    at = jnp.arange(2 * TOK, dtype=jnp.int32)
    earlier = (at[None, :] < at[:, None]).astype(BF)
    before = jnp.einsum("ab,lbe->lae", earlier, onehot, preferred_element_type=F32)
    rank = jnp.sum(before * onehot.astype(F32), axis=-1).astype(jnp.int32)
    return (flat * CAP + rank).reshape(routes.shape)


def per_device(
    inputs, cotangent, w_qkv, w_attn_out, gain_attn, gain_ffn, rel_bias, w_in, w_out, routes, gates
):
    section = lax.axis_index("section")
    shard = lax.axis_index("shard")
    first_proj, second_proj = w_in[0, 0], w_out[0, 0]
    hidden0 = lax.dynamic_index_in_dim(inputs[:, 0], section, 0, keepdims=False)
    cot = lax.dynamic_index_in_dim(cotangent[:, 0], section, 0, keepdims=False)
    table = pack_tables()
    table_t = table.T

    parcels = parcels_of(w_qkv[0], gain_attn, gain_ffn, rel_bias[0])
    got = lax.all_to_all(parcels, ("section", "shard"), split_axis=0, concat_axis=0, tiled=True)
    full0 = tokens_of_all(after(hidden0, parcels))

    def by_layer_rows(own):
        other = swap(own)
        return jnp.where(section == 0, own, other), jnp.where(section == 0, other, own)

    def gather(own, *when):
        return lax.all_gather(after(own, *when), "shard", axis=0, tiled=True)

    ao_rows = by_layer_rows(w_attn_out[0])
    ao0 = gather(ao_rows[0], *full0[1:4])
    got, *full0 = lax.optimization_barrier((got, *full0))
    gain_a, gain_f, bias = small_parts(got)
    tiles = [bias_tiles(bias[l]) for l in range(2)]

    def both_layers(values):
        own = lax.dynamic_index_in_dim(values[0, :, 0], section, 0, keepdims=False)
        other = swap(lax.dynamic_index_in_dim(values[0, :, 0], 1 - section, 0, keepdims=False))
        return jnp.where(section == 0, jnp.stack([own, other]), jnp.stack([other, own]))

    slot_cols = slot_tables(both_layers(routes))
    slot_rows = slot_cols.transpose(0, 2, 1)
    gate_cols = both_layers(gates)

    cot_rows = grad_rows(1, cot, slot_rows, gate_cols, table_t)
    own_index = shard.reshape(1)
    normed0, qkv0 = project(0, own_index, got, gain_a, full0)
    ctx0, weights0 = attention(qkv0, tiles[0])
    ctx0_tok = across(ctx0.reshape(8, TOK, LANES))
    ctx0_tok, cot_rows, slot_cols, slot_rows, gate_cols, table, table_t = lax.optimization_barrier(
        (ctx0_tok, cot_rows, slot_cols, slot_rows, gate_cols, table, table_t)
    )
    middle0, send, ctx0_own = middle_part(0, ctx0_tok, ao0, hidden0, gain_f, slot_rows, table_t, cot_rows)
    arrived0 = spread(send)
    x0, act0, slope0, made = expert_forward(arrived0, first_proj, second_proj, table, table_t)
    back = spread(made)
    ctx0_full = gather(ctx0_own)
    ao1 = gather(ao_rows[1], made, ctx0_full)
    qkv_rows = by_layer_rows(after(w_qkv[0], made))
    out0 = combine(0, back, middle0, slot_cols, gate_cols, table)

    normed1, qkv1 = project(1, own_index, got, gain_a, tokens_of_all(out0))
    ctx1, weights1 = attention(qkv1, tiles[1])
    ctx1_tok = across(ctx1.reshape(8, TOK, LANES))
    middle1, send, ctx1_own = middle_part(
        1, ctx1_tok, ao1, out0, gain_f, slot_rows, table_t, cot_rows
    )
    ctx1_full = gather(ctx1_own)
    arrived1 = spread(send)
    x1, g1, act1, dup1, dmade1 = expert_both(arrived1, arrived0, first_proj, second_proj, table, table_t)

    qkv_full1 = gather(qkv_rows[1], dmade1, ctx1_full)
    made1 = expert_out(act1, second_proj, table_t)
    back, made1 = lax.optimization_barrier((spread(dmade1), made1))
    dmid1, branch1, send, dgain_f1 = middle_back(1, back, slot_cols, table, cot, middle1, gain_f, ao1)
    dproj1, diag1 = attention_back(qkv1, weights1, across(send).reshape(SEQ, LANES))
    dproj1_tok = across(dproj1.reshape(8, TOK, 3 * LANES))
    branch1_full = gather(branch1, dproj1_tok, qkv_full1)
    dh1, send = hidden_back_send(1, dproj1_tok, qkv_full1, out0, gain_a, dmid1, slot_rows, gate_cols, table_t)

    arrived = spread(send)
    qkv_full0 = gather(qkv_rows[0], arrived, branch1_full)
    g0, dup0, dmade0 = expert_back(
        section.reshape(1), arrived, first_proj, second_proj, slope0, table, table_t, made1
    )
    back = spread(dmade0)

    def own(a, b):
        return jnp.where(section == 0, a, b)

    grad_in = mm_tn(own(x0, x1), own(dup0, dup1))
    grad_out = mm_tn(own(act0, act1), own(g0, g1))
    back, grad_in, grad_out = lax.optimization_barrier((back, grad_in, grad_out))
    out1 = combine(1, back, middle1, slot_cols, gate_cols, table)
    dmid0, branch0, send, dgain_f0 = middle_back(0, back, slot_cols, table, dh1, middle0, gain_f, ao0)
    branch0_full = gather(branch0, qkv_full0)
    dproj0, diag0 = attention_back(qkv0, weights0, across(send).reshape(SEQ, LANES))

    dproj0_tok = across(dproj0.reshape(8, TOK, 3 * LANES))
    parcels = dense_grads(1, own_index, normed1, dproj1, ctx1_full, branch1_full)
    parcels = dense_grads(0, own_index, normed0, dproj0, ctx0_full, branch0_full, parcels)
    parcels = after(parcels, dproj0_tok)
    got = spread(parcels)

    tail = jnp.concatenate(
        [dgain_f0, dgain_f1]
        + [jnp.pad(bias_grad(d).reshape(1, 2 * RELB), ((0, 0), (0, D - 2 * RELB))) for d in (diag0, diag1)],
        axis=0,
    ).astype(BF)
    dh0 = hidden_back(0, dproj0_tok, qkv_full0, hidden0, gain_a, dmid0)
    tails = after(gather(jnp.pad(tail, ((0, ROWS_OWN - 4), (0, 0)))), dh0, out1).reshape(8, ROWS_OWN, D)[:, :4].astype(F32)
    gain_sums = jnp.sum(tails[:, :2], axis=0)
    gain_sums = lax.dynamic_slice_in_dim(gain_sums, shard * ROWS_OWN, ROWS_OWN, 1)
    biases = lax.dynamic_slice_in_dim(tails[:PAIRS, 2:, : 2 * RELB], shard * 8, 8, 2)
    biases = biases.reshape(PAIRS, 2, 4, 2).transpose(1, 2, 0, 3).reshape(2, 4 * H)
    smalls = jnp.concatenate(
        [
            jnp.pad(gain_sums, ((0, 0), (0, LANES - ROWS_OWN))),
            jnp.pad(biases, ((0, 0), (0, 2 * LANES - 4 * H))),
        ],
        axis=1,
    )
    mine, theirs = own(smalls[0:1], smalls[1:2]), own(smalls[1:2], smalls[0:1])
    theirs = swap(jnp.pad(theirs, ((0, PIECE - 1), (0, 0))).astype(BF))
    small = (jnp.pad(mine, ((0, PIECE - 1), (0, 0))) + theirs.astype(F32)).astype(BF)

    got, dh0, small = lax.optimization_barrier((got, dh0, small))
    summed = jnp.sum(got.reshape(16, 8, PIECE, TILES * LANES).astype(F32), axis=0).astype(BF)
    summed = jnp.concatenate([summed, small[None]], axis=0)

    blocks = [summed] + [
        lax.ppermute(summed, "rep", [(r, r // 4 * 4 + (r + k) % 4) for r in range(8)]) for k in range(1, 4)
    ]
    blocks = blocks + [lax.ppermute(b, "rep", [(r, (r + 4) % 8) for r in range(8)]) for b in blocks]
    grad_qkv, grad_ao, dgain_a, dgain_f, drel = finish(
        lax.axis_index("rep").reshape(1), w_qkv[0], gain_attn.astype(F32), blocks
    )
    grad_bias = drel[:, : 4 * H].reshape(1, 4, H)

    def by_layer(layer0, layer1):
        keep = jnp.where(section == 0, layer0, layer1)
        other = swap(jnp.where(section == 0, layer1, layer0))
        pair = jnp.where(section == 0, jnp.stack([keep, other]), jnp.stack([other, keep]))
        return pair.reshape(1, 2, 1, TOK, D)

    return (
        by_layer(out0, out1),
        by_layer(dh0, dh1),
        grad_qkv[None],
        grad_ao[None],
        dgain_a,
        dgain_f,
        grad_bias,
        grad_in[None, None],
        grad_out[None, None],
    )


def solution(mesh):
    placed = (
        P(None, "rep", "shard", None),
        P(None, "rep", "shard", None),
        P("section", "shard", None),
        P("section", "shard", None),
        P("section", "shard"),
        P("section", "shard"),
        P("section", "shard", None),
        P("section", ("rep", "shard"), None, None),
        P("section", ("rep", "shard"), None, None),
        P("section", None, "rep", "shard", None),
        P("section", None, "rep", "shard", None),
    )
    return jax.shard_map(
        per_device,
        mesh=mesh,
        in_specs=placed,
        out_specs=(
            P("section", None, "rep", "shard", None),
            P("section", None, "rep", "shard", None),
            P("section", "shard", None),
            P("section", "shard", None),
            P("section", "shard"),
            P("section", "shard"),
            P("section", "shard", None),
            P("section", ("rep", "shard"), None, None),
            P("section", ("rep", "shard"), None, None),
        ),
        check_vma=False,
    )
```

```python
from functools import partial

import jax
import jax.numpy as jnp
from jax import lax
from jax.experimental import pallas as pl
from jax.experimental.pallas import tpu as pltpu
from jax.sharding import PartitionSpec as P

F32 = jnp.float32
BF = jnp.bfloat16
D = 768
H = 12
HD = 64
FF = 3072
SEQ = 1024
TOK = 128
BLOCK = 256
RELB = 32
EXPERTS = 64
CAP = 5
LANES = 128
COLS = D // LANES
CHUNK = 32
GROUP = 16
SLOTS = EXPERTS * CAP
GROUPS_ALL = 2 * EXPERTS // GROUP
ROWS = 2 * EXPERTS * CAP
PAIRS = H // 2
EPS = 1e-05
ROWS_OWN = 96
EXTRA = 16
EVERYONE = ("section", "rep", "shard")
HIGHEST = lax.Precision.HIGHEST
MIB = 1 << 20


def mm(a, b):
    return lax.dot_general(a, b, (((1,), (0,)), ((), ())), preferred_element_type=F32)


def mm_nt(a, b):
    return lax.dot_general(a, b, (((1,), (1,)), ((), ())), preferred_element_type=F32)


def mm_tn(a, b):
    return lax.dot_general(a, b, (((0,), (0,)), ((), ())), preferred_element_type=F32)


def call(kernel, outs, name, flops, moved, vmem=32, free=(), **more):
    run = pl.pallas_call(
        kernel,
        out_shape=outs,
        name=name,
        compiler_params=pltpu.CompilerParams(vmem_limit_bytes=vmem * MIB),
        cost_estimate=pl.CostEstimate(flops=flops, bytes_accessed=moved, transcendentals=0),
        **more,
    )

    def placed(*operands):
        return run(
            *(
                x if x.ndim == 1 or n in free else pltpu.with_memory_space_constraint(x, pltpu.HBM)
                for n, x in enumerate(operands)
            )
        )

    return placed


def shape(*dims, dtype=BF):
    return pltpu.HBM(dims, dtype)


VMEM = pl.BlockSpec(memory_space=pltpu.VMEM)
ANYWHERE = pl.BlockSpec(memory_space=pl.ANY)
SMEM = pl.BlockSpec(memory_space=pltpu.SMEM)


def pack_tables():
    row = jnp.arange(GROUP * CAP * COLS, dtype=jnp.int32)[:, None]
    col = jnp.arange(GROUP * CHUNK, dtype=jnp.int32)[None, :]
    block, inside = row // (GROUP * CAP), row % (GROUP * CAP)
    place = (inside // CAP) * CHUNK + block * CAP + inside % CAP
    return (place == col).astype(BF)


def unpack(chunks, table, target):
    size = GROUP * CAP
    for g in range(0, chunks.shape[0] // GROUP, 2):
        raw = [chunks[k * GROUP : (k + 1) * GROUP].reshape(GROUP * CHUNK, LANES) for k in (g, g + 1)]
        rows = mm(table, jnp.concatenate(raw, axis=1)).astype(BF)
        for k in range(2):
            for c in range(COLS):
                target[(g + k) * size : (g + k + 1) * size, c * LANES : (c + 1) * LANES] = rows[
                    c * size : (c + 1) * size, k * LANES : (k + 1) * LANES
                ]


def pack(rows, table_t, target, first):
    size = GROUP * CAP
    for g in range(0, rows.shape[0] // size, 2):
        stacked = jnp.concatenate(
            [
                jnp.concatenate(
                    [rows[k * size : (k + 1) * size, c * LANES : (c + 1) * LANES] for k in (g, g + 1)], axis=1
                )
                for c in range(COLS)
            ],
            axis=0,
        )
        both = mm(table_t, stacked).astype(BF)
        for k in range(2):
            chunk = both[:, k * LANES : (k + 1) * LANES].reshape(GROUP, CHUNK, LANES)
            target[first + (g + k) * GROUP : first + (g + k + 1) * GROUP] = chunk


def slots_by_token(slot_rows):
    places = lax.broadcasted_iota(jnp.int32, (SLOTS, TOK), 0)
    return [jnp.where(places == slot_rows[k : k + 1, :], 1.0, 0.0).astype(BF) for k in range(2)]


def tokens_by_slot(slot_cols):
    places = lax.broadcasted_iota(jnp.int32, (TOK, SLOTS), 1)
    return [jnp.where(places == slot_cols[:, k : k + 1], 1.0, 0.0).astype(BF) for k in range(2)]


def norm_of(hidden, gain):
    scaling = lax.rsqrt(jnp.mean(hidden * hidden, axis=-1, keepdims=True) + EPS)
    return hidden * scaling * gain, scaling


def norm_back(hidden, scaling, gain, grad):
    gain_grad = jnp.sum(grad * hidden * scaling, axis=0, keepdims=True)
    weighted = grad * gain
    inner = jnp.mean(weighted * hidden, axis=-1, keepdims=True)
    return weighted * scaling - hidden * (scaling * scaling * scaling * inner), gain_grad


def bias_tiles_kernel(line_ref, out_ref):
    for h in range(2):
        for delta in range(4):
            line = jnp.broadcast_to(line_ref[h * 4 + delta : h * 4 + delta + 1, :], (BLOCK, 2 * BLOCK))
            turned = pltpu.roll(line, 0, 1, stride=1, stride_axis=0)
            out_ref[h * 4 + delta] = turned[:, :BLOCK].astype(BF)


def bias_tiles(table):
    m = jnp.arange(2 * BLOCK, dtype=jnp.int32)
    ahead = jnp.where(m < BLOCK, m, m - 2 * BLOCK)
    distance = jnp.arange(4, dtype=jnp.int32)[:, None] * BLOCK - ahead[None, :]
    bucket = jnp.clip((distance + BLOCK) * RELB // (SEQ + BLOCK), 0, RELB - 1)
    onehot = (bucket[..., None] == jnp.arange(RELB, dtype=jnp.int32)).astype(F32)
    lines = jnp.einsum("dmb,bh->hdm", onehot, table, precision=HIGHEST).reshape(8, 2 * BLOCK)
    return call(bias_tiles_kernel, shape(8, BLOCK, BLOCK), "bias_tiles", 0, 1 << 20)(lines)


def head_mask(h, rows):
    lane = lax.broadcasted_iota(jnp.int32, (rows, LANES), 1)
    return (lane < HD) if h == 0 else (lane >= HD)


ATT_STEP = 256


def weight_blocks():
    return [(i, h) for i in range(4) for h in range(2)]


def weight_copy(i, h, vmem, hbm, sems, into):
    rows, keys = pl.ds(i * BLOCK, BLOCK), pl.ds(0, (i + 1) * BLOCK)
    ends = vmem.at[h, rows, keys], hbm.at[h, rows, keys]
    return pltpu.make_async_copy(*(ends if into else ends[::-1]), sems.at[h, i])


def attention_kernel(qkv_ref, bias_ref, ctx_ref, weights_hbm, held, sems):
    step = ATT_STEP
    for i in range(4):
        keys = (i + 1) * BLOCK
        key = qkv_ref[0:keys, LANES : 2 * LANES]
        value = qkv_ref[0:keys, 2 * LANES : 3 * LANES]
        for part in range(BLOCK // step):
            first = i * BLOCK + part * step
            query = qkv_ref[first : first + step, 0:LANES] * jnp.asarray(HD**-0.5, BF)
            zero = jnp.zeros_like(query)
            own = jnp.concatenate([jnp.where(head_mask(h, step), query, zero) for h in range(2)], axis=0)
            offset = jnp.concatenate(
                [
                    jnp.concatenate(
                        [bias_ref[h * 4 + i - b, part * step : (part + 1) * step, :] for b in range(i + 1)], axis=1
                    )
                    for h in range(2)
                ],
                axis=0,
            ).astype(F32)
            scores = mm_nt(own, key) + offset
            top = jnp.max(scores, axis=-1, keepdims=True)
            terms = jnp.exp(scores - top)
            total = jnp.sum(terms, axis=-1, keepdims=True)
            weights = (terms * (1.0 / total)).astype(BF)
            for h in range(2):
                held[h, first : first + step, 0:keys] = weights[h * step : (h + 1) * step]
            mixed = mm(weights, value)
            ctx_ref[first : first + step, :] = jnp.where(head_mask(0, step), mixed[:step], mixed[step:]).astype(BF)
        for h in range(2):
            weight_copy(i, h, held, weights_hbm, sems, True).start()
    for i, h in weight_blocks():
        weight_copy(i, h, held, weights_hbm, sems, True).wait()


def attention(qkv, tiles):
    return call(
        attention_kernel,
        (shape(SEQ, LANES), shape(2, SEQ, SEQ)),
        "attention",
        2 * 2 * 2 * SEQ * SEQ * LANES,
        8 << 20,
        in_specs=[VMEM] * 2,
        out_specs=(VMEM, ANYWHERE),
        scratch_shapes=[pltpu.VMEM((2, SEQ, SEQ), BF), pltpu.SemaphoreType.DMA((2, 4))],
    )(qkv, tiles)


def attention_back_kernel(qkv_ref, weights_hbm, dout_ref, flip_ref, dproj_ref, diag_ref, dkey, dvalue, tiles, held, sems):
    step = ATT_STEP
    for i, h in weight_blocks():
        weight_copy(i, h, held, weights_hbm, sems, False).start()
    dkey[...] = jnp.zeros_like(dkey)
    dvalue[...] = jnp.zeros_like(dvalue)
    for i in range(4):
        keys = (i + 1) * BLOCK
        key = qkv_ref[0:keys, LANES : 2 * LANES]
        value = qkv_ref[0:keys, 2 * LANES : 3 * LANES]
        for h in range(2):
            weight_copy(i, h, held, weights_hbm, sems, False).wait()
        for part in range(BLOCK // step):
            first = i * BLOCK + part * step
            rows = slice(part * step, (part + 1) * step)
            query = qkv_ref[first : first + step, 0:LANES]
            dout = dout_ref[first : first + step, :]
            query_t = query.astype(F32).T.astype(BF)
            dout_t = dout.astype(F32).T.astype(BF)
            zero = jnp.zeros_like(dout)
            own = jnp.concatenate([jnp.where(head_mask(h, step), dout, zero) for h in range(2)], axis=0)
            low = jnp.concatenate([held[h, first : first + step, 0:keys] for h in range(2)], axis=0)
            weights = low.astype(F32)
            dweights = mm_nt(own, value)
            delta = jnp.sum(weights * dweights, axis=-1, keepdims=True)
            dscores = weights * (dweights - delta)
            dlow = dscores.astype(BF)
            moved = mm(dlow, key)
            for h in range(2):
                mine = slice(h * step, (h + 1) * step)
                for b in range(i + 1):
                    tile = dscores[mine, b * BLOCK : (b + 1) * BLOCK]
                    n = h * 4 + i - b
                    tiles[n, rows, :] = tile if b == 0 else tiles[n, rows, :] + tile
                head = slice(h * HD, (h + 1) * HD)
                dkey[head, 0:keys] += mm(query_t[head], dlow[mine])
                dvalue[head, 0:keys] += mm(dout_t[head], low[mine])
            dquery = jnp.where(head_mask(0, step), moved[:step], moved[step:]) * HD**-0.5
            dproj_ref[first : first + step, 0:LANES] = dquery.astype(BF)
    dproj_ref[:, LANES : 2 * LANES] = (dkey[...] * HD**-0.5).T.astype(BF)
    dproj_ref[:, 2 * LANES : 3 * LANES] = dvalue[...].T.astype(BF)
    for n in range(8):
        tile = tiles[n]
        high = tile.astype(BF)
        rest = (tile - high.astype(F32)).astype(BF)
        flipped = mm(high, flip_ref[...]) + mm(rest, flip_ref[...])
        wide = jnp.concatenate([flipped, jnp.zeros_like(flipped)], axis=1)
        turned = pltpu.roll(wide, 0, 1, stride=1, stride_axis=0)
        diag_ref[n : n + 1, :] = jnp.sum(turned, axis=0, keepdims=True)


def attention_back(qkv, weights, dout):
    at = jnp.arange(BLOCK, dtype=jnp.int32)
    flip = (at[:, None] + at[None, :] == BLOCK - 1).astype(BF)
    return call(
        attention_back_kernel,
        (shape(SEQ, 3 * LANES), shape(8, 2 * BLOCK, dtype=F32)),
        "attention_back",
        2 * 4 * 2 * SEQ * SEQ * LANES,
        8 << 20,
        free=(2,),
        in_specs=[VMEM, ANYWHERE, VMEM, VMEM],
        out_specs=(VMEM, VMEM),
        scratch_shapes=[
            pltpu.VMEM((LANES, SEQ), F32),
            pltpu.VMEM((LANES, SEQ), F32),
            pltpu.VMEM((8, BLOCK, BLOCK), F32),
            pltpu.VMEM((2, SEQ, SEQ), BF),
            pltpu.SemaphoreType.DMA((2, 4)),
        ],
    )(qkv, weights, dout, flip)


def bias_grad(diag):
    m = jnp.arange(2 * BLOCK, dtype=jnp.int32)
    distance = jnp.arange(4, dtype=jnp.int32)[:, None] * BLOCK + m[None, :] - (BLOCK - 1)
    bucket = jnp.clip((distance + BLOCK) * RELB // (SEQ + BLOCK), 0, RELB - 1)
    onehot = (bucket[..., None] == jnp.arange(RELB, dtype=jnp.int32)).astype(F32)
    return jnp.einsum("hdm,dmb->bh", diag.reshape(2, 4, 2 * BLOCK), onehot, precision=HIGHEST)


def middle_kernel(
    layer, ctx_ref, wao_hbm, hidden_ref, gain_ref, slots_ref, table_ref, other_ref, middle_ref, out_ref, context_ref, wao_ref, sem
):
    load = pltpu.make_async_copy(wao_hbm, wao_ref, sem)
    load.start()
    context = jnp.concatenate([ctx_ref[g] for g in range(PAIRS)], axis=1)
    context_ref[...] = context
    load.wait()
    middle = hidden_ref[...].astype(F32) + mm(context, wao_ref[...])
    middle_ref[...] = middle
    normed = norm_of(middle, gain_ref[layer])[0].astype(BF)
    first, second = slots_by_token(slots_ref[layer])
    rows = mm(first + second, normed).astype(BF)
    pack(rows, table_ref[...], out_ref, layer * EXPERTS)
    other = (1 - layer) * EXPERTS
    out_ref[other : other + EXPERTS] = other_ref[...]


def weight_space(columns):
    return [pltpu.VMEM((D, columns), BF), pltpu.SemaphoreType.DMA]


def middle_part(layer, ctx, wao, hidden, gain, slot_rows, table_t, other):
    return call(
        partial(middle_kernel, layer),
        (shape(TOK, D, dtype=F32), shape(2 * EXPERTS, CHUNK, LANES), shape(TOK, D)),
        "middle",
        2 * TOK * D * D + 2 * SLOTS * TOK * D * 5,
        4 << 20,
        free=(0,),
        in_specs=[VMEM, ANYWHERE, VMEM, VMEM, VMEM, VMEM, VMEM],
        scratch_shapes=weight_space(D),
    )(ctx, wao, hidden, gain, slot_rows, table_t, other)


def combined(layer, back_ref, middle_ref, slots_ref, gates_ref, table_ref, rows):
    unpack(back_ref.at[layer * EXPERTS : (layer + 1) * EXPERTS], table_ref[...], rows)
    picks = tokens_by_slot(slots_ref[layer])
    gates = gates_ref[layer]
    total = middle_ref[...]
    for k in range(2):
        total = total + gates[:, k : k + 1] * mm(picks[k], rows[...])
    return total.astype(BF)


def combine_kernel(layer, back_ref, middle_ref, slots_ref, gates_ref, table_ref, out_ref, rows):
    out_ref[...] = combined(layer, back_ref, middle_ref, slots_ref, gates_ref, table_ref, rows)


def combine(layer, back, middle, slot_cols, gates, table):
    return call(
        partial(combine_kernel, layer),
        shape(TOK, D),
        "combine",
        2 * TOK * SLOTS * D * 6,
        4 << 20,
        free=(0,),
        in_specs=[VMEM, VMEM, VMEM, VMEM, VMEM],
        scratch_shapes=[pltpu.VMEM((SLOTS, D), BF)],
    )(back, middle, slot_cols, gates, table)


def grad_chunks(dout, slot_rows, gates, table_t, out_ref, first):
    picks = slots_by_token(slot_rows)
    wide = dout.astype(F32)
    rows = mm(picks[0], (wide * gates[:, 0:1]).astype(BF)) + mm(picks[1], (wide * gates[:, 1:2]).astype(BF))
    pack(rows.astype(BF), table_t, out_ref, first)


def grad_rows_kernel(layer, dout_ref, slots_ref, gates_ref, table_ref, out_ref):
    grad_chunks(dout_ref[...], slots_ref[layer], gates_ref[layer], table_ref[...], out_ref, 0)


def grad_rows(layer, dout, slot_rows, gates, table_t):
    return call(
        partial(grad_rows_kernel, layer),
        shape(EXPERTS, CHUNK, LANES),
        "grad_rows",
        4 * TOK * SLOTS * D * 3,
        2 << 20,
    )(dout, slot_rows, gates, table_t)


def middle_back_kernel(
    layer, back_ref, slots_ref, table_ref, dout_ref, middle_ref, gain_ref, wao_hbm, dmid_ref, branch_ref, send_ref, dgain_ref,
    rows, wao_ref, sem,
):
    load = pltpu.make_async_copy(wao_hbm, wao_ref, sem)
    load.start()
    unpack(back_ref.at[layer * EXPERTS : (layer + 1) * EXPERTS], table_ref[...], rows)
    first, second = tokens_by_slot(slots_ref[layer])
    dnormed = mm(first + second, rows[...])
    middle = middle_ref[...]
    gain = gain_ref[layer]
    scaling = lax.rsqrt(jnp.mean(middle * middle, axis=-1, keepdims=True) + EPS)
    moved, dgain = norm_back(middle, scaling, gain, dnormed)
    dgain_ref[...] = dgain
    dmid = dout_ref[...].astype(F32) + moved
    dmid_ref[...] = dmid
    branch = dmid.astype(BF)
    branch_ref[...] = branch
    load.wait()
    dcontext = mm_nt(branch, wao_ref[...]).astype(BF)
    for g in range(PAIRS):
        send_ref[g] = dcontext[:, g * LANES : (g + 1) * LANES]
    send_ref[PAIRS:8] = jnp.zeros((8 - PAIRS, TOK, LANES), BF)


def middle_back(layer, back, slot_cols, table, dout, middle, gain, wao):
    return call(
        partial(middle_back_kernel, layer),
        (shape(TOK, D, dtype=F32), shape(TOK, D), shape(8, TOK, LANES), shape(1, D, dtype=F32)),
        "middle_back",
        2 * TOK * D * D + 2 * TOK * SLOTS * D * 5,
        4 << 20,
        free=(0,),
        in_specs=[VMEM] * 6 + [ANYWHERE],
        scratch_shapes=[pltpu.VMEM((SLOTS, D), BF)] + weight_space(D),
    )(back, slot_cols, table, dout, middle, gain, wao)


def hidden_grad(layer, back_ref, wqkv_hbm, hidden_ref, gain_ref, dmid_ref, wqkv_ref, sem):
    load = pltpu.make_async_copy(wqkv_hbm, wqkv_ref, sem)
    load.start()
    parts = [
        back_ref[g, :, part * LANES : (part + 1) * LANES] for part in range(3) for g in range(PAIRS)
    ]
    hidden = hidden_ref[...].astype(F32)
    scaling = lax.rsqrt(jnp.mean(hidden * hidden, axis=-1, keepdims=True) + EPS)
    load.wait()
    dnormed = mm_nt(jnp.concatenate(parts, axis=1), wqkv_ref[...])
    moved, _ = norm_back(hidden, scaling, gain_ref[layer], dnormed)
    return (dmid_ref[...] + moved).astype(BF)


def hidden_back_kernel(layer, back_ref, wqkv_hbm, hidden_ref, gain_ref, dmid_ref, dh_ref, wqkv_ref, sem):
    dh_ref[...] = hidden_grad(layer, back_ref, wqkv_hbm, hidden_ref, gain_ref, dmid_ref, wqkv_ref, sem)


def hidden_back_send_kernel(
    layer, back_ref, wqkv_hbm, hidden_ref, gain_ref, dmid_ref, slots_ref, gates_ref, table_ref, dh_ref, out_ref, wqkv_ref, sem
):
    dh = hidden_grad(layer, back_ref, wqkv_hbm, hidden_ref, gain_ref, dmid_ref, wqkv_ref, sem)
    dh_ref[...] = dh
    below = layer - 1
    grad_chunks(dh, slots_ref[below], gates_ref[below], table_ref[...], out_ref, below * EXPERTS)
    out_ref[layer * EXPERTS : (layer + 1) * EXPERTS] = jnp.zeros((EXPERTS, CHUNK, LANES), BF)


def hidden_back(layer, back, wqkv, hidden, gain, dmid):
    return call(
        partial(hidden_back_kernel, layer),
        shape(TOK, D),
        "hidden_back",
        2 * TOK * D * 3 * D,
        5 << 20,
        free=(0,),
        in_specs=[VMEM, ANYWHERE, VMEM, VMEM, VMEM],
        scratch_shapes=weight_space(3 * D),
    )(back, wqkv, hidden, gain, dmid)


def hidden_back_send(layer, back, wqkv, hidden, gain, dmid, slot_rows, gates, table_t):
    return call(
        partial(hidden_back_send_kernel, layer),
        (shape(TOK, D), shape(2 * EXPERTS, CHUNK, LANES)),
        "hidden_back_send",
        2 * TOK * D * 3 * D,
        6 << 20,
        free=(0,),
        in_specs=[VMEM, ANYWHERE] + [VMEM] * 6,
        scratch_shapes=weight_space(3 * D),
    )(back, wqkv, hidden, gain, dmid, slot_rows, gates, table_t)


FF_STEP = 1024
ROW_STEP = 320
CHUNKS = (2 * EXPERTS, CHUNK, LANES)


def gelu_parts(up):
    phi = 0.5 + 0.5 * lax.erf(up * 0.5**0.5)
    return up * phi, phi + up * (jnp.exp(up * up * -0.5) * 0.3989422804014327)


def row_blocks():
    return [slice(r, r + ROW_STEP) for r in range(0, ROWS, ROW_STEP)]


def over_hidden_units(one, weights, buffers, targets, sems):
    def copy(f, slot, k):
        columns = pl.ds(pl.multiple_of(f * FF_STEP, FF_STEP), FF_STEP)
        return pltpu.make_async_copy(buffers[k].at[slot], targets[k].at[:, columns], sems.at[slot, k])

    def step(f, carry):
        slot = lax.rem(f, 2)

        @pl.when(f >= 2)
        def _():
            for k in range(len(buffers)):
                copy(f - 2, slot, k).wait()

        for load in weights(f):
            load.wait()
        one(pl.ds(pl.multiple_of(f * FF_STEP, FF_STEP), FF_STEP), [b.at[slot] for b in buffers])
        for k in range(len(buffers)):
            copy(f, slot, k).start()
        return carry

    last = FF // FF_STEP
    lax.fori_loop(0, last, step, 0)
    for f in range(last - 2, last):
        for k in range(len(buffers)):
            copy(f, f % 2, k).wait()


def start_weights(win_hbm, wout_hbm, win_ref, wout_ref, sems, slope_hbm=None, slope=None):
    def copies(f):
        units = pl.ds(pl.multiple_of(f * FF_STEP, FF_STEP), FF_STEP)
        loads = [
            pltpu.make_async_copy(win_hbm.at[:, units], win_ref.at[:, units], sems.at[f, 0]),
            pltpu.make_async_copy(wout_hbm.at[units, :], wout_ref.at[units, :], sems.at[f, 1]),
        ]
        if slope is not None:
            loads.append(pltpu.make_async_copy(slope_hbm.at[:, units], slope.at[:, units], sems.at[f, 2]))
        return loads

    for f in range(FF // FF_STEP):
        for load in copies(f):
            load.start()
    return copies


def expert_space():
    return [
        pltpu.VMEM((D, FF), BF),
        pltpu.VMEM((FF, D), BF),
        pltpu.SemaphoreType.DMA((FF // FF_STEP, 3)),
    ]


def held_blocks():
    return pltpu.VMEM((2, ROWS, FF_STEP), BF)


def expert_forward_kernel(
    in_ref, win_hbm, wout_hbm, table_ref, table_t_ref, x_ref, act_hbm, slope_hbm, out_ref,
    win_ref, wout_ref, weight_sems, total, act_held, slope_held, sems,
):
    weights = start_weights(win_hbm, wout_hbm, win_ref, wout_ref, weight_sems)
    unpack(in_ref, table_ref[...], x_ref)
    total[...] = jnp.zeros_like(total)

    def one(columns, held):
        blocks = row_blocks()
        ups = mm(x_ref[blocks[0], :], win_ref[:, columns])
        for n, rows in enumerate(blocks):
            up = ups
            if n + 1 < len(blocks):
                ups = mm(x_ref[blocks[n + 1], :], win_ref[:, columns])
            act, slope = gelu_parts(up)
            act = act.astype(BF)
            held[0][rows, :] = act
            held[1][rows, :] = slope.astype(BF)
            total[rows, :] += mm(act, wout_ref[columns, :])

    over_hidden_units(one, weights, [act_held, slope_held], [act_hbm, slope_hbm], sems)
    pack(total[...].astype(BF), table_t_ref[...], out_ref, 0)


def expert_forward(arrived, first, second, table, table_t):
    return call(
        expert_forward_kernel,
        (shape(ROWS, D), shape(ROWS, FF), shape(ROWS, FF), shape(*CHUNKS)),
        "expert_forward",
        4 * ROWS * D * FF,
        20 << 20,
        vmem=40,
        free=(0,),
        in_specs=[VMEM, ANYWHERE, ANYWHERE, VMEM, VMEM],
        out_specs=(VMEM, ANYWHERE, ANYWHERE, VMEM),
        scratch_shapes=expert_space()
        + [pltpu.VMEM((ROWS, D), F32), held_blocks(), held_blocks(), pltpu.SemaphoreType.DMA((2, 2))],
    )(arrived, first, second, table, table_t)


def expert_back_kernel(
    section_ref, in_ref, win_hbm, wout_hbm, slope_hbm, table_ref, table_t_ref, other_ref, grad_ref, dup_hbm, out_ref,
    win_ref, wout_ref, weight_sems, total, slope, dup_held, sems,
):
    weights = start_weights(win_hbm, wout_hbm, win_ref, wout_ref, weight_sems, slope_hbm, slope)
    unpack(in_ref, table_ref[...], grad_ref)
    total[...] = jnp.zeros_like(total)

    def one(columns, held):
        blocks = row_blocks()
        dacts = mm_nt(grad_ref[blocks[0], :], wout_ref[columns, :])
        for n, rows in enumerate(blocks):
            dact = dacts
            if n + 1 < len(blocks):
                dacts = mm_nt(grad_ref[blocks[n + 1], :], wout_ref[columns, :])
            dup = (dact * slope[rows, columns].astype(F32)).astype(BF)
            held[0][rows, :] = dup
            total[rows, :] += mm_nt(dup, win_ref[:, columns])

    over_hidden_units(one, weights, [dup_held], [dup_hbm], sems)

    @pl.when(section_ref[0] == 0)
    def _():
        pack(total[...].astype(BF), table_t_ref[...], out_ref, 0)

    @pl.when(section_ref[0] == 1)
    def _():
        out_ref[...] = other_ref[...]


def expert_back(section, arrived, first, second, slope, table, table_t, other):
    return call(
        expert_back_kernel,
        (shape(ROWS, D), shape(ROWS, FF), shape(*CHUNKS)),
        "expert_back",
        4 * ROWS * D * FF,
        20 << 20,
        vmem=40,
        free=(1,),
        in_specs=[SMEM, VMEM, ANYWHERE, ANYWHERE, ANYWHERE, VMEM, VMEM, VMEM],
        out_specs=(VMEM, ANYWHERE, VMEM),
        scratch_shapes=expert_space()
        + [
            pltpu.VMEM((ROWS, D), F32),
            pltpu.VMEM((ROWS, FF), BF),
            held_blocks(),
            pltpu.SemaphoreType.DMA((2, 1)),
        ],
    )(section, arrived, first, second, slope, table, table_t, other)


def expert_both_kernel(
    in_ref, gin_ref, win_hbm, wout_hbm, table_ref, table_t_ref, x_ref, grad_ref, act_hbm, dup_hbm, back_ref,
    win_ref, wout_ref, weight_sems, dtotal, act_held, dup_held, sems,
):
    weights = start_weights(win_hbm, wout_hbm, win_ref, wout_ref, weight_sems)
    unpack(in_ref, table_ref[...], x_ref)
    unpack(gin_ref, table_ref[...], grad_ref)
    dtotal[...] = jnp.zeros_like(dtotal)

    def one(columns, held):
        blocks = row_blocks()

        def first_products(rows):
            return mm(x_ref[rows, :], win_ref[:, columns]), mm_nt(grad_ref[rows, :], wout_ref[columns, :])

        ahead = first_products(blocks[0])
        for n, rows in enumerate(blocks):
            up, dact = ahead
            if n + 1 < len(blocks):
                ahead = first_products(blocks[n + 1])
            act, slope = gelu_parts(up)
            dup = (dact * slope).astype(BF)
            act = act.astype(BF)
            held[0][rows, :] = act
            held[1][rows, :] = dup
            dtotal[rows, :] += mm_nt(dup, win_ref[:, columns])

    over_hidden_units(one, weights, [act_held, dup_held], [act_hbm, dup_hbm], sems)
    pack(dtotal[...].astype(BF), table_t_ref[...], back_ref, 0)


def expert_both(arrived, grads, first, second, table, table_t):
    return call(
        expert_both_kernel,
        (shape(ROWS, D), shape(ROWS, D), shape(ROWS, FF), shape(ROWS, FF), shape(*CHUNKS)),
        "expert_both",
        6 * ROWS * D * FF,
        24 << 20,
        vmem=44,
        free=(0, 1),
        in_specs=[VMEM, VMEM, ANYWHERE, ANYWHERE, VMEM, VMEM],
        out_specs=(VMEM, VMEM, ANYWHERE, ANYWHERE, VMEM),
        scratch_shapes=expert_space()
        + [
            pltpu.VMEM((ROWS, D), F32),
            held_blocks(),
            held_blocks(),
            pltpu.SemaphoreType.DMA((2, 2)),
        ],
    )(arrived, grads, first, second, table, table_t)


def expert_out_kernel(act_ref, wout_ref, table_t_ref, out_ref):
    pack(mm(act_ref[...], wout_ref[...]).astype(BF), table_t_ref[...], out_ref, 0)


def expert_out(act, second, table_t):
    return call(
        expert_out_kernel,
        shape(*CHUNKS),
        "expert_out",
        2 * ROWS * D * FF,
        10 << 20,
    )(act, second, table_t)


def parcel_kernel(w_ref, tail_ref, out_ref):
    for g in range(8):
        for part in range(3):
            lanes = slice(part * LANES, (part + 1) * LANES)
            if g < PAIRS:
                block = w_ref[:, part * D + g * LANES : part * D + (g + 1) * LANES]
            else:
                block = jnp.zeros((ROWS_OWN, LANES), BF)
            out_ref[g, 0:ROWS_OWN, lanes] = block
            out_ref[8 + g, 0:ROWS_OWN, lanes] = block
        out_ref[g, ROWS_OWN:, :] = tail_ref[...]
        out_ref[8 + g, ROWS_OWN:, :] = tail_ref[...]


def parcels_of(w_qkv, gain_attn, gain_ffn, rel_bias):
    row = jnp.concatenate([gain_attn.reshape(1, -1), gain_ffn.reshape(1, -1), rel_bias.reshape(1, -1)], axis=1)
    tail = jnp.pad(row, ((0, EXTRA - 1), (0, 3 * LANES - row.shape[1])))
    return call(parcel_kernel, shape(16, ROWS_OWN + EXTRA, 3 * LANES), "parcels", 0, 2 << 20)(w_qkv, tail)


def small_parts(parcels):
    rows = parcels[:, ROWS_OWN].astype(F32).reshape(2, 8, 3 * LANES)
    gain_a = rows[:, :, :ROWS_OWN].reshape(2, 1, D)
    gain_f = rows[:, :, ROWS_OWN : 2 * ROWS_OWN].reshape(2, 1, D)
    bias = rows[:, :, 2 * ROWS_OWN : 2 * ROWS_OWN + 4 * H].reshape(2, RELB, H)
    first = 2 * jnp.minimum(lax.axis_index("shard"), PAIRS - 1)
    return gain_a, gain_f, lax.dynamic_slice_in_dim(bias, first, 2, 2)


def project_kernel(layer, shard_ref, parcel_ref, gain_ref, *refs):
    blocks, normed_ref, qkv_ref = refs[:8], refs[8], refs[9]
    own = jnp.concatenate([parcel_ref[layer * 8 + j, 0:ROWS_OWN, :] for j in range(8)], axis=0)
    shard = shard_ref[0]
    for n in range(8):
        back, other = n % 4, n // 4
        source = lax.rem(shard + 8 - 2 * back, 8)
        if other:
            source = source + 1 - 2 * lax.rem(source, 2)
        rows = pl.ds(pl.multiple_of(source * TOK, TOK), TOK)
        normed = norm_of(blocks[n][0:TOK, :].astype(F32), gain_ref[layer])[0].astype(BF)
        normed_ref[rows, :] = normed
        qkv_ref[rows, :] = mm(normed, own).astype(BF)


def project(layer, shard, parcels, gain, blocks):
    return call(
        partial(project_kernel, layer),
        (shape(SEQ, D), shape(SEQ, 3 * LANES)),
        "project",
        2 * SEQ * D * 3 * LANES,
        5 << 20,
        in_specs=[SMEM] + [VMEM] * 10,
    )(shard, parcels, gain, *blocks)


WIDE = 4 * LANES


PIECE = 16
TILES = 3


def dense_grads_kernel(layer, shard_ref, normed_ref, dproj_ref, context_ref, branch_ref, *refs):
    out_hbm, held, sem = refs[-3:]
    dqkv = mm_tn(normed_ref[...], dproj_ref[...]).astype(BF)
    group = jnp.minimum(shard_ref[0], PAIRS - 1)
    columns = pl.ds(pl.multiple_of(group * LANES, LANES), LANES)
    dao = mm_tn(context_ref[...], branch_ref[:, columns]).astype(BF)
    for j in range(8):
        for tile in range(8 * TILES):
            first = j * ROWS_OWN + tile // 4 * PIECE
            part = tile % 4
            source = dqkv[:, part * LANES : (part + 1) * LANES] if part < 3 else dao
            lanes = slice(tile % TILES * LANES, (tile % TILES + 1) * LANES)
            held[tile // TILES * 8 + j, :, lanes] = source[first : first + PIECE]
    store = pltpu.make_async_copy(held, out_hbm.at[layer * 64 : (layer + 1) * 64], sem)
    store.start()
    store.wait()


def dense_grads(layer, shard, normed, dproj, context, branch, filled=None):
    more = () if filled is None else (filled,)
    return call(
        partial(dense_grads_kernel, layer),
        shape(128, PIECE, TILES * LANES),
        "dense_grads",
        2 * SEQ * D * 4 * LANES,
        6 << 20,
        in_specs=[SMEM] + [VMEM] * 4 + [ANYWHERE] * len(more),
        out_specs=ANYWHERE,
        scratch_shapes=[pltpu.VMEM((64, PIECE, TILES * LANES), BF), pltpu.SemaphoreType.DMA],
        input_output_aliases={5: 0} if more else {},
    )(shard, normed, dproj, context, branch, *more)


def finish_kernel(rep_ref, w_ref, gain_ref, *refs):
    blocks, (qkv_ref, ao_ref, gain_a_ref, gain_f_ref, bias_ref) = refs[:8], refs[8:]
    rep = rep_ref[0]
    for n in range(8):
        other, back = n // 4, n % 4
        piece = lax.rem(rep + 4 - back, 4) + lax.rem(rep // 4 + other, 2) * 4
        block = blocks[n]
        for q in range(TILES):
            tile = piece * TILES + q
            rows = pl.ds(pl.multiple_of(tile // 4 * PIECE, PIECE), PIECE)
            part = lax.rem(tile, 4)
            lanes = slice(q * LANES, (q + 1) * LANES)

            @pl.when(part < 3)
            def _(block=block, rows=rows, part=part, lanes=lanes):
                for g in range(PAIRS):
                    columns = pl.ds(pl.multiple_of(part * D + g * LANES, LANES), LANES)
                    qkv_ref[rows, columns] = block[g, :, lanes].astype(F32)

            @pl.when(part == 3)
            def _(block=block, rows=rows, lanes=lanes):
                for g in range(PAIRS):
                    ao_ref[rows, g * LANES : (g + 1) * LANES] = block[g, :, lanes].astype(F32)

    small = sum(blocks[n][8].astype(F32)[0:1, :] for n in range(8))
    gain_f_ref[...] = small[:, 0:ROWS_OWN]
    bias_ref[...] = small[:, LANES : 2 * LANES]
    products = jnp.zeros((ROWS_OWN, LANES), F32)
    for first in range(0, 3 * D, LANES):
        columns = slice(first, first + LANES)
        products = products + qkv_ref[:, columns] * w_ref[:, columns].astype(F32)
    sums = lax.dot_general(
        jnp.ones((8, LANES), F32), products, (((1,), (1,)), ((), ())), precision=HIGHEST, preferred_element_type=F32
    )
    gain_a_ref[...] = sums[0:1, :] / gain_ref[...]


def finish(rep, w_qkv, gain, blocks):
    return call(
        finish_kernel,
        (
            shape(ROWS_OWN, 3 * D, dtype=F32),
            shape(ROWS_OWN, D, dtype=F32),
            shape(1, ROWS_OWN, dtype=F32),
            shape(1, ROWS_OWN, dtype=F32),
            shape(1, LANES, dtype=F32),
        ),
        "finish",
        0,
        2 << 20,
        in_specs=[SMEM] + [VMEM] * 10,
    )(rep, w_qkv, gain, *blocks)


def spread(chunks):
    return lax.all_to_all(chunks, EVERYONE, split_axis=0, concat_axis=0, tiled=True)


def across(chunks):
    return lax.all_to_all(chunks, "shard", split_axis=0, concat_axis=0, tiled=True)


def swap(value):
    return lax.ppermute(value, "section", [(0, 1), (1, 0)])


def after(value, *others):
    return lax.optimization_barrier((value, *others))[0]


def tokens_of_all(own):
    n = 8

    def from_chip(back):
        return lax.ppermute(own, "shard", [(j, (j + 2 * back) % n) for j in range(n)])

    same_core = [own, from_chip(1), from_chip(2), from_chip(3)]
    return same_core + [lax.ppermute(block, "shard", [(j, j ^ 1) for j in range(n)]) for block in same_core]


def slot_tables(routes):
    flat = routes.reshape(2, 2 * TOK)
    onehot = (flat[..., None] == jnp.arange(EXPERTS, dtype=jnp.int32)).astype(BF)
    at = jnp.arange(2 * TOK, dtype=jnp.int32)
    earlier = (at[None, :] < at[:, None]).astype(BF)
    before = jnp.einsum("ab,lbe->lae", earlier, onehot, preferred_element_type=F32)
    rank = jnp.sum(before * onehot.astype(F32), axis=-1).astype(jnp.int32)
    return (flat * CAP + rank).reshape(routes.shape)


def per_device(
    inputs, cotangent, w_qkv, w_attn_out, gain_attn, gain_ffn, rel_bias, w_in, w_out, routes, gates
):
    section = lax.axis_index("section")
    shard = lax.axis_index("shard")
    first_proj, second_proj = w_in[0, 0], w_out[0, 0]
    hidden0 = lax.dynamic_index_in_dim(inputs[:, 0], section, 0, keepdims=False)
    cot = lax.dynamic_index_in_dim(cotangent[:, 0], section, 0, keepdims=False)
    table = pack_tables()
    table_t = table.T

    parcels = parcels_of(w_qkv[0], gain_attn, gain_ffn, rel_bias[0])
    got = lax.all_to_all(parcels, ("section", "shard"), split_axis=0, concat_axis=0, tiled=True)
    full0 = tokens_of_all(after(hidden0, parcels))

    def by_layer_rows(own):
        other = swap(own)
        return jnp.where(section == 0, own, other), jnp.where(section == 0, other, own)

    def gather(own, *when):
        return lax.all_gather(after(own, *when), "shard", axis=0, tiled=True)

    ao_rows = by_layer_rows(w_attn_out[0])
    ao0 = gather(ao_rows[0], *full0[1:4])
    got, *full0 = lax.optimization_barrier((got, *full0))
    gain_a, gain_f, bias = small_parts(got)
    tiles = [bias_tiles(bias[l]) for l in range(2)]

    def both_layers(values):
        own = lax.dynamic_index_in_dim(values[0, :, 0], section, 0, keepdims=False)
        other = swap(lax.dynamic_index_in_dim(values[0, :, 0], 1 - section, 0, keepdims=False))
        return jnp.where(section == 0, jnp.stack([own, other]), jnp.stack([other, own]))

    slot_cols = slot_tables(both_layers(routes))
    slot_rows = slot_cols.transpose(0, 2, 1)
    gate_cols = both_layers(gates)

    cot_rows = grad_rows(1, cot, slot_rows, gate_cols, table_t)
    own_index = shard.reshape(1)
    normed0, qkv0 = project(0, own_index, got, gain_a, full0)
    ctx0, weights0 = attention(qkv0, tiles[0])
    ctx0_tok = across(ctx0.reshape(8, TOK, LANES))
    ctx0_tok, cot_rows, slot_cols, slot_rows, gate_cols, table, table_t = lax.optimization_barrier(
        (ctx0_tok, cot_rows, slot_cols, slot_rows, gate_cols, table, table_t)
    )
    middle0, send, ctx0_own = middle_part(0, ctx0_tok, ao0, hidden0, gain_f, slot_rows, table_t, cot_rows)
    arrived0 = spread(send)
    x0, act0, slope0, made = expert_forward(arrived0, first_proj, second_proj, table, table_t)
    back, tiles[1] = lax.optimization_barrier((spread(made), tiles[1]))
    ctx0_full = gather(ctx0_own)
    ao1 = gather(ao_rows[1], made, ctx0_full)
    qkv_rows = by_layer_rows(after(w_qkv[0], made))
    out0 = combine(0, back, middle0, slot_cols, gate_cols, table)

    normed1, qkv1 = project(1, own_index, got, gain_a, tokens_of_all(out0))
    ctx1, weights1 = attention(qkv1, tiles[1])
    ctx1_tok = across(ctx1.reshape(8, TOK, LANES))
    middle1, send, ctx1_own = middle_part(
        1, ctx1_tok, ao1, out0, gain_f, slot_rows, table_t, cot_rows
    )
    ctx1_full = gather(ctx1_own)
    arrived1 = spread(send)
    x1, g1, act1, dup1, dmade1 = expert_both(arrived1, arrived0, first_proj, second_proj, table, table_t)

    qkv_full1 = gather(qkv_rows[1], dmade1, ctx1_full)
    made1 = expert_out(act1, second_proj, table_t)
    back, made1 = lax.optimization_barrier((spread(dmade1), made1))
    dmid1, branch1, send, dgain_f1 = middle_back(1, back, slot_cols, table, cot, middle1, gain_f, ao1)
    dproj1, diag1 = attention_back(qkv1, weights1, across(send).reshape(SEQ, LANES))
    dproj1_tok = across(dproj1.reshape(8, TOK, 3 * LANES))
    branch1_full = gather(branch1, dproj1_tok, qkv_full1)
    dh1, send = hidden_back_send(1, dproj1_tok, qkv_full1, out0, gain_a, dmid1, slot_rows, gate_cols, table_t)

    arrived = spread(send)
    qkv_full0 = gather(qkv_rows[0], arrived, branch1_full)
    g0, dup0, dmade0 = expert_back(
        section.reshape(1), arrived, first_proj, second_proj, slope0, table, table_t, made1
    )
    back = spread(dmade0)

    def own(a, b):
        return jnp.where(section == 0, a, b)

    grad_in = mm_tn(own(x0, x1), own(dup0, dup1))
    grad_out = mm_tn(own(act0, act1), own(g0, g1))
    back, grad_in, grad_out = lax.optimization_barrier((back, grad_in, grad_out))
    out1 = combine(1, back, middle1, slot_cols, gate_cols, table)
    dmid0, branch0, send, dgain_f0 = middle_back(0, back, slot_cols, table, dh1, middle0, gain_f, ao0)
    branch0_full = gather(branch0, qkv_full0)
    dproj0, diag0 = attention_back(qkv0, weights0, across(send).reshape(SEQ, LANES))

    dproj0_tok = across(dproj0.reshape(8, TOK, 3 * LANES))
    parcels = dense_grads(1, own_index, normed1, dproj1, ctx1_full, branch1_full)
    parcels = dense_grads(0, own_index, normed0, dproj0, ctx0_full, branch0_full, parcels)
    parcels = after(parcels, dproj0_tok)
    got = spread(parcels)

    tail = jnp.concatenate(
        [dgain_f0, dgain_f1]
        + [jnp.pad(bias_grad(d).reshape(1, 2 * RELB), ((0, 0), (0, D - 2 * RELB))) for d in (diag0, diag1)],
        axis=0,
    ).astype(BF)
    dh0 = hidden_back(0, dproj0_tok, qkv_full0, hidden0, gain_a, dmid0)
    tails = after(gather(jnp.pad(tail, ((0, ROWS_OWN - 4), (0, 0)))), dh0, out1).reshape(8, ROWS_OWN, D)[:, :4].astype(F32)
    gain_sums = jnp.sum(tails[:, :2], axis=0)
    gain_sums = lax.dynamic_slice_in_dim(gain_sums, shard * ROWS_OWN, ROWS_OWN, 1)
    biases = lax.dynamic_slice_in_dim(tails[:PAIRS, 2:, : 2 * RELB], shard * 8, 8, 2)
    biases = biases.reshape(PAIRS, 2, 4, 2).transpose(1, 2, 0, 3).reshape(2, 4 * H)
    smalls = jnp.concatenate(
        [
            jnp.pad(gain_sums, ((0, 0), (0, LANES - ROWS_OWN))),
            jnp.pad(biases, ((0, 0), (0, 2 * LANES - 4 * H))),
        ],
        axis=1,
    )
    mine, theirs = own(smalls[0:1], smalls[1:2]), own(smalls[1:2], smalls[0:1])
    theirs = swap(jnp.pad(theirs, ((0, PIECE - 1), (0, 0))).astype(BF))
    small = (jnp.pad(mine, ((0, PIECE - 1), (0, 0))) + theirs.astype(F32)).astype(BF)

    got, dh0, small = lax.optimization_barrier((got, dh0, small))
    summed = jnp.sum(got.reshape(16, 8, PIECE, TILES * LANES).astype(F32), axis=0).astype(BF)
    summed = jnp.concatenate([summed, small[None]], axis=0)

    blocks = [summed] + [
        lax.ppermute(summed, "rep", [(r, r // 4 * 4 + (r + k) % 4) for r in range(8)]) for k in range(1, 4)
    ]
    blocks = blocks + [lax.ppermute(b, "rep", [(r, (r + 4) % 8) for r in range(8)]) for b in blocks]
    grad_qkv, grad_ao, dgain_a, dgain_f, drel = finish(
        lax.axis_index("rep").reshape(1), w_qkv[0], gain_attn.astype(F32), blocks
    )
    grad_bias = drel[:, : 4 * H].reshape(1, 4, H)

    def by_layer(layer0, layer1):
        keep = jnp.where(section == 0, layer0, layer1)
        other = swap(jnp.where(section == 0, layer1, layer0))
        pair = jnp.where(section == 0, jnp.stack([keep, other]), jnp.stack([other, keep]))
        return pair.reshape(1, 2, 1, TOK, D)

    return (
        by_layer(out0, out1),
        by_layer(dh0, dh1),
        grad_qkv[None],
        grad_ao[None],
        dgain_a,
        dgain_f,
        grad_bias,
        grad_in[None, None],
        grad_out[None, None],
    )


def solution(mesh):
    placed = (
        P(None, "rep", "shard", None),
        P(None, "rep", "shard", None),
        P("section", "shard", None),
        P("section", "shard", None),
        P("section", "shard"),
        P("section", "shard"),
        P("section", "shard", None),
        P("section", ("rep", "shard"), None, None),
        P("section", ("rep", "shard"), None, None),
        P("section", None, "rep", "shard", None),
        P("section", None, "rep", "shard", None),
    )
    return jax.shard_map(
        per_device,
        mesh=mesh,
        in_specs=placed,
        out_specs=(
            P("section", None, "rep", "shard", None),
            P("section", None, "rep", "shard", None),
            P("section", "shard", None),
            P("section", "shard", None),
            P("section", "shard"),
            P("section", "shard"),
            P("section", "shard", None),
            P("section", ("rep", "shard"), None, None),
            P("section", ("rep", "shard"), None, None),
        ),
        check_vma=False,
    )
```
